128 devices in a mesh: rows: 16 (over y, z), cols: 8 (over x, core).
Axes of the slice: x: 4, y: 4, z: 4, core: 2. Of those that a mesh axis runs over, the one named last changes fastest.
Arguments:
- coefficients: float32 [4, 2048, 4, 256], P(None, 'rows'), may hold values from -0.03 to 0.09
- support: int32 [4, 2048, 4], P(None, 'rows'), may hold values from 0 to 23, all different within a row
- primal: float32 [24, 256, 256], P('cols'), may hold values from -0.5 to 9, as said below
- dual_inverse: float32 [24, 256, 256], P('cols'), may hold values from -0.5 to 9, as said below
- block_sizes: int32 [24], P('cols'), may hold values from 64 to 256, as said below
- damping: float32 [4, 2048], P(None, 'rows'), may hold values from 0.5 to 2
- right_sides: float32 [4, 32, 2048], P(None, 'cols', 'rows'), may hold values from -6 to 6
Outputs:
- updated: float32 [4, 2048, 8192], P(None, 'rows', 'cols')
- panel_factor: float32 [4, 2048, 128], P(None, 'rows')
- solved: float32 [4, 32, 2048], P(None, 'cols', 'rows')
The draws below stay inside these ranges and needn't reach their ends.
Inputs may be any that keep to these rules, and one draw needn't show every extreme that they name: `primal`: each block is symmetric positive definite. `dual_inverse`: each block is symmetric positive definite. `block_sizes`: some block has order 256.
All inputs are finite; a program needn't handle non-finite values.
Results may differ from the reference program's by a relative error of at most 0.00015.
Values sent between devices are 32-bit elements; how exact they have to be, the bound alone decides.
No kernel may reach another device: no remote copies, remote signals or barrier semaphores. Data moves between devices by JAX's collectives and lax.ppermute only.
A program may use at most 192 MiB of HBM per device.

```python
import math
import jax
import jax.numpy as jnp
from jax import lax

BS = 256
K = 4
TILE = 128
NRHS = 32
TPR = 4
SPAN = 2048
NB = 24
N_ROWS = 16


def definite_blocks(key):
    first_key, second_key = jax.random.split(key)
    floor_value, ceiling, spread = (1.0, 4.0, 0.4)
    diagonal = jnp.exp(jax.random.uniform(first_key, (NB, BS), jnp.float32, math.log(floor_value), math.log(ceiling)))
    noise = jax.random.normal(second_key, (NB, BS, BS), jnp.float32) * (spread / math.sqrt(BS))
    symmetric = (noise + jnp.swapaxes(noise, 1, 2)) / math.sqrt(2.0)
    return symmetric + diagonal[:, :, None] * jnp.eye(BS, dtype=jnp.float32)[None, :, :]


def draw_primal(key, part):
    return definite_blocks(jax.random.fold_in(key, 11))


def draw_dual_inverse(key, part):
    return definite_blocks(jax.random.fold_in(key, 23))


def draw_block_sizes(key, part):
    orders = jax.random.randint(jax.random.fold_in(key, 31), (NB,), BS // 4, BS + 1)
    picked = jax.random.randint(jax.random.fold_in(key, 37), (), 0, NB)
    return jnp.where(jnp.arange(NB) == picked, BS, orders).astype(jnp.int32)


def block_levels(rng, extent, pieces, least, high):
    loudness, own = 1.0, jax.random.fold_in(rng, 6)
    for position, blocks in pieces:
        draws = jnp.exp(jax.random.uniform(jax.random.fold_in(own, position), (blocks,), jnp.float32, least / len(pieces), high / len(pieces)))
        loudness = loudness * jnp.repeat(draws, extent[position] // blocks).reshape([-1 if axis == position else 1 for axis in range(len(extent))])
    return loudness


def different_ones(stream_key, rows, number_of, top, lift):
    sequence = jax.random.permutation(jax.random.fold_in(stream_key, 1), number_of)
    pull = sequence
    for power in range(3):
        pull = pull * pull // number_of
    pull = pull * lift // number_of
    chance = jax.random.randint(jax.random.fold_in(stream_key, 2), (rows, number_of), 0, 4096) + pull
    fixed_rows = jax.random.permutation(jax.random.fold_in(stream_key, 3), rows)[jnp.arange(number_of) % rows]
    chance = jnp.where(jnp.arange(rows)[:, None] == fixed_rows[None, :], 1 << 14, chance)
    merit = chance * number_of + jnp.arange(number_of)
    return lax.top_k(merit.astype(jnp.int32), top)[1].astype(jnp.int32)


def gaussian(stream_key, extent, scale, reach, pieces=(), kind=jnp.bfloat16):
    drawn = jax.random.normal(stream_key, extent, jnp.float32) * scale
    if len(pieces) > 0:
        drawn = block_levels(stream_key, extent, pieces, -0.22, 0.18) * drawn
    return jnp.clip(drawn, min=-reach, max=reach).astype(kind)


def setup_inputs(seed: int = 0) -> dict:
    streams_of = jax.random.split(jax.random.key(seed), 8)
    return {
        "coefficients": jnp.clip(-0.03 + 0.120000003 * jax.random.uniform(streams_of[0], (TPR, SPAN, K, BS), jnp.float32) ** block_levels(streams_of[0], (TPR, SPAN, K, BS), ((1, 16),), -0.2, 0.2), -0.03, 0.09),
        "support": different_ones(streams_of[1], TPR * SPAN, NB, K, 2730).reshape((TPR, SPAN, K)),
        "primal": draw_primal(jax.random.fold_in(streams_of[7], 71), 0),
        "dual_inverse": draw_dual_inverse(jax.random.fold_in(streams_of[7], 71), 0),
        "block_sizes": draw_block_sizes(jax.random.fold_in(streams_of[7], 71), 0),
        "damping": jnp.clip(jnp.exp(math.log(2.0) - 1.3862944 * jax.random.uniform(streams_of[5], (TPR, SPAN), jnp.float32) ** block_levels(streams_of[5], (TPR, SPAN), ((1, 16),), -0.2, 0.2)), 0.5, 2.0),
        "right_sides": gaussian(streams_of[6], (TPR, NRHS, SPAN), 1.0, 6.0, ((1, 8), (2, 16)), jnp.float32),
    }


highest = lax.Precision.HIGHEST

def reference(coefficients, support, primal, dual_inverse, block_sizes, damping, right_sides):
    count_all = TPR * TILE * N_ROWS
    flat_coef = coefficients.reshape(count_all, K, BS)
    flat_support = support.reshape(count_all, K)
    positions = jnp.arange(BS, dtype=jnp.int32)
    schur_full = jnp.zeros((count_all, count_all), jnp.float32)
    for block_id in range(NB):
        chosen = (flat_support == block_id).astype(jnp.float32)
        dense_rows = jnp.einsum('mk,mkd->md', chosen, flat_coef, precision=highest)
        active = (positions < block_sizes[block_id]).astype(jnp.float32)
        weights = primal[block_id] * dual_inverse[block_id] * active[:, None] * active[None, :]
        weighted = jnp.dot(dense_rows.astype(jnp.float32), weights.astype(jnp.float32), precision=highest, preferred_element_type=jnp.float32)
        schur_full = schur_full + jnp.dot(weighted.astype(jnp.float32), dense_rows.T.astype(jnp.float32), precision=highest, preferred_element_type=jnp.float32)
    schur_full = schur_full + jnp.diag(damping.reshape(count_all))
    corner = schur_full[:TILE, :TILE]
    factor = jnp.linalg.cholesky(corner)
    identity = jnp.eye(TILE, dtype=jnp.float32)
    inverse = jax.scipy.linalg.solve_triangular(factor, identity, lower=True)
    panel_rows = jnp.dot(schur_full[:, :TILE].astype(jnp.float32), inverse.T.astype(jnp.float32), precision=highest, preferred_element_type=jnp.float32)
    outer_term = jnp.dot(panel_rows.astype(jnp.float32), panel_rows.T.astype(jnp.float32), precision=highest, preferred_element_type=jnp.float32)
    later = jnp.arange(count_all) >= TILE
    updated = schur_full - jnp.where(later[:, None] & later[None, :], outer_term, 0.0)
    all_sides = jnp.transpose(right_sides, (1, 0, 2)).reshape(NRHS, count_all)
    leading = jnp.dot(all_sides[:, :TILE].astype(jnp.float32), inverse.T.astype(jnp.float32), precision=highest, preferred_element_type=jnp.float32)
    remainder = all_sides - jnp.dot(leading.astype(jnp.float32), panel_rows.T.astype(jnp.float32), precision=highest, preferred_element_type=jnp.float32)
    padded_lead = jnp.pad(leading, ((0, 0), (0, count_all - TILE)))
    solved = jnp.where(later[None, :], remainder, padded_lead)
    solved = jnp.transpose(solved.reshape(NRHS, TPR, N_ROWS * TILE), (1, 0, 2))
    return (updated.reshape(TPR, N_ROWS * TILE, count_all), panel_rows.reshape(TPR, N_ROWS * TILE, TILE), solved)
```

```python
import functools
import jax
import jax.numpy as jnp
from jax.sharding import PartitionSpec as P
from jax import lax
from jax.experimental import pallas as pl
from jax.experimental.pallas import tpu as pltpu
BF=jnp.bfloat16; F32=jnp.float32
NT=(((1,),(1,)),((),()))
NN=(((1,),(0,)),((),()))

def split(v):
    h=v.astype(BF)
    return h,(v-h.astype(F32)).astype(BF)

def dot3(ah,al,bh,bl,dims):
    d=functools.partial(lax.dot_general,dimension_numbers=dims,preferred_element_type=F32)
    return d(ah,bh)+d(al,bh)+d(ah,bl)

def pick(block,masks_src,vals):
    out=None
    m=[s==block for s in masks_src]
    for k in range(4):
        v=vals[k]
        out=jnp.where(m[k],v,jnp.zeros_like(v) if out is None else out)
    return out

def weigh_body(ids,c_ref,s_ref,w_ref,vh_ref,vl_ref,ac_ref,ch,cl):
    b=pl.program_id(0)
    @pl.when(b==0)
    def _():
        for k in range(4):
            h,l=split(c_ref[k]); ch[k]=h; cl[k]=l
        ac_ref[...]=jnp.zeros_like(ac_ref)
    block=ids[b].astype(F32).astype(BF)
    wh,wl=split(w_ref[0])
    sup=[s_ref[k] for k in range(4)]
    def dense(src):
        return jnp.concatenate([pick(block,sup,[src[k,:,q*128:(q+1)*128] for k in range(4)]) for q in range(2)],axis=1)
    dh=dense(ch); dl=dense(cl)
    v=dot3(dh,dl,wh,wl,NN)
    vh,vl=split(v)
    for q in range(2):
        vh_ref[q]=vh[:,q*128:(q+1)*128]; vl_ref[q]=vl[:,q*128:(q+1)*128]
    n=dh.shape[0]
    ac_ref[...]+=dot3(vh,vl,dh[n-128:],dl[n-128:],NT)

def weigh(ids,c,s,w):
    n=c.shape[1]
    grid=pltpu.PrefetchScalarGridSpec(num_scalar_prefetch=1,grid=(24,),
        in_specs=[pl.BlockSpec((4,n,256),lambda b,i:(0,0,0)),pl.BlockSpec((4,n,128),lambda b,i:(0,0,0)),pl.BlockSpec((1,256,256),lambda b,i:(b,0,0))],
        out_specs=[pl.BlockSpec((2,n,128),lambda b,i:(0,0,b)),pl.BlockSpec((2,n,128),lambda b,i:(0,0,b)),pl.BlockSpec((n,128),lambda b,i:(0,0))],
        scratch_shapes=[pltpu.VMEM((4,n,256),BF),pltpu.VMEM((4,n,256),BF)])
    return pl.pallas_call(weigh_body,grid_spec=grid,out_shape=[jax.ShapeDtypeStruct((2,n,3072),BF)]*2+[jax.ShapeDtypeStruct((n,128),F32)],
        compiler_params=pltpu.CompilerParams(vmem_limit_bytes=48<<20),name="weigh",
        cost_estimate=pl.CostEstimate(flops=2*3*n*6144*384,bytes_accessed=20<<20,transcendentals=0))(ids,c,s,w)

def prod_body(has_acc,ids,pid,vh_ref,vl_ref,c_ref,s_ref,*rest):
    if has_acc: a_ref,o_ref,ch,cl=rest
    else: o_ref,ch,cl=rest
    g=pl.program_id(0)
    @pl.when(g==0)
    def _():
        for t in range(8):
            for k in range(4):
                h,l=split(c_ref[t,k*128:(k+1)*128])
                ch[k,t*128:(t+1)*128]=h; cl[k,t*128:(t+1)*128]=l
        o_ref[...]=a_ref[...] if has_acc else jnp.zeros_like(o_ref)
    blocks=[ids[2*g+u].astype(F32).astype(BF) for u in range(2)]
    vh=vh_ref[0]; vl=vl_ref[0]
    for q in range(4):
        r=slice(q*256,(q+1)*256)
        sup=[s_ref[k,r] for k in range(4)]
        dh=jnp.concatenate([pick(bk,sup,[ch[k,r] for k in range(4)]) for bk in blocks],axis=1)
        dl=jnp.concatenate([pick(bk,sup,[cl[k,r] for k in range(4)]) for bk in blocks],axis=1)
        o_ref[:,r]+=dot3(vh,vl,dh,dl,NT)

def prod(ids,pid,vh,vl,c,s,acc=None):
    n=vh.shape[1]
    vspec=pl.BlockSpec((1,n,256),lambda g,i,p:(p[0],0,g))
    full=pl.BlockSpec((n,1024),lambda g,i,p:(0,0))
    grid=pltpu.PrefetchScalarGridSpec(num_scalar_prefetch=2,grid=(12,),
        in_specs=[vspec,vspec,pl.BlockSpec((8,520,128),lambda g,i,p:(0,0,0)),pl.BlockSpec((4,1024,128),lambda g,i,p:(0,0,0))]+([full] if acc is not None else []),
        out_specs=full,scratch_shapes=[pltpu.VMEM((4,1024,128),BF),pltpu.VMEM((4,1024,128),BF)])
    return pl.pallas_call(functools.partial(prod_body,acc is not None),grid_spec=grid,out_shape=jax.ShapeDtypeStruct((n,1024),F32),
        compiler_params=pltpu.CompilerParams(vmem_limit_bytes=48<<20),name="prod",
        cost_estimate=pl.CostEstimate(flops=2*3*n*3072*1024,bytes_accessed=16<<20,transcendentals=0))(ids,pid,vh,vl,c,s,*([acc] if acc is not None else []))

def inverse_body(c_ref,o_ref):
    n=128
    row=lax.broadcasted_iota(jnp.int32,(n,2*n),0)
    col=lax.broadcasted_iota(jnp.int32,(n,2*n),1)
    rowc=lax.broadcasted_iota(jnp.int32,(n,1),0)
    m=jnp.concatenate([c_ref[...],jnp.where(row[:,:n]==col[:,:n],1.0,0.0).astype(F32)],axis=1)
    o_ref[...]=m
    lane=lax.broadcasted_iota(jnp.int32,(1,n),1)
    sub=lax.broadcasted_iota(jnp.int32,(n,n),0)
    def step(k,_):
        line=o_ref[pl.ds(k,1),:]
        left=line[:,:n]
        piv=jnp.sum(jnp.where(lane==k,left,0.0),axis=1,keepdims=True)
        r=lax.rsqrt(piv)
        colk=jnp.sum(jnp.where(lane==k,o_ref[:,:n],0.0),axis=1,keepdims=True)
        f=jnp.where(rowc>k,colk*r,0.0)
        scaled=line*r
        o_ref[...]=o_ref[...]-f*scaled
        o_ref[pl.ds(k,1),:]=scaled
        return 0
    lax.fori_loop(0,n,step,0)

def inverse_aug(c):
    return pl.pallas_call(inverse_body,out_shape=jax.ShapeDtypeStruct((128,256),F32),name="inverse")(c)


highest = lax.Precision.HIGHEST
SWAP = [(i, i ^ 1) for i in range(8)]
UP = [(2 * x + c, 2 * ((x + 1) % 4) + c) for x in range(4) for c in range(2)]
DOWN = [(2 * x + c, 2 * ((x + 3) % 4) + c) for x in range(4) for c in range(2)]


def over_cols(v, pairs):
    return lax.ppermute(v, "cols", pairs)


def over_rows(v, pairs):
    return lax.ppermute(v, "rows", pairs)


def gather_weights(w):
    below = over_cols(w, UP)
    above = over_cols(w, DOWN)
    far = jnp.concatenate([over_cols(below[:, :128], UP), over_cols(above[:, 128:], DOWN)], axis=1)
    parts = [w, below, above, far]
    return jnp.concatenate(parts + [over_cols(v, SWAP) for v in parts], axis=0)


def spread_first(v, r):
    one = over_rows(v, [(0, 1)])
    three = over_rows(v, [(0, 3)])
    two = over_rows(one, [(1, 2)])
    line = jnp.where(r == 0, v, one + three + two)
    first = over_rows(line, [(z, 4 + z) for z in range(4)])
    third = over_rows(line, [(z, 12 + z) for z in range(4)])
    second = over_rows(first, [(4 + z, 8 + z) for z in range(4)])
    return jnp.where(r < 4, line, first + third + second)


def lanes(s):
    return jnp.broadcast_to(s[:, :, None], s.shape + (128,)).astype(BF)


def by_slot(v):
    return jnp.transpose(v, (1, 0, 2)).reshape(512, 128)


def local(coefficients, support, primal, dual_inverse, block_sizes, damping, right_sides):
    col = lax.axis_index("cols")
    r = lax.axis_index("rows")
    x = col // 2
    p = col % 2
    positions = jnp.arange(256, dtype=jnp.int32)
    active = (positions[None, :] < block_sizes[:, None]).astype(F32)
    w = primal * dual_inverse * active[:, :, None] * active[:, None, :]
    sup = support.astype(F32)

    def piece(t):
        tile = lax.dynamic_index_in_dim(coefficients, t, 0, keepdims=False)
        return by_slot(lax.dynamic_slice_in_dim(tile, p * 128, 128, 2))

    mine = jnp.concatenate([piece(x), lax.dynamic_index_in_dim(sup, x, 0, keepdims=False).T,
                            jnp.zeros((4, 128), F32)], axis=0)
    gathered = lax.all_gather(mine, "rows")
    head = jnp.concatenate([piece(0), sup[0].T, right_sides[0], damping[:1], jnp.zeros((7, 128), F32)], axis=0)
    head = spread_first(head, r)
    head_other = over_cols(head[:512], SWAP)
    weights = gather_weights(w)
    near = (2 * ((x + jnp.array([0, 3, 1, 2])) % 4))
    ids = jnp.concatenate([near + p, near + 1 - p])
    ids = (ids[:, None] * 3 + jnp.arange(3)).reshape(24).astype(jnp.int32)

    lo = jnp.where(p == 0, head[:512], head_other).reshape(4, 128, 128)
    hi = jnp.where(p == 0, head_other, head[:512]).reshape(4, 128, 128)
    own = jnp.transpose(coefficients, (2, 0, 1, 3)).reshape(4, 512, 256)
    rows = jnp.concatenate([own, jnp.concatenate([lo, hi], axis=2)], axis=1)
    row_sup = lanes(jnp.concatenate([jnp.transpose(sup, (2, 0, 1)).reshape(4, 512), head[512:516]], axis=1))
    vh, vl, ac = weigh(ids, rows, row_sup, weights)

    eye = jnp.eye(128, dtype=F32)
    corner = ac[512:] + eye * head[520]
    inverse = inverse_aug(corner)[:, 128:]
    top = jnp.where(r == 0, corner, ac[:128])
    panel = lax.dot_general(jnp.concatenate([top, ac[128:512]], axis=0), inverse, NT, precision=highest)
    leading = lax.dot_general(head[516:520], inverse, NT, precision=highest)
    panel_factor = panel.reshape(4, 128, 128)
    remainder = right_sides - jnp.einsum("sk,tak->tsa", leading, panel_factor, precision=highest)
    solved = jnp.where(((jnp.arange(4) > 0) | (r > 0))[:, None, None], remainder, leading[None])

    kept = lax.dynamic_slice_in_dim(gathered, 8 * p, 8, 0)
    given = lax.dynamic_slice_in_dim(gathered, 8 * (1 - p), 8, 0)
    swapped = over_cols(given, SWAP)
    col_sup = lanes(jnp.transpose(kept[:, 512:516], (1, 0, 2)).reshape(4, 1024))
    which = p.astype(jnp.int32)[None]
    out = prod(ids, which, vh, vl, kept, col_sup)
    out = prod(ids, 1 - which, vh, vl, swapped, col_sup, out)

    row_global = ((jnp.arange(4)[:, None] * 16 + r) * 128 + jnp.arange(128)[None, :]).reshape(512)
    col_global = col * 1024 + jnp.arange(1024)
    schur = out[:512] + jnp.where(row_global[:, None] == col_global[None, :], damping.reshape(512)[:, None], 0.0)
    col_panel = jnp.dot(inverse, out[512:], precision=highest)
    outer = jnp.dot(panel, col_panel, precision=lax.Precision.HIGH)
    later = (row_global >= 128)[:, None] & (col_global >= 128)[None, :]
    updated = schur - jnp.where(later, outer, 0.0)
    return updated.reshape(4, 128, 1024), panel_factor, solved


def solution(mesh):
    in_specs = (
        P(None, "rows", None, None),
        P(None, "rows", None),
        P("cols", None, None),
        P("cols", None, None),
        P("cols"),
        P(None, "rows"),
        P(None, "cols", "rows"),
    )
    out_specs = (P(None, "rows", "cols"), P(None, "rows", None), P(None, "cols", "rows"))
    return jax.shard_map(local, mesh=mesh, in_specs=in_specs, out_specs=out_specs, check_vma=False)
```

```python
import functools
import jax
import jax.numpy as jnp
from jax import lax
from jax.experimental import pallas as pl
from jax.experimental.pallas import tpu as pltpu
from jax.sharding import PartitionSpec as P

BF = jnp.bfloat16
F32 = jnp.float32
NT = (((1,), (1,)), ((), ()))
NN = (((1,), (0,)), ((), ()))
VMEM = 56 << 20
highest = lax.Precision.HIGHEST


def split(v):
    h = v.astype(BF)
    return h, (v - h.astype(F32)).astype(BF)


def product(ah, al, bh, bl, dims):
    side = dims[0][1][0]
    left = jnp.concatenate([ah, al, ah], axis=1)
    right = jnp.concatenate([bh, bh, bl], axis=side)
    return lax.dot_general(left, right, dims, preferred_element_type=F32)


def choose(masks, values):
    out = jnp.zeros_like(values[0])
    for m, v in zip(masks, values):
        out = jnp.where(m, v, out)
    return out


def label(ids, i):
    return ids[i].astype(F32).astype(BF)


def dense_rows(block, sup, src):
    m = [s == block for s in sup]
    return jnp.concatenate([choose(m, [src[k, :, q * 128:(q + 1) * 128] for k in range(4)]) for q in range(2)], axis=1)


def corner_body(ids, c_ref, s_ref, w_ref, o_ref):
    parts = [split(c_ref[k]) for k in range(4)]
    high = jnp.stack([h for h, _ in parts])
    low = jnp.stack([l for _, l in parts])
    sup = [s_ref[k] for k in range(4)]
    total = jnp.zeros((128, 128), F32)
    for u in range(3):
        block = label(ids, u)
        dh, dl = dense_rows(block, sup, high), dense_rows(block, sup, low)
        wh, wl = split(w_ref[u])
        vh, vl = split(product(dh, dl, wh, wl, NN))
        total = total + product(vh, vl, dh, dl, NT)
    o_ref[...] = total


def corner_part(ids, c, s, w):
    grid = pltpu.PrefetchScalarGridSpec(
        num_scalar_prefetch=1, grid=(1,),
        in_specs=[pl.BlockSpec((4, 128, 256), lambda g, i: (0, 0, 0)), pl.BlockSpec((4, 128, 128), lambda g, i: (0, 0, 0)),
                  pl.BlockSpec((3, 256, 256), lambda g, i: (0, 0, 0))],
        out_specs=pl.BlockSpec((128, 128), lambda g, i: (0, 0)))
    return pl.pallas_call(corner_body, grid_spec=grid, out_shape=jax.ShapeDtypeStruct((128, 128), F32),
                          compiler_params=pltpu.CompilerParams(vmem_limit_bytes=VMEM), name="corner",
                          cost_estimate=pl.CostEstimate(flops=2 * 3 * 128 * 768 * 384, bytes_accessed=2 << 20, transcendentals=0))(ids, c, s, w)


def weigh_body(ids, c_ref, s_ref, *rest):
    w_refs, (vh_ref, vl_ref, a_ref, ch, cl, wh, wl) = rest[:10], rest[10:]
    g = pl.program_id(0)

    @pl.when(g == 0)
    def _():
        for k in range(4):
            ch[k], cl[k] = split(c_ref[k])
        a_ref[...] = jnp.zeros_like(a_ref)

    for i in range(8):
        @pl.when(g == i)
        def _(i=i):
            base = 5 * (i // 4)
            if i % 4 < 3:
                wh[...], wl[...] = split(w_refs[base + i % 4][...])
            else:
                wh[:, :128], wl[:, :128] = split(w_refs[base + 3][...])
                wh[:, 128:], wl[:, 128:] = split(w_refs[base + 4][...])

    sup = [s_ref[k] for k in range(4)]
    n = vh_ref.shape[1]
    kept = []
    for u in range(3):
        block = label(ids, 3 * g + u)
        dh, dl = dense_rows(block, sup, ch), dense_rows(block, sup, cl)
        vh, vl = split(product(dh[:n], dl[:n], wh[u], wl[u], NN))
        for q in range(2):
            vh_ref[q, :, u * 128:(u + 1) * 128] = vh[:, q * 128:(q + 1) * 128]
            vl_ref[q, :, u * 128:(u + 1) * 128] = vl[:, q * 128:(q + 1) * 128]
        kept.append((vh, vl, dh[n:], dl[n:]))
    vh, vl, dh, dl = [jnp.concatenate(list(v), axis=1) for v in zip(*kept)]
    a_ref[...] += product(vh, vl, dh, dl, NT)


def weigh(ids, c, s, parts):
    m = c.shape[1]
    n = m - 128
    whole = lambda v: pl.BlockSpec(v.shape, lambda g, i: (0,) * v.ndim)
    grid = pltpu.PrefetchScalarGridSpec(
        num_scalar_prefetch=1, grid=(8,),
        in_specs=[whole(c), whole(s)] + [whole(v) for v in parts],
        out_specs=[pl.BlockSpec((2, n, 384), lambda g, i: (0, 0, g))] * 2 + [pl.BlockSpec((n, 128), lambda g, i: (0, 0))],
        scratch_shapes=[pltpu.VMEM((4, m, 256), BF)] * 2 + [pltpu.VMEM((3, 256, 256), BF)] * 2)
    return pl.pallas_call(weigh_body, grid_spec=grid,
                          out_shape=[jax.ShapeDtypeStruct((2, n, 3072), BF)] * 2 + [jax.ShapeDtypeStruct((n, 128), F32)],
                          compiler_params=pltpu.CompilerParams(vmem_limit_bytes=VMEM), name="weigh",
                          cost_estimate=pl.CostEstimate(flops=2 * 3 * n * 6144 * 384, bytes_accessed=20 << 20, transcendentals=0))(ids, c, s, *parts)


def block_body(has_sum, ids, which, vh_ref, vl_ref, c_ref, s_ref, *rest):
    if has_sum:
        a_ref, o_ref, ch, cl = rest
    else:
        o_ref, ch, cl = rest
    g = pl.program_id(0)

    @pl.when(g == 0)
    def _():
        for t in range(8):
            for k in range(4):
                ch[k, :, t * 128:(t + 1) * 128], cl[k, :, t * 128:(t + 1) * 128] = split(c_ref[t, k * 128:(k + 1) * 128])
        o_ref[...] = a_ref[...] if has_sum else jnp.zeros_like(o_ref)

    vh, vl = vh_ref[0], vl_ref[0]
    for q in range(2):
        r = slice(q * 512, (q + 1) * 512)
        sup = [s_ref[k:k + 1, r] for k in range(4)]
        highs, lows = [], []
        for u in range(6):
            block = label(ids, 6 * g + u)
            m = [jnp.broadcast_to(s, (128, 512)).astype(BF) == block for s in sup]
            highs.append(choose(m, [ch[k, :, r] for k in range(4)]))
            lows.append(choose(m, [cl[k, :, r] for k in range(4)]))
        o_ref[:, r] += product(vh, vl, jnp.concatenate(highs, axis=0), jnp.concatenate(lows, axis=0), NN)


def block_product(ids, which, vh, vl, c, s, start=None):
    n = vh.shape[1]
    side = pl.BlockSpec((1, n, 768), lambda g, i, w: (w[0], 0, g))
    full = pl.BlockSpec((n, 1024), lambda g, i, w: (0, 0))
    extra = [] if start is None else [start]
    grid = pltpu.PrefetchScalarGridSpec(
        num_scalar_prefetch=2, grid=(4,),
        in_specs=[side, side, pl.BlockSpec((8, 520, 128), lambda g, i, w: (0, 0, 0)),
                  pl.BlockSpec((8, 1024), lambda g, i, w: (0, 0))] + [full] * len(extra),
        out_specs=full, scratch_shapes=[pltpu.VMEM((4, 128, 1024), BF)] * 2)
    return pl.pallas_call(functools.partial(block_body, start is not None), grid_spec=grid,
                          out_shape=jax.ShapeDtypeStruct((n, 1024), F32),
                          compiler_params=pltpu.CompilerParams(vmem_limit_bytes=VMEM), name="block",
                          cost_estimate=pl.CostEstimate(flops=2 * 3 * n * 3072 * 1024, bytes_accessed=16 << 20, transcendentals=0))(ids, which, vh, vl, c, s, *extra)


def inverse_body(c_ref, o_ref):
    n = 128
    row = lax.broadcasted_iota(jnp.int32, (n, n), 0)
    col = lax.broadcasted_iota(jnp.int32, (n, n), 1)
    below = lax.broadcasted_iota(jnp.int32, (n, 1), 0)
    lane = lax.broadcasted_iota(jnp.int32, (1, n), 1)
    o_ref[...] = jnp.concatenate([c_ref[...], jnp.where(row == col, 1.0, 0.0).astype(F32)], axis=1)

    def step(k, _):
        line = o_ref[pl.ds(k, 1), :]
        pivot = jnp.sum(jnp.where(lane == k, line[:, :n], 0.0), axis=1, keepdims=True)
        scale = lax.rsqrt(pivot)
        column = jnp.sum(jnp.where(lane == k, o_ref[:, :n], 0.0), axis=1, keepdims=True)
        factor = jnp.where(below > k, column * scale, 0.0)
        scaled = line * scale
        o_ref[...] = o_ref[...] - factor * scaled
        o_ref[pl.ds(k, 1), :] = scaled
        return 0

    lax.fori_loop(0, n, step, 0)


def inverse_of(c):
    return pl.pallas_call(inverse_body, out_shape=jax.ShapeDtypeStruct((128, 256), F32), name="inverse",
                          cost_estimate=pl.CostEstimate(flops=2 * 3 * 512 * 3072 * 1024, bytes_accessed=1 << 20, transcendentals=0))(c)


def finish_body(where, place, s_ref, p_ref, q_ref, d_ref, o_ref):
    g = pl.program_id(0)
    r, col = where[0], where[1]
    row = lax.broadcasted_iota(jnp.int32, (128, 128), 0)
    lane = lax.broadcasted_iota(jnp.int32, (128, 128), 1)
    qh, ql = split(q_ref[0])
    across = col * 8 + g
    for t in range(4):
        ph, plo = split(p_ref[t])
        down = t * 16 + r
        outer = product(ph, plo, qh, ql, NT)
        diagonal = jnp.where((row == lane) & (down == across), jnp.broadcast_to(d_ref[t:t + 1], (128, 128)), 0.0)
        o_ref[t] = s_ref[t] + diagonal - jnp.where((down > 0) & (across > 0), outer, 0.0)


def finish(where, place, s, p, q, d):
    grid = pltpu.PrefetchScalarGridSpec(
        num_scalar_prefetch=2, grid=(8,),
        in_specs=[pl.BlockSpec((4, 128, 128), lambda g, w, i: (0, 0, g)), pl.BlockSpec((4, 128, 128), lambda g, w, i: (0, 0, 0)),
                  pl.BlockSpec((1, 128, 128), lambda g, w, i: (i[g], 0, 0)), pl.BlockSpec((4, 128), lambda g, w, i: (0, 0))],
        out_specs=pl.BlockSpec((4, 128, 128), lambda g, w, i: (0, 0, g)))
    return pl.pallas_call(finish_body, grid_spec=grid, out_shape=jax.ShapeDtypeStruct((4, 128, 1024), F32),
                          compiler_params=pltpu.CompilerParams(vmem_limit_bytes=VMEM), name="finish",
                          cost_estimate=pl.CostEstimate(flops=2 * 3 * 512 * 128 * 1024, bytes_accessed=5 << 20, transcendentals=0))(where, place, s, p, q, d)


def chips(step):
    return [(2 * x + c, 2 * step(x) + c) for x in range(4) for c in range(2)]


SWAP = [(i, i ^ 1) for i in range(8)]
UP = chips(lambda x: (x + 1) % 4)
DOWN = chips(lambda x: (x + 3) % 4)
PAIR = chips(lambda x: x ^ 1)
FAR = chips(lambda x: x ^ 2)
ALONG_Z = [[(4 * y + z, 4 * y + (z + d) % 4) for y in range(4) for z in range(4)] for d in (1, 3, 2)]
ALONG_Y = [[(4 * y + z, 4 * ((y + d) % 4) + z) for y in range(4) for z in range(4)] for d in (1, 3, 2)]


def over_cols(v, pairs):
    return lax.ppermute(v, "cols", pairs)


def over_rows(v, pairs):
    return lax.ppermute(v, "rows", pairs)


def gather_weights(w):
    below = over_cols(w, UP)
    above = over_cols(w, DOWN)
    parts = [w, below, above, over_cols(below[:, :128], UP), over_cols(above[:, 128:], DOWN)]
    return parts + [over_cols(v, SWAP) for v in parts]


def spread_first(v, r):
    one = over_rows(v, [(0, 1)])
    three = over_rows(v, [(0, 3)])
    two = over_rows(one, [(1, 2)])
    line = jnp.where(r == 0, v, one + three + two)
    first = over_rows(line, [(z, 4 + z) for z in range(4)])
    third = over_rows(line, [(z, 12 + z) for z in range(4)])
    second = over_rows(first, [(4 + z, 8 + z) for z in range(4)])
    return jnp.where(r < 4, line, first + third + second)


def gather_plane(v):
    line = jnp.stack([v] + [over_rows(v, s) for s in ALONG_Z])
    return jnp.concatenate([line] + [over_rows(line, s) for s in ALONG_Y])


def lanes(s):
    return jnp.broadcast_to(s[:, :, None], s.shape + (128,)).astype(BF)


def local(coefficients, support, primal, dual_inverse, block_sizes, damping, right_sides):
    col = lax.axis_index("cols")
    r = lax.axis_index("rows")
    x = col // 2
    p = col % 2
    positions = jnp.arange(256, dtype=jnp.int32)
    active = (positions[None, :] < block_sizes[:, None]).astype(F32)
    w = primal * dual_inverse * active[:, :, None] * active[:, None, :]
    weights = gather_weights(w)
    sup = support.astype(F32)

    def piece(t):
        tile = lax.dynamic_index_in_dim(coefficients, t, 0, keepdims=False)
        return lax.dynamic_slice_in_dim(tile, p * 128, 128, 2)

    mine = jnp.concatenate([jnp.transpose(piece(x), (1, 2, 0)).reshape(512, 128),
                            lax.dynamic_index_in_dim(sup, x, 0, keepdims=False).T, jnp.zeros((4, 128), F32)], axis=0)
    gathered = lax.all_gather(mine, "rows")
    near = 2 * ((x + jnp.array([0, 3, 1, 2])) % 4)
    ids = jnp.concatenate([near + p, near + 1 - p])
    ids = (ids[:, None] * 3 + jnp.arange(3)).reshape(24).astype(jnp.int32)

    own = jnp.transpose(coefficients, (2, 0, 1, 3)).reshape(4, 512, 256)
    own_sup = jnp.transpose(sup, (2, 0, 1)).reshape(4, 512)
    corner = corner_part(ids, own[:, :128], lanes(own_sup[:, :128]), w)
    for pairs in (SWAP, PAIR, FAR):
        corner = corner + over_cols(corner, pairs)
    corner = corner + jnp.eye(128, dtype=F32) * damping[0]
    both = spread_first(inverse_of(corner)[:, 128:], r)
    inverse = both

    head = jnp.concatenate([jnp.transpose(piece(0), (1, 0, 2)).reshape(512, 128), sup[0].T, right_sides[0],
                            damping[:1], jnp.zeros((7, 128), F32)], axis=0)
    head = spread_first(head, r)
    head_other = over_cols(head[:512], SWAP)
    lo = jnp.where(p == 0, head[:512], head_other).reshape(4, 128, 128)
    hi = jnp.where(p == 0, head_other, head[:512]).reshape(4, 128, 128)
    rows = jnp.concatenate([own, jnp.concatenate([lo, hi], axis=2)], axis=1)
    row_sup = lanes(jnp.concatenate([own_sup, head[512:516]], axis=1))
    vh, vl, first = weigh(ids, rows, row_sup, weights)

    shift = jnp.where(r == 0, damping[0], 0.0) * jnp.eye(128, dtype=F32)
    first = first.at[:128].add(shift)
    panel_factor = lax.dot_general(first, inverse, NT, precision=highest).reshape(4, 128, 128)
    every = gather_plane(lax.dynamic_index_in_dim(panel_factor, x, 0, keepdims=False))
    leading = lax.dot_general(head[516:520], inverse, NT, precision=highest)
    remainder = right_sides - jnp.einsum("sk,tak->tsa", leading, panel_factor, precision=highest)
    solved = jnp.where(((jnp.arange(4) > 0) | (r > 0))[:, None, None], remainder, leading[None])

    kept = lax.dynamic_slice_in_dim(gathered, 8 * p, 8, 0)
    given = lax.dynamic_slice_in_dim(gathered, 8 * (1 - p), 8, 0)
    swapped = over_cols(given, SWAP)
    col_sup = jnp.pad(jnp.transpose(kept[:, 512:516], (1, 0, 2)).reshape(4, 1024), ((0, 4), (0, 0)))
    which = p.astype(jnp.int32)[None]
    out = block_product(ids, which, vh, vl, kept, col_sup)
    out = block_product(ids, 1 - which, vh, vl, swapped, col_sup, out)

    order = jnp.array([0, 2, 3, 1])
    tiles = 8 * p + jnp.arange(8)
    place = order[(tiles // 4 - r // 4) % 4] * 4 + order[(tiles % 4 - r % 4) % 4]
    updated = finish(jnp.stack([r, col]).astype(jnp.int32), place.astype(jnp.int32), out.reshape(4, 128, 1024), panel_factor, every, damping)
    return updated, panel_factor, solved


def solution(mesh):
    in_specs = (
        P(None, "rows", None, None),
        P(None, "rows", None),
        P("cols", None, None),
        P("cols", None, None),
        P("cols"),
        P(None, "rows"),
        P(None, "cols", "rows"),
    )
    out_specs = (P(None, "rows", "cols"), P(None, "rows", None), P(None, "cols", "rows"))
    return jax.shard_map(local, mesh=mesh, in_specs=in_specs, out_specs=out_specs, check_vma=False)
```

```python
import functools
import jax
import jax.numpy as jnp
from jax import lax
from jax.experimental import pallas as pl
from jax.experimental.pallas import tpu as pltpu
from jax.sharding import PartitionSpec as P

BF = jnp.bfloat16
F32 = jnp.float32
NT = (((1,), (1,)), ((), ()))
NN = (((1,), (0,)), ((), ()))
VMEM = 56 << 20
highest = lax.Precision.HIGHEST


def split(v):
    h = v.astype(BF)
    return h, (v - h.astype(F32)).astype(BF)


def product(ah, al, bh, bl, dims):
    side = dims[0][1][0]
    left = jnp.concatenate([ah, al, ah], axis=1)
    right = jnp.concatenate([bh, bh, bl], axis=side)
    return lax.dot_general(left, right, dims, preferred_element_type=F32)


def choose(masks, values):
    out = jnp.zeros_like(values[0])
    for m, v in zip(masks, values):
        out = jnp.where(m, v, out)
    return out


def label(ids, i):
    return ids[i].astype(F32).astype(BF)


def partial_body(ids, c_ref, s_ref, w_ref, v_ref, o_ref):
    total = jnp.zeros((128, 128), F32)
    for u in range(3):
        block = ids[u].astype(F32)
        wh, wl = split(w_ref[u])
        m = [s_ref[k] == block for k in range(4)]
        d = jnp.concatenate([choose(m, [c_ref[k, :, q * 128:(q + 1) * 128] for k in range(4)]) for q in range(2)], axis=1)
        dh, dl = split(d)
        v = product(dh, dl, wh, wl, NN)
        vh, vl = split(v[:128])
        total = total + product(vh, vl, dh[:128], dl[:128], NT)
        for q in range(2):
            for t in range(4):
                part = v[t * 128:(t + 1) * 128, q * 128:(q + 1) * 128]
                for k in range(4):
                    before = jnp.zeros_like(part) if u == 0 else v_ref[q, t, k]
                    v_ref[q, t, k] = jnp.where(m[k][t * 128:(t + 1) * 128], part, before)
    o_ref[...] = total


def partial(ids, c, s, w):
    whole = lambda shape: pl.BlockSpec(shape, lambda g, i: (0,) * len(shape))
    shapes = [(2, 4, 4, 128, 128), (128, 128)]
    grid = pltpu.PrefetchScalarGridSpec(num_scalar_prefetch=1, grid=(1,), in_specs=[whole(c.shape), whole(s.shape), whole(w.shape)],
                                        out_specs=[whole(v) for v in shapes])
    return pl.pallas_call(partial_body, grid_spec=grid, out_shape=[jax.ShapeDtypeStruct(v, F32) for v in shapes],
                          compiler_params=pltpu.CompilerParams(vmem_limit_bytes=VMEM), name="partial",
                          cost_estimate=pl.CostEstimate(flops=2 * 3 * 512 * 768 * 256, bytes_accessed=6 << 20, transcendentals=0))(ids, c, s, w)


def fill_rows(v_ref, high, low):
    for t in range(4):
        for k in range(4):
            high[k, t * 128:(t + 1) * 128], low[k, t * 128:(t + 1) * 128] = split(v_ref[t, k])


def gather_blocks(ids, base, sup, high, low, axis):
    highs, lows = [], []
    for u in range(6):
        block = label(ids, base + u)
        m = [s == block for s in sup]
        highs.append(choose(m, [high(k) for k in range(4)]))
        lows.append(choose(m, [low(k) for k in range(4)]))
    return jnp.concatenate(highs, axis=axis), jnp.concatenate(lows, axis=axis)


def lead_body(ids, v0_ref, v1_ref, s_ref, d_ref, z_ref, i_ref, h_ref, p_ref, vh, vl, dh, dl, total):
    g = pl.program_id(0)

    @pl.when(g == 0)
    def _():
        for j, ref in enumerate((v0_ref, v1_ref)):
            fill_rows(ref, vh.at[j], vl.at[j])
            for k in range(4):
                dh[j, k], dl[j, k] = split(d_ref[j, k])
        total[...] = jnp.zeros_like(total)

    sup = [s_ref[k] for k in range(4)]
    first = [z_ref[k] for k in range(4)]
    for j in range(2):
        ah, al = gather_blocks(ids, 6 * g, sup, lambda k: vh[j, k], lambda k: vl[j, k], 1)
        bh, bl = gather_blocks(ids, 6 * g, first, lambda k: dh[j, k], lambda k: dl[j, k], 1)
        total[...] += product(ah, al, bh, bl, NT)

    @pl.when(g == 3)
    def _():
        ih, il = split(i_ref[...])
        total[:128] += h_ref[...]
        ah, al = split(total[...])
        p_ref[...] = product(ah, al, ih, il, NT)


def lead(ids, v0, v1, s, d, z, inverse, shift):
    whole = lambda v: pl.BlockSpec(v.shape, lambda g, i: (0,) * v.ndim)
    args = [v0, v1, s, d, z, inverse, shift]
    grid = pltpu.PrefetchScalarGridSpec(
        num_scalar_prefetch=1, grid=(4,), in_specs=[whole(v) for v in args], out_specs=pl.BlockSpec((512, 128), lambda g, i: (0, 0)),
        scratch_shapes=[pltpu.VMEM((2, 4, 512, 128), BF)] * 2 + [pltpu.VMEM((2, 4, 128, 128), BF)] * 2 + [pltpu.VMEM((512, 128), F32)])
    return pl.pallas_call(lead_body, grid_spec=grid, out_shape=jax.ShapeDtypeStruct((512, 128), F32),
                          compiler_params=pltpu.CompilerParams(vmem_limit_bytes=VMEM), name="lead",
                          cost_estimate=pl.CostEstimate(flops=2 * 3 * 512 * 6144 * 128, bytes_accessed=6 << 20, transcendentals=0))(ids, *args)


def block_body(has_sum, ids, v_ref, r_ref, c_ref, s_ref, *rest):
    if has_sum:
        a_ref, o_ref, vh, vl, ch, cl = rest
    else:
        o_ref, vh, vl, ch, cl = rest
    g = pl.program_id(0)

    @pl.when(g == 0)
    def _():
        fill_rows(v_ref, vh, vl)
        for t in range(8):
            for k in range(4):
                ch[k, :, t * 128:(t + 1) * 128], cl[k, :, t * 128:(t + 1) * 128] = split(c_ref[t, k * 128:(k + 1) * 128])
        o_ref[...] = a_ref[...] if has_sum else jnp.zeros_like(o_ref)

    rows = [r_ref[k] for k in range(4)]
    ah, al = gather_blocks(ids, 6 * g, rows, lambda k: vh[k], lambda k: vl[k], 1)
    for q in range(2):
        r = slice(q * 512, (q + 1) * 512)
        sup = [jnp.broadcast_to(s_ref[k:k + 1, r], (128, 512)).astype(BF) for k in range(4)]
        bh, bl = gather_blocks(ids, 6 * g, sup, lambda k: ch[k, :, r], lambda k: cl[k, :, r], 0)
        o_ref[:, r] += product(ah, al, bh, bl, NN)


def block_product(ids, v, r, c, s, start=None):
    whole = lambda u: pl.BlockSpec(u.shape, lambda g, i: (0,) * u.ndim)
    args = [v, r, c, s] + ([] if start is None else [start])
    grid = pltpu.PrefetchScalarGridSpec(
        num_scalar_prefetch=1, grid=(4,), in_specs=[whole(u) for u in args], out_specs=pl.BlockSpec((512, 1024), lambda g, i: (0, 0)),
        scratch_shapes=[pltpu.VMEM((4, 512, 128), BF)] * 2 + [pltpu.VMEM((4, 128, 1024), BF)] * 2)
    return pl.pallas_call(functools.partial(block_body, start is not None), grid_spec=grid,
                          out_shape=jax.ShapeDtypeStruct((512, 1024), F32),
                          compiler_params=pltpu.CompilerParams(vmem_limit_bytes=VMEM), name="block",
                          cost_estimate=pl.CostEstimate(flops=2 * 3 * 512 * 3072 * 1024, bytes_accessed=10 << 20, transcendentals=0))(ids, *args)


def inverse_body(c_ref, o_ref):
    n = 128
    row = lax.broadcasted_iota(jnp.int32, (n, n), 0)
    col = lax.broadcasted_iota(jnp.int32, (n, n), 1)
    below = lax.broadcasted_iota(jnp.int32, (n, 1), 0)
    lane = lax.broadcasted_iota(jnp.int32, (1, n), 1)
    o_ref[...] = jnp.concatenate([c_ref[...], jnp.where(row == col, 1.0, 0.0).astype(F32)], axis=1)

    def at(v, k):
        return jnp.sum(jnp.where(lane == k, v, 0.0), axis=1, keepdims=True)

    def step(i, _):
        k = 2 * i
        line0 = o_ref[pl.ds(k, 1), :]
        line1 = o_ref[pl.ds(k + 1, 1), :]
        left = o_ref[:, :n]
        a, b, c = at(line0[:, :n], k), at(line0[:, :n], k + 1), at(line1[:, :n], k + 1)
        col0, col1 = at(left, k), at(left, k + 1)
        s0 = lax.rsqrt(a)
        b = b * s0
        s1 = lax.rsqrt(c - b * b)
        line0 = line0 * s0
        line1 = (line1 - b * line0) * s1
        f0 = jnp.where(below > k + 1, col0 * s0, 0.0)
        f1 = jnp.where(below > k + 1, (col1 - f0 * b) * s1, 0.0)
        o_ref[...] = o_ref[...] - f0 * line0 - f1 * line1
        o_ref[pl.ds(k, 1), :] = line0
        o_ref[pl.ds(k + 1, 1), :] = line1
        return 0

    lax.fori_loop(0, n // 2, step, 0)


def inverse_of(c):
    return pl.pallas_call(inverse_body, out_shape=jax.ShapeDtypeStruct((128, 256), F32), name="inverse",
                          cost_estimate=pl.CostEstimate(flops=2 * 3 * 512 * 3072 * 768, bytes_accessed=1 << 20, transcendentals=0))(c)


def finish_body(where, s_ref, p_ref, q_ref, d_ref, o_ref):
    g = pl.program_id(0)
    r, col = where[0], where[1]
    row = lax.broadcasted_iota(jnp.int32, (128, 128), 0)
    lane = lax.broadcasted_iota(jnp.int32, (128, 128), 1)
    for j in range(2):
        qh, ql = split(q_ref[j])
        across = col * 8 + 2 * g + j
        span = slice(j * 128, (j + 1) * 128)
        for t in range(4):
            ph, plo = split(p_ref[t])
            down = t * 16 + r
            outer = product(ph, plo, qh, ql, NT)
            diagonal = jnp.where((row == lane) & (down == across), jnp.broadcast_to(d_ref[t:t + 1], (128, 128)), 0.0)
            o_ref[t, :, span] = s_ref[t, :, span] + diagonal - jnp.where((down > 0) & (across > 0), outer, 0.0)


def finish(where, s, p, q, d):
    grid = pltpu.PrefetchScalarGridSpec(
        num_scalar_prefetch=1, grid=(4,),
        in_specs=[pl.BlockSpec((4, 128, 256), lambda g, w: (0, 0, g)), pl.BlockSpec((4, 128, 128), lambda g, w: (0, 0, 0)),
                  pl.BlockSpec((2, 128, 128), lambda g, w: (w[2] * 4 + g, 0, 0)), pl.BlockSpec((4, 128), lambda g, w: (0, 0))],
        out_specs=pl.BlockSpec((4, 128, 256), lambda g, w: (0, 0, g)))
    return pl.pallas_call(finish_body, grid_spec=grid, out_shape=jax.ShapeDtypeStruct((4, 128, 1024), F32),
                          compiler_params=pltpu.CompilerParams(vmem_limit_bytes=VMEM), name="finish",
                          cost_estimate=pl.CostEstimate(flops=2 * 3 * 512 * 128 * 1024, bytes_accessed=5 << 20, transcendentals=0))(where, s, p, q, d)


SWAP = [(i, i ^ 1) for i in range(8)]
CHIPS = [[0, 2, 4, 6], [1, 3, 5, 7]]


def swap(v):
    return lax.ppermute(v, "cols", SWAP)


def exchange(v, axis, groups=None):
    return lax.all_to_all(v, axis, 0, 0, axis_index_groups=groups, tiled=True)


def repeat(v, n):
    return jnp.broadcast_to(v[None], (n,) + v.shape)


def lanes(s):
    return jnp.broadcast_to(s[:, :, None], s.shape + (128,))


def local(coefficients, support, primal, dual_inverse, block_sizes, damping, right_sides):
    col = lax.axis_index("cols")
    r = lax.axis_index("rows")
    x = col // 2
    p = col % 2
    sup = support.astype(F32)
    tile = lax.dynamic_index_in_dim(coefficients, x, 0, keepdims=False)
    tile = lax.dynamic_slice_in_dim(tile, p * 128, 128, 2)
    mine = jnp.concatenate([jnp.transpose(tile, (1, 2, 0)).reshape(512, 128),
                            lax.dynamic_index_in_dim(sup, x, 0, keepdims=False).T, jnp.zeros((4, 128), F32)], axis=0)
    gathered = lax.all_gather(mine, "rows")

    positions = jnp.arange(256, dtype=jnp.int32)
    active = (positions[None, :] < block_sizes[:, None]).astype(F32)
    w = primal * dual_inverse * active[:, :, None] * active[:, None, :]
    ids = jnp.arange(24, dtype=jnp.int32)
    owned = (col * 3 + jnp.arange(3)).astype(jnp.int32)
    own = jnp.transpose(coefficients, (2, 0, 1, 3)).reshape(4, 512, 256)
    own_sup = lanes(jnp.transpose(sup, (2, 0, 1)).reshape(4, 512))
    part, corner = partial(owned, own, own_sup, w)
    eye = jnp.eye(128, dtype=F32)

    half = lax.dynamic_index_in_dim(part, p, 0, keepdims=False)
    half = half + swap(lax.dynamic_index_in_dim(part, 1 - p, 0, keepdims=False))
    corner = jnp.sum(exchange(repeat(corner, 8), "cols").reshape(8, 128, 128), axis=0) + eye * damping[0]
    tile_sum = jnp.sum(exchange(half, "cols", CHIPS), axis=0)
    v_own = exchange(repeat(tile_sum, 4), "cols", CHIPS)
    v_other = swap(v_own)
    inverse = exchange(repeat(inverse_of(corner)[:, 128:], 16), "rows")[0]

    head = lax.dynamic_slice_in_dim(lax.dynamic_index_in_dim(coefficients[0], x, 1, keepdims=False), p * 128, 128, 1)
    head = jnp.concatenate([head, sup[0].T, right_sides[0], damping[:1], jnp.zeros((7, 128), F32)], axis=0)
    head = exchange(repeat(head, 16), "rows")[0]
    first = exchange(repeat(head[:128], 8), "cols").reshape(4, 2, 128, 128)
    first = jnp.stack([jnp.where(p == 0, first[:, 0], first[:, 1]), jnp.where(p == 0, first[:, 1], first[:, 0])])
    first_sup = lanes(head[128:132]).astype(BF)
    row_sup = own_sup.astype(BF)
    shift = jnp.where(r == 0, damping[0], 0.0) * eye
    panel_factor = lead(ids, v_own, v_other, row_sup, first, first_sup, inverse, shift).reshape(4, 128, 128)
    every = exchange(repeat(lax.dynamic_index_in_dim(panel_factor, x, 0, keepdims=False), 16), "rows")
    leading = lax.dot_general(head[132:136], inverse, NT, precision=highest)
    remainder = right_sides - jnp.einsum("sk,tak->tsa", leading, panel_factor, precision=highest)
    solved = jnp.where(((jnp.arange(4) > 0) | (r > 0))[:, None, None], remainder, leading[None])

    kept = lax.dynamic_slice_in_dim(gathered, 8 * p, 8, 0)
    swapped = swap(lax.dynamic_slice_in_dim(gathered, 8 * (1 - p), 8, 0))
    col_sup = jnp.pad(jnp.transpose(kept[:, 512:516], (1, 0, 2)).reshape(4, 1024), ((0, 4), (0, 0)))
    out = block_product(ids, v_own, row_sup, kept, col_sup)
    out = block_product(ids, v_other, row_sup, swapped, col_sup, out)
    updated = finish(jnp.stack([r, col, p]).astype(jnp.int32), out.reshape(4, 128, 1024), panel_factor, every, damping)
    return updated, panel_factor, solved


def solution(mesh):
    in_specs = (
        P(None, "rows", None, None),
        P(None, "rows", None),
        P("cols", None, None),
        P("cols", None, None),
        P("cols"),
        P(None, "rows"),
        P(None, "cols", "rows"),
    )
    out_specs = (P(None, "rows", "cols"), P(None, "rows", None), P(None, "cols", "rows"))
    return jax.shard_map(local, mesh=mesh, in_specs=in_specs, out_specs=out_specs, check_vma=False)
```

```python
import functools
import jax
import jax.numpy as jnp
from jax import lax
from jax.experimental import pallas as pl
from jax.experimental.pallas import tpu as pltpu
from jax.sharding import PartitionSpec as P

BF = jnp.bfloat16
F32 = jnp.float32
NT = (((1,), (1,)), ((), ()))
NN = (((1,), (0,)), ((), ()))
VMEM = 56 << 20
highest = lax.Precision.HIGHEST


def split(v):
    h = v.astype(BF)
    return h, (v - h.astype(F32)).astype(BF)


def product(ah, al, bh, bl, dims):
    side = dims[0][1][0]
    left = jnp.concatenate([ah, al, ah], axis=1)
    right = jnp.concatenate([bh, bh, bl], axis=side)
    return lax.dot_general(left, right, dims, preferred_element_type=F32)


def choose(masks, values):
    out = jnp.zeros_like(values[0])
    for m, v in zip(masks, values):
        out = jnp.where(m, v, out)
    return out


def partial_body(info, c_ref, s_ref, w_ref, v_ref, g_ref):
    p = info[2]
    mine = pl.ds(pl.multiple_of(p * 128, 128), 128)
    other = pl.ds(pl.multiple_of((1 - p) * 128, 128), 128)
    total = jnp.zeros((128, 128), F32)
    for u in range(3):
        block = (info[1] * 3 + u).astype(F32)
        w = jnp.concatenate([w_ref[u, :, mine], w_ref[u, :, other]], axis=1)
        wh, wl = split(w)
        m = [s_ref[k] == block for k in range(4)]
        d = jnp.concatenate([choose(m, [c_ref[k, :, q * 128:(q + 1) * 128] for k in range(4)]) for q in range(2)], axis=1)
        dh, dl = split(d)
        v = product(dh, dl, wh, wl, NN)
        vh, vl = split(v[:128])
        top = [z[:128] for z in m]
        e = jnp.concatenate([choose(top, [c_ref[k, :128, h] for k in range(4)]) for h in (mine, other)], axis=1)
        eh, el = split(e)
        total = total + product(vh, vl, eh, el, NT)
        for ref, q in ((v_ref, 0), (g_ref, 1)):
            for t in range(4):
                part = v[t * 128:(t + 1) * 128, q * 128:(q + 1) * 128]
                for k in range(4):
                    before = jnp.zeros_like(part) if u == 0 else ref[t, k]
                    ref[t, k] = jnp.where(m[k][t * 128:(t + 1) * 128], part, before)
    for ref in (v_ref, g_ref):
        for t in range(4):
            ref[t, 4] = total


def whole(v):
    return pl.BlockSpec(v.shape, lambda g, i: (0,) * v.ndim)


def partial(info, c, s, w):
    out = jax.ShapeDtypeStruct((4, 5, 128, 128), F32)
    grid = pltpu.PrefetchScalarGridSpec(num_scalar_prefetch=1, grid=(1,), in_specs=[whole(c), whole(s), whole(w)],
                                        out_specs=[pl.BlockSpec((4, 5, 128, 128), lambda g, i: (0, 0, 0, 0))] * 2)
    return pl.pallas_call(partial_body, grid_spec=grid, out_shape=[out, out],
                          compiler_params=pltpu.CompilerParams(vmem_limit_bytes=VMEM), name="partial",
                          cost_estimate=pl.CostEstimate(flops=2 * 3 * 512 * 768 * 256, bytes_accessed=6 << 20, transcendentals=0))(info, c, s, w)


def gather_blocks(base, sup, high, low, axis):
    highs, lows = [], []
    for u in range(6):
        block = (base + u).astype(F32).astype(BF)
        m = [s == block for s in sup]
        highs.append(choose(m, [high(k) for k in range(4)]))
        lows.append(choose(m, [low(k) for k in range(4)]))
    return jnp.concatenate(highs, axis=axis), jnp.concatenate(lows, axis=axis)


def column_labels(rows, n):
    return jnp.broadcast_to(jnp.concatenate(rows, axis=1), (128, n)).astype(BF)


def lead_body(info, v0_ref, v1_ref, s_ref, d0_ref, d1_ref, a_ref, vh, vl, dh, dl):
    g = pl.program_id(0)
    x = info[3]

    @pl.when(g == 0)
    def _():
        for j, (v_ref, d_ref) in enumerate(((v0_ref, d0_ref), (v1_ref, d1_ref))):
            for k in range(4):
                vh[j, k], vl[j, k] = split(v_ref[x, k])
                dh[j, k], dl[j, k] = split(d_ref[k * 128:(k + 1) * 128])
        a_ref[...] = jnp.zeros_like(a_ref)

    here = pl.ds(pl.multiple_of(x * 128, 128), 128)
    sup = [s_ref[k, here].astype(BF) for k in range(4)]
    first = [column_labels([d0_ref[512 + k:513 + k]], 128) for k in range(4)]
    for j in range(2):
        ah, al = gather_blocks(6 * g, sup, lambda k: vh[j, k], lambda k: vl[j, k], 1)
        bh, bl = gather_blocks(6 * g, first, lambda k: dh[j, k], lambda k: dl[j, k], 0)
        a_ref[...] += product(ah, al, bh, bl, NN)


def lead(info, v0, v1, s, d0, d1):
    args = [v0, v1, s, d0, d1]
    grid = pltpu.PrefetchScalarGridSpec(
        num_scalar_prefetch=1, grid=(4,), in_specs=[whole(v) for v in args], out_specs=pl.BlockSpec((128, 128), lambda g, i: (0, 0)),
        scratch_shapes=[pltpu.VMEM((2, 4, 128, 128), BF)] * 4)
    return pl.pallas_call(lead_body, grid_spec=grid, out_shape=jax.ShapeDtypeStruct((128, 128), F32),
                          compiler_params=pltpu.CompilerParams(vmem_limit_bytes=VMEM), name="lead",
                          cost_estimate=pl.CostEstimate(flops=2 * 3 * 128 * 6144 * 128, bytes_accessed=6 << 20, transcendentals=0))(info, *args)


def block_body(has_sum, info, v_ref, r_ref, c_ref, z_ref, d_ref, *rest):
    if has_sum:
        s_ref, b_ref, o_ref, a_ref, vh, vl, ch, cl = rest
    else:
        o_ref, a_ref, vh, vl, ch, cl = rest
    g = pl.program_id(0)

    @pl.when(g == 0)
    def _():
        for k in range(4):
            for t in range(4):
                vh[k, t * 128:(t + 1) * 128], vl[k, t * 128:(t + 1) * 128] = split(v_ref[t, k])
            for t in range(8):
                ch[k, :, t * 128:(t + 1) * 128], cl[k, :, t * 128:(t + 1) * 128] = split(c_ref[t, k * 128:(k + 1) * 128])
            ch[k, :, 1024:], cl[k, :, 1024:] = split(d_ref[k * 128:(k + 1) * 128])
        o_ref[...] = s_ref[...] if has_sum else jnp.zeros_like(o_ref)
        a_ref[...] = b_ref[...] if has_sum else jnp.zeros_like(a_ref)

    rows = [r_ref[k].astype(BF) for k in range(4)]
    ah, al = gather_blocks(6 * g, rows, lambda k: vh[k], lambda k: vl[k], 1)
    for q in range(3):
        n = 512 if q < 2 else 128
        r = slice(q * 512, q * 512 + n)
        if q < 2:
            sup = [column_labels([c_ref[4 * q + t, 512 + k:513 + k] for t in range(4)], n) for k in range(4)]
        else:
            sup = [column_labels([z_ref[512 + k:513 + k]], n) for k in range(4)]
        bh, bl = gather_blocks(6 * g, sup, lambda k: ch[k, :, r], lambda k: cl[k, :, r], 0)
        value = product(ah, al, bh, bl, NN)
        if q < 2:
            o_ref[:, r] += value
        else:
            a_ref[...] += value


def block_product(info, v, r, c, pick, z, d, start=None):
    args = [v, r, c, z, d] + ([] if start is None else list(start))
    specs = [whole(u) for u in args]
    specs[2] = pl.BlockSpec((8, 520, 128), pick)
    shapes = [(512, 1024), (512, 128)]
    grid = pltpu.PrefetchScalarGridSpec(
        num_scalar_prefetch=1, grid=(4,), in_specs=specs, out_specs=[pl.BlockSpec(u, lambda g, i: (0, 0)) for u in shapes],
        scratch_shapes=[pltpu.VMEM((4, 512, 128), BF)] * 2 + [pltpu.VMEM((4, 128, 1152), BF)] * 2)
    return pl.pallas_call(functools.partial(block_body, start is not None), grid_spec=grid,
                          out_shape=[jax.ShapeDtypeStruct(u, F32) for u in shapes],
                          compiler_params=pltpu.CompilerParams(vmem_limit_bytes=VMEM), name="block",
                          cost_estimate=pl.CostEstimate(flops=2 * 3 * 512 * 3072 * 1152, bytes_accessed=10 << 20, transcendentals=0))(info, *args)


def inverse_body(c_ref, o_ref):
    n = 128
    row = lax.broadcasted_iota(jnp.int32, (n, n), 0)
    col = lax.broadcasted_iota(jnp.int32, (n, n), 1)
    below = lax.broadcasted_iota(jnp.int32, (n, 1), 0)
    lane = lax.broadcasted_iota(jnp.int32, (1, n), 1)
    o_ref[...] = jnp.concatenate([c_ref[...], jnp.where(row == col, 1.0, 0.0).astype(F32)], axis=1)

    def at(v, k):
        return jnp.sum(jnp.where(lane == k, v, 0.0), axis=1, keepdims=True)

    def step(i, _):
        k = 2 * i
        line0 = o_ref[pl.ds(k, 1), :]
        line1 = o_ref[pl.ds(k + 1, 1), :]
        left = o_ref[:, :n]
        a, b, c = at(line0[:, :n], k), at(line0[:, :n], k + 1), at(line1[:, :n], k + 1)
        col0, col1 = at(left, k), at(left, k + 1)
        s0 = lax.rsqrt(a)
        b = b * s0
        s1 = lax.rsqrt(c - b * b)
        line0 = line0 * s0
        line1 = (line1 - b * line0) * s1
        f0 = jnp.where(below > k + 1, col0 * s0, 0.0)
        f1 = jnp.where(below > k + 1, (col1 - f0 * b) * s1, 0.0)
        o_ref[...] = o_ref[...] - f0 * line0 - f1 * line1
        o_ref[pl.ds(k, 1), :] = line0
        o_ref[pl.ds(k + 1, 1), :] = line1
        return 0

    lax.fori_loop(0, n // 2, step, 0)


def inverse_of(c):
    return pl.pallas_call(inverse_body, out_shape=jax.ShapeDtypeStruct((128, 256), F32), name="inverse",
                          cost_estimate=pl.CostEstimate(flops=2 * 3 * 512 * 3072 * 768, bytes_accessed=1 << 20, transcendentals=0))(c)


def finish_body(where, s_ref, p_ref, q_ref, d_ref, o_ref):
    g = pl.program_id(0)
    r, col = where[0], where[1]
    row = lax.broadcasted_iota(jnp.int32, (128, 128), 0)
    lane = lax.broadcasted_iota(jnp.int32, (128, 128), 1)
    for j in range(2):
        qh, ql = split(q_ref[j])
        across = col * 8 + 2 * g + j
        span = slice(j * 128, (j + 1) * 128)
        for t in range(4):
            ph, plo = split(p_ref[t])
            down = t * 16 + r
            outer = product(ph, plo, qh, ql, NT)
            diagonal = jnp.where((row == lane) & (down == across), jnp.broadcast_to(d_ref[t:t + 1], (128, 128)), 0.0)
            o_ref[t, :, span] = s_ref[t, :, span] + diagonal - jnp.where((down > 0) & (across > 0), outer, 0.0)


def finish(where, s, p, q, d):
    grid = pltpu.PrefetchScalarGridSpec(
        num_scalar_prefetch=1, grid=(4,),
        in_specs=[pl.BlockSpec((4, 128, 256), lambda g, w: (0, 0, g)), pl.BlockSpec((4, 128, 128), lambda g, w: (0, 0, 0)),
                  pl.BlockSpec((2, 128, 128), lambda g, w: (g, 0, 0)), pl.BlockSpec((4, 128), lambda g, w: (0, 0))],
        out_specs=pl.BlockSpec((4, 128, 256), lambda g, w: (0, 0, g)))
    return pl.pallas_call(finish_body, grid_spec=grid, out_shape=jax.ShapeDtypeStruct((4, 128, 1024), F32),
                          compiler_params=pltpu.CompilerParams(vmem_limit_bytes=VMEM), name="finish",
                          cost_estimate=pl.CostEstimate(flops=2 * 3 * 512 * 128 * 1024, bytes_accessed=5 << 20, transcendentals=0))(where, s, p, q, d)


SWAP = [(i, i ^ 1) for i in range(8)]
CHIPS = [[0, 2, 4, 6], [1, 3, 5, 7]]


def swap(v):
    return lax.ppermute(v, "cols", SWAP)


def exchange(v, axis, groups=None):
    return lax.all_to_all(v, axis, 0, 0, axis_index_groups=groups, tiled=True)


def repeat(v, n):
    return jnp.broadcast_to(v[None], (n,) + v.shape)


def lanes(s):
    return jnp.broadcast_to(s[:, :, None], s.shape + (128,))


def over_rows(v, pairs):
    return lax.ppermute(v, "rows", pairs)


def spread_first(v, r):
    one = over_rows(v, [(0, 1)])
    three = over_rows(v, [(0, 3)])
    two = over_rows(one, [(1, 2)])
    line = jnp.where(r == 0, v, one + three + two)
    first = over_rows(line, [(z, 4 + z) for z in range(4)])
    third = over_rows(line, [(z, 12 + z) for z in range(4)])
    second = over_rows(first, [(4 + z, 8 + z) for z in range(4)])
    return jnp.where(r < 4, line, first + third + second)


def local(coefficients, support, primal, dual_inverse, block_sizes, damping, right_sides):
    col = lax.axis_index("cols")
    r = lax.axis_index("rows")
    x = col // 2
    p = col % 2
    info = jnp.stack([r, col, p, x]).astype(jnp.int32)
    sup = support.astype(F32)

    def message(t, extra):
        tile = lax.dynamic_index_in_dim(coefficients, t, 0, keepdims=False)
        tile = lax.dynamic_slice_in_dim(tile, p * 128, 128, 2)
        return jnp.concatenate([jnp.transpose(tile, (1, 2, 0)).reshape(512, 128),
                                lax.dynamic_index_in_dim(sup, t, 0, keepdims=False).T, extra], axis=0)

    gathered = lax.all_gather(message(x, jnp.zeros((4, 128), F32)), "rows")

    positions = jnp.arange(256, dtype=jnp.int32)
    active = (positions[None, :] < block_sizes[:, None]).astype(F32)
    w = primal * dual_inverse * active[:, :, None] * active[:, None, :]
    own = jnp.transpose(coefficients, (2, 0, 1, 3)).reshape(4, 512, 256)
    own_sup = lanes(jnp.transpose(sup, (2, 0, 1)).reshape(4, 512))
    kept, given = partial(info, own, own_sup, w)
    half = kept + swap(given)
    total = jnp.sum(exchange(half, "cols", CHIPS), axis=0)
    v_own = exchange(repeat(total[:4], 4), "cols", CHIPS)
    v_other = swap(v_own)
    eye = jnp.eye(128, dtype=F32)
    inverse = inverse_of(total[4] + eye * damping[0])[:, 128:]

    head = spread_first(message(0, right_sides[0]), r)
    head_other = swap(head[:512])
    tile = lead(info, v_own, v_other, own_sup, head, head_other)
    every = exchange(repeat(jnp.concatenate([tile, inverse], axis=0), 16), "rows")

    swapped = swap(lax.dynamic_slice_in_dim(gathered, 8 * (1 - p), 8, 0))
    start = block_product(info, v_own, own_sup, gathered, lambda g, i: (i[2], 0, 0), head, head)
    out, first = block_product(info, v_other, own_sup, swapped, lambda g, i: (0, 0, 0), head, head_other, start)

    every, out, first = lax.optimization_barrier((every, out, first))
    inverse = every[0, 128:]
    tiles = lax.dynamic_slice(every, (8 * p, 0, 0), (8, 128, 128)).reshape(1024, 128)
    col_panel = lax.dot_general(tiles, inverse, NT, precision=highest).reshape(8, 128, 128)
    first = first.at[:128].add(jnp.where(r == 0, damping[0], 0.0) * eye)
    panel_factor = lax.dot_general(first, inverse, NT, precision=highest).reshape(4, 128, 128)
    leading = lax.dot_general(head[516:520], inverse, NT, precision=highest)
    remainder = right_sides - jnp.einsum("sk,tak->tsa", leading, panel_factor, precision=highest)
    solved = jnp.where(((jnp.arange(4) > 0) | (r > 0))[:, None, None], remainder, leading[None])
    updated = finish(info, out.reshape(4, 128, 1024), panel_factor, col_panel, damping)
    return updated, panel_factor, solved


def solution(mesh):
    in_specs = (
        P(None, "rows", None, None),
        P(None, "rows", None),
        P("cols", None, None),
        P("cols", None, None),
        P("cols"),
        P(None, "rows"),
        P(None, "cols", "rows"),
    )
    out_specs = (P(None, "rows", "cols"), P(None, "rows", None), P(None, "cols", "rows"))
    return jax.shard_map(local, mesh=mesh, in_specs=in_specs, out_specs=out_specs, check_vma=False)
```

```python
import functools
import jax
import jax.numpy as jnp
from jax import lax
from jax.experimental import pallas as pl
from jax.experimental.pallas import tpu as pltpu
from jax.sharding import PartitionSpec as P

BF = jnp.bfloat16
F32 = jnp.float32
NT = (((1,), (1,)), ((), ()))
NN = (((1,), (0,)), ((), ()))
VMEM = 56 << 20


def split(v):
    h = v.astype(BF)
    return h, (v - h.astype(F32)).astype(BF)


def product(ah, al, bh, bl, dims):
    side = dims[0][1][0]
    left = jnp.concatenate([ah, al, ah], axis=1)
    right = jnp.concatenate([bh, bh, bl], axis=side)
    return lax.dot_general(left, right, dims, preferred_element_type=F32)


def choose(masks, values):
    out = jnp.zeros_like(values[0])
    for m, v in zip(masks, values):
        out = jnp.where(m, v, out)
    return out


def partial_body(info, c_ref, s_ref, w_ref, v_ref, g_ref):
    p = info[2]
    mine = pl.ds(pl.multiple_of(p * 128, 128), 128)
    other = pl.ds(pl.multiple_of((1 - p) * 128, 128), 128)
    total = jnp.zeros((128, 128), F32)
    for u in range(3):
        block = (info[1] * 3 + u).astype(F32)
        w = jnp.concatenate([w_ref[u, :, mine], w_ref[u, :, other]], axis=1)
        wh, wl = split(w)
        m = [jnp.broadcast_to(s_ref[:, k:k + 1], (512, 128)) == block for k in range(4)]
        d = jnp.concatenate([choose(m, [c_ref[k, :, q * 128:(q + 1) * 128] for k in range(4)]) for q in range(2)], axis=1)
        dh, dl = split(d)
        v = product(dh, dl, wh, wl, NN)
        vh, vl = split(v[:128])
        top = [z[:128] for z in m]
        e = jnp.concatenate([choose(top, [c_ref[k, :128, h] for k in range(4)]) for h in (mine, other)], axis=1)
        eh, el = split(e)
        total = total + product(vh, vl, eh, el, NT)
        for ref, q in ((v_ref, 0), (g_ref, 1)):
            for t in range(4):
                part = v[t * 128:(t + 1) * 128, q * 128:(q + 1) * 128]
                for k in range(4):
                    before = jnp.zeros_like(part) if u == 0 else ref[t, k]
                    ref[t, k] = jnp.where(m[k][t * 128:(t + 1) * 128], part, before)
    for ref in (v_ref, g_ref):
        for t in range(4):
            ref[t, 4] = total


def whole(v):
    return pl.BlockSpec(v.shape, lambda g, i: (0,) * v.ndim)


def partial(info, c, s, w):
    out = jax.ShapeDtypeStruct((4, 5, 128, 128), F32)
    grid = pltpu.PrefetchScalarGridSpec(num_scalar_prefetch=1, grid=(1,), in_specs=[whole(c), whole(s), whole(w)],
                                        out_specs=[pl.BlockSpec((4, 5, 128, 128), lambda g, i: (0, 0, 0, 0))] * 2)
    return pl.pallas_call(partial_body, grid_spec=grid, out_shape=[out, out],
                          compiler_params=pltpu.CompilerParams(vmem_limit_bytes=VMEM), name="partial",
                          cost_estimate=pl.CostEstimate(flops=2 * 3 * 512 * 768 * 256, bytes_accessed=6 << 20, transcendentals=0))(info, c, s, w)


def gather_blocks(base, sup, high, low, axis):
    highs, lows = [], []
    for u in range(6):
        block = (base + u).astype(F32).astype(BF)
        m = [s == block for s in sup]
        highs.append(choose(m, [high(k) for k in range(4)]))
        lows.append(choose(m, [low(k) for k in range(4)]))
    return jnp.concatenate(highs, axis=axis), jnp.concatenate(lows, axis=axis)


def column_labels(rows, n):
    return jnp.broadcast_to(jnp.concatenate(rows, axis=1), (128, n)).astype(BF)


def lead_body(info, v0_ref, v1_ref, s_ref, d0_ref, d1_ref, a_ref, vh, vl, dh, dl, rs):
    g = pl.program_id(0)
    x = info[3]

    @pl.when(g == 0)
    def _():
        for j, (v_ref, d_ref) in enumerate(((v0_ref, d0_ref), (v1_ref, d1_ref))):
            for k in range(4):
                vh[j, k], vl[j, k] = split(v_ref[x, k])
                dh[j, k], dl[j, k] = split(d_ref[k * 128:(k + 1) * 128])
        here = pl.ds(pl.multiple_of(x * 128, 128), 128)
        for k in range(4):
            rs[k] = jnp.broadcast_to(s_ref[here, k:k + 1], (128, 128)).astype(BF)
        a_ref[...] = jnp.zeros_like(a_ref)

    sup = [rs[k] for k in range(4)]
    first = [column_labels([d0_ref[512 + k:513 + k]], 128) for k in range(4)]
    for j in range(2):
        ah, al = gather_blocks(6 * g, sup, lambda k: vh[j, k], lambda k: vl[j, k], 1)
        bh, bl = gather_blocks(6 * g, first, lambda k: dh[j, k], lambda k: dl[j, k], 0)
        a_ref[...] += product(ah, al, bh, bl, NN)


def lead(info, v0, v1, s, d0, d1):
    args = [v0, v1, s, d0, d1]
    grid = pltpu.PrefetchScalarGridSpec(
        num_scalar_prefetch=1, grid=(4,), in_specs=[whole(v) for v in args], out_specs=pl.BlockSpec((128, 128), lambda g, i: (0, 0)),
        scratch_shapes=[pltpu.VMEM((2, 4, 128, 128), BF)] * 4 + [pltpu.VMEM((4, 128, 128), BF)])
    return pl.pallas_call(lead_body, grid_spec=grid, out_shape=jax.ShapeDtypeStruct((128, 128), F32),
                          compiler_params=pltpu.CompilerParams(vmem_limit_bytes=VMEM), name="lead",
                          cost_estimate=pl.CostEstimate(flops=2 * 3 * 128 * 6144 * 128, bytes_accessed=6 << 20, transcendentals=0))(info, *args)


def block_body(last, info, v_ref, r_ref, c_ref, z_ref, d_ref, *rest):
    if last:
        s_ref, b_ref, e_ref, h_ref, y_ref, o_ref, p_ref, x_ref, vh, vl, ch, cl, rs, total = rest
    else:
        o_ref, total, vh, vl, ch, cl, rs = rest
    g = pl.program_id(0)

    @pl.when(g == 0)
    def _():
        for k in range(4):
            rs[k] = jnp.broadcast_to(r_ref[:, k:k + 1], (512, 128)).astype(BF)
            for t in range(4):
                vh[k, t * 128:(t + 1) * 128], vl[k, t * 128:(t + 1) * 128] = split(v_ref[t, k])
            for t in range(8):
                ch[k, :, t * 128:(t + 1) * 128], cl[k, :, t * 128:(t + 1) * 128] = split(c_ref[t, k * 128:(k + 1) * 128])
            ch[k, :, 1024:], cl[k, :, 1024:] = split(d_ref[k * 128:(k + 1) * 128])
        o_ref[...] = s_ref[...] if last else jnp.zeros_like(o_ref)
        total[...] = b_ref[...] if last else jnp.zeros_like(total)

    rows = [rs[k] for k in range(4)]
    ah, al = gather_blocks(6 * g, rows, lambda k: vh[k], lambda k: vl[k], 1)
    for q in range(3):
        n = 512 if q < 2 else 128
        r = slice(q * 512, q * 512 + n)
        if q < 2:
            sup = [column_labels([c_ref[4 * q + t, 512 + k:513 + k] for t in range(4)], n) for k in range(4)]
        else:
            sup = [column_labels([z_ref[512 + k:513 + k]], n) for k in range(4)]
        bh, bl = gather_blocks(6 * g, sup, lambda k: ch[k, :, r], lambda k: cl[k, :, r], 0)
        value = product(ah, al, bh, bl, NN)
        if q < 2:
            o_ref[:, r] += value
        else:
            total[...] += value

    if last:
        @pl.when(g == 3)
        def _():
            row, col, p = info[0], info[1], info[2]
            same = lax.broadcasted_iota(jnp.int32, (128, 128), 0) == lax.broadcasted_iota(jnp.int32, (128, 128), 1)
            ih, il = split(e_ref[8 * (1 - p)])
            total[:128] += jnp.where(same & (row == 0), jnp.broadcast_to(h_ref[:1], (128, 128)), 0.0)
            th, tl = split(total[...])
            panel = product(th, tl, ih, il, NT)
            p_ref[...] = panel
            ph, plo = split(panel)
            zh, zl = split(z_ref[512:520])
            sides = product(zh, zl, ih, il, NT)
            xh, xl = split(sides)
            for t in range(4):
                tile = slice(t * 128, (t + 1) * 128)
                taken = product(xh, xl, ph[tile], plo[tile], NT)
                x_ref[t] = jnp.where(t * 16 + row > 0, y_ref[t] - taken[4:], sides[4:])
            for j in range(8):
                span = slice(j * 128, (j + 1) * 128)
                eh, el = split(e_ref[8 * p + j])
                qh, ql = split(product(eh, el, ih, il, NT))
                outer = product(ph, plo, qh, ql, NT)
                across = col * 8 + j
                for t in range(4):
                    tile = slice(t * 128, (t + 1) * 128)
                    down = t * 16 + row
                    diagonal = jnp.where(same & (down == across), jnp.broadcast_to(h_ref[t:t + 1], (128, 128)), 0.0)
                    o_ref[tile, span] += diagonal - jnp.where((down > 0) & (across > 0), outer[tile], 0.0)


def block_product(info, v, r, c, pick, z, d, tail=None):
    last = tail is not None
    args = [v, r, c, z, d] + (list(tail) if last else [])
    specs = [whole(u) for u in args]
    specs[2] = pl.BlockSpec((8, 520, 128), pick)
    shapes = [(512, 1024), (512, 128)] + ([(4, 4, 128)] if last else [])
    outs = [pl.BlockSpec((512, 1024), lambda g, i: (0, 0)), pl.BlockSpec((512, 128), lambda g, i: (0, 0)),
            pl.BlockSpec((4, 4, 128), lambda g, i: (0, 0, 0))]
    grid = pltpu.PrefetchScalarGridSpec(
        num_scalar_prefetch=1, grid=(4,), in_specs=specs, out_specs=outs[:len(shapes)],
        scratch_shapes=[pltpu.VMEM((4, 512, 128), BF)] * 2 + [pltpu.VMEM((4, 128, 1152), BF)] * 2
        + [pltpu.VMEM((4, 512, 128), BF)] + ([pltpu.VMEM((512, 128), F32)] if last else []))
    return pl.pallas_call(functools.partial(block_body, last), grid_spec=grid,
                          out_shape=[jax.ShapeDtypeStruct(u, F32) for u in shapes],
                          compiler_params=pltpu.CompilerParams(vmem_limit_bytes=VMEM), name="block",
                          cost_estimate=pl.CostEstimate(flops=2 * 3 * 512 * 3072 * 1152, bytes_accessed=10 << 20, transcendentals=0))(info, *args)


def inverse_body(c_ref, o_ref):
    n = 128
    row = lax.broadcasted_iota(jnp.int32, (n, n), 0)
    col = lax.broadcasted_iota(jnp.int32, (n, n), 1)
    below = lax.broadcasted_iota(jnp.int32, (n, 1), 0)
    lane = lax.broadcasted_iota(jnp.int32, (1, n), 1)
    o_ref[...] = jnp.concatenate([c_ref[...], jnp.where(row == col, 1.0, 0.0).astype(F32)], axis=1)

    def at(v, k):
        return jnp.sum(jnp.where(lane == k, v, 0.0), axis=1, keepdims=True)

    def step(i, _):
        k = 2 * i
        line0 = o_ref[pl.ds(k, 1), :]
        line1 = o_ref[pl.ds(k + 1, 1), :]
        left = o_ref[:, :n]
        a, b, c = at(line0[:, :n], k), at(line0[:, :n], k + 1), at(line1[:, :n], k + 1)
        col0, col1 = at(left, k), at(left, k + 1)
        s0 = lax.rsqrt(a)
        b = b * s0
        s1 = lax.rsqrt(c - b * b)
        line0 = line0 * s0
        line1 = (line1 - b * line0) * s1
        f0 = jnp.where(below > k + 1, col0 * s0, 0.0)
        f1 = jnp.where(below > k + 1, (col1 - f0 * b) * s1, 0.0)
        o_ref[...] = o_ref[...] - f0 * line0 - f1 * line1
        o_ref[pl.ds(k, 1), :] = line0
        o_ref[pl.ds(k + 1, 1), :] = line1
        return 0

    lax.fori_loop(0, n // 2, step, 0)


def inverse_of(c):
    return pl.pallas_call(inverse_body, out_shape=jax.ShapeDtypeStruct((128, 256), F32), name="inverse",
                          cost_estimate=pl.CostEstimate(flops=2 * 3 * 512 * 3072 * 768, bytes_accessed=1 << 20, transcendentals=0))(c)


SWAP = [(i, i ^ 1) for i in range(8)]
CHIPS = [[0, 2, 4, 6], [1, 3, 5, 7]]


def swap(v):
    return lax.ppermute(v, "cols", SWAP)


def exchange(v, axis, groups=None):
    return lax.all_to_all(v, axis, 0, 0, axis_index_groups=groups, tiled=True)


def repeat(v, n):
    return jnp.broadcast_to(v[None], (n,) + v.shape)


def over_rows(v, pairs):
    return lax.ppermute(v, "rows", pairs)


def local(coefficients, support, primal, dual_inverse, block_sizes, damping, right_sides):
    col = lax.axis_index("cols")
    r = lax.axis_index("rows")
    x = col // 2
    p = col % 2
    info = jnp.stack([r, col, p, x]).astype(jnp.int32)
    sup = support.astype(F32)

    def message(t, extra):
        tile = lax.dynamic_index_in_dim(coefficients, t, 0, keepdims=False)
        tile = lax.dynamic_slice_in_dim(tile, p * 128, 128, 2)
        return jnp.concatenate([jnp.transpose(tile, (1, 2, 0)).reshape(512, 128),
                                lax.dynamic_index_in_dim(sup, t, 0, keepdims=False).T, extra], axis=0)

    gathered = lax.all_gather(message(x, jnp.zeros((4, 128), F32)), "rows")

    positions = jnp.arange(256, dtype=jnp.int32)
    active = (positions[None, :] < block_sizes[:, None]).astype(F32)
    w = primal * dual_inverse * active[:, :, None] * active[:, None, :]
    own = jnp.transpose(coefficients, (2, 0, 1, 3)).reshape(4, 512, 256)
    own_sup = sup.reshape(512, 4)
    eye = jnp.eye(128, dtype=F32)

    head = jnp.where(r == 0, message(0, right_sides[0]), 0.0)
    head_next = over_rows(head, [(0, 2)])
    kept, given = partial(info, own, own_sup, w)
    head_next, kept, given = lax.optimization_barrier((head_next, kept, given))
    head = head + head_next
    head_next = over_rows(head, [(0, 1), (2, 3)])
    half = kept + swap(given)
    head_next, half = lax.optimization_barrier((head_next, half))
    head = head + head_next
    head_next = over_rows(head, [(z, 8 + z) for z in range(4)])
    terms = exchange(half, "cols", CHIPS)
    head_next, terms = lax.optimization_barrier((head_next, terms))
    head = head + head_next
    head_next = over_rows(head, [(y + z, y + 4 + z) for y in (0, 8) for z in range(4)])
    total = jnp.sum(terms, axis=0)
    v_own = exchange(repeat(total[:4], 4), "cols", CHIPS)
    inverse = inverse_of(total[4] + eye * damping[0])
    head_next, v_own, inverse, gathered = lax.optimization_barrier((head_next, v_own, inverse, gathered))
    v_other = swap(v_own)
    head = head + head_next
    inverse = inverse[:, 128:]
    head_other = swap(head[:512])
    tile = lead(info, v_own, v_other, own_sup, head, head_other)
    sent = jnp.where((r == 0) & (p == 1), inverse, jnp.where((r == 8) & (p == 0), over_rows(inverse, [(0, 8)]), tile))
    every = exchange(repeat(sent, 16), "rows")

    swapped = swap(gathered)
    start = block_product(info, v_own, own_sup, gathered, lambda g, i: (i[2], 0, 0), head, head)
    updated, panel, solved = block_product(info, v_other, own_sup, swapped, lambda g, i: (i[2], 0, 0), head, head_other,
                                           list(start) + [every, damping, right_sides])
    return updated.reshape(4, 128, 1024), panel.reshape(4, 128, 128), solved


def solution(mesh):
    in_specs = (
        P(None, "rows", None, None),
        P(None, "rows", None),
        P("cols", None, None),
        P("cols", None, None),
        P("cols"),
        P(None, "rows"),
        P(None, "cols", "rows"),
    )
    out_specs = (P(None, "rows", "cols"), P(None, "rows", None), P(None, "cols", "rows"))
    return jax.shard_map(local, mesh=mesh, in_specs=in_specs, out_specs=out_specs, check_vma=False)
```

```python
import functools
import jax
import jax.numpy as jnp
from jax import lax
from jax.experimental import pallas as pl
from jax.experimental.pallas import tpu as pltpu
from jax.sharding import PartitionSpec as P

BF = jnp.bfloat16
F32 = jnp.float32
NT = (((1,), (1,)), ((), ()))
NN = (((1,), (0,)), ((), ()))
VMEM = 56 << 20


def split(v):
    h = v.astype(BF)
    return h, (v - h.astype(F32)).astype(BF)


def product(ah, al, bh, bl, dims):
    side = dims[0][1][0]
    left = jnp.concatenate([ah, al, ah], axis=1)
    right = jnp.concatenate([bh, bh, bl], axis=side)
    return lax.dot_general(left, right, dims, preferred_element_type=F32)


def choose(masks, values):
    out = jnp.zeros_like(values[0])
    for m, v in zip(masks, values):
        out = jnp.where(m, v, out)
    return out


def partial_body(info, c_ref, s_ref, x_ref, y_ref, v_ref, g_ref, wh, wl, total):
    t = pl.program_id(0)
    p = info[2]
    mine = pl.ds(pl.multiple_of(p * 128, 128), 128)
    other = pl.ds(pl.multiple_of((1 - p) * 128, 128), 128)

    @pl.when(t == 0)
    def _():
        row = lax.broadcasted_iota(jnp.int32, (256, 128), 0)
        lane = lax.broadcasted_iota(jnp.int32, (256, 128), 1)
        for u in range(3):
            size = info[4 + u]
            for q, (h, base) in enumerate(((mine, p * 128), (other, (1 - p) * 128))):
                w = jnp.where((row < size) & (lane + base < size), x_ref[u, :, h] * y_ref[u, :, h], 0.0)
                wh[u, :, q * 128:(q + 1) * 128], wl[u, :, q * 128:(q + 1) * 128] = split(w)

    corner = jnp.zeros((128, 128), F32)
    parts = [None] * 8
    for u in range(3):
        block = (info[1] * 3 + u).astype(F32)
        m = [s_ref[k] == block for k in range(4)]
        d = jnp.concatenate([choose(m, [c_ref[k, :, q * 128:(q + 1) * 128] for k in range(4)]) for q in range(2)], axis=1)
        dh, dl = split(d)
        v = product(dh, dl, wh[u], wl[u], NN)
        vh, vl = split(v)
        e = jnp.concatenate([choose(m, [c_ref[k, :, h] for k in range(4)]) for h in (mine, other)], axis=1)
        eh, el = split(e)
        corner = corner + product(vh, vl, eh, el, NT)
        for q in range(2):
            part = v[:, q * 128:(q + 1) * 128]
            for k in range(4):
                before = jnp.zeros_like(part) if u == 0 else parts[4 * q + k]
                parts[4 * q + k] = jnp.where(m[k], part, before)

    @pl.when(t == 0)
    def _():
        total[...] = corner

    for q, ref in enumerate((v_ref, g_ref)):
        for k in range(4):
            ref[0, k] = parts[4 * q + k]
        ref[0, 4] = total[...]


def whole(v):
    return pl.BlockSpec(v.shape, lambda g, i: (0,) * v.ndim)


def partial(info, c, s, x, y):
    out = jax.ShapeDtypeStruct((4, 5, 128, 128), F32)
    grid = pltpu.PrefetchScalarGridSpec(
        num_scalar_prefetch=1, grid=(4,),
        in_specs=[pl.BlockSpec((4, 128, 256), lambda t, i: (0, t, 0)), pl.BlockSpec((4, 128, 128), lambda t, i: (0, t, 0)), whole(x), whole(y)],
        out_specs=[pl.BlockSpec((1, 5, 128, 128), lambda t, i: (t, 0, 0, 0))] * 2,
        scratch_shapes=[pltpu.VMEM((3, 256, 256), BF)] * 2 + [pltpu.VMEM((128, 128), F32)])
    return pl.pallas_call(partial_body, grid_spec=grid, out_shape=[out, out],
                          compiler_params=pltpu.CompilerParams(vmem_limit_bytes=VMEM), name="partial",
                          cost_estimate=pl.CostEstimate(flops=2 * 3 * 512 * 768 * 256, bytes_accessed=8 << 20, transcendentals=0))(info, c, s, x, y)


def gather_blocks(base, sup, high, low, axis):
    highs, lows = [], []
    for u in range(6):
        block = (base + u).astype(F32).astype(BF)
        m = [s == block for s in sup]
        highs.append(choose(m, [high(k) for k in range(4)]))
        lows.append(choose(m, [low(k) for k in range(4)]))
    return jnp.concatenate(highs, axis=axis), jnp.concatenate(lows, axis=axis)


def column_labels(rows, n):
    return jnp.broadcast_to(jnp.concatenate(rows, axis=1), (128, n)).astype(BF)


def lead_body(info, v0_ref, v1_ref, s_ref, d0_ref, d1_ref, f_ref, n_ref, o_ref, vh, vl, dh, dl, a_ref):
    g = pl.program_id(0)

    @pl.when(g == 0)
    def _():
        for j, (v_ref, d_ref) in enumerate(((v0_ref, d0_ref), (v1_ref, d1_ref))):
            for k in range(4):
                vh[j, k], vl[j, k] = split(v_ref[0, k])
                dh[j, k], dl[j, k] = split(d_ref[k * 128:(k + 1) * 128])
        a_ref[...] = jnp.zeros_like(a_ref)

    sup = [s_ref[k].astype(BF) for k in range(4)]
    first = [column_labels([d0_ref[512 + k:513 + k]], 128) for k in range(4)]
    for j in range(2):
        ah, al = gather_blocks(6 * g, sup, lambda k: vh[j, k], lambda k: vl[j, k], 1)
        bh, bl = gather_blocks(6 * g, first, lambda k: dh[j, k], lambda k: dl[j, k], 0)
        a_ref[...] += product(ah, al, bh, bl, NN)

    @pl.when(g == 3)
    def _():
        r, p = info[0], info[2]
        sent = jnp.where((r == 0) & (p == 1), f_ref[...], jnp.where((r == 8) & (p == 0), n_ref[...], a_ref[...]))
        for j in range(16):
            o_ref[j] = sent


def lead(info, v0, v1, s, d0, d1, f, n):
    args = [v0, v1, s, d0, d1, f, n]
    specs = [whole(v) for v in args]
    specs[0] = specs[1] = pl.BlockSpec((1, 4, 128, 128), lambda g, i: (i[3], 0, 0, 0))
    specs[2] = pl.BlockSpec((4, 128, 128), lambda g, i: (0, i[3], 0))
    grid = pltpu.PrefetchScalarGridSpec(
        num_scalar_prefetch=1, grid=(4,), in_specs=specs, out_specs=pl.BlockSpec((16, 128, 128), lambda g, i: (0, 0, 0)),
        scratch_shapes=[pltpu.VMEM((2, 4, 128, 128), BF)] * 4 + [pltpu.VMEM((128, 128), F32)])
    return pl.pallas_call(lead_body, grid_spec=grid, out_shape=jax.ShapeDtypeStruct((16, 128, 128), F32),
                          compiler_params=pltpu.CompilerParams(vmem_limit_bytes=VMEM), name="lead",
                          cost_estimate=pl.CostEstimate(flops=2 * 3 * 128 * 6144 * 128, bytes_accessed=6 << 20, transcendentals=0))(info, *args)


def block_body(last, info, v_ref, r_ref, c_ref, z_ref, d_ref, *rest):
    if last:
        s_ref, b_ref, e_ref, h_ref, y_ref, o_ref, p_ref, x_ref, vh, vl, ch, cl, total = rest
    else:
        o_ref, total, vh, vl, ch, cl = rest
    g = pl.program_id(0)

    @pl.when(g == 0)
    def _():
        for k in range(4):
            for t in range(4):
                vh[k, t * 128:(t + 1) * 128], vl[k, t * 128:(t + 1) * 128] = split(v_ref[t, k])
            for t in range(8):
                ch[k, :, t * 128:(t + 1) * 128], cl[k, :, t * 128:(t + 1) * 128] = split(c_ref[t, k * 128:(k + 1) * 128])
            ch[k, :, 1024:], cl[k, :, 1024:] = split(d_ref[k * 128:(k + 1) * 128])
        o_ref[...] = s_ref[...] if last else jnp.zeros_like(o_ref)
        total[...] = b_ref[...] if last else jnp.zeros_like(total)

    rows = [r_ref[k].astype(BF) for k in range(4)]
    ah, al = gather_blocks(6 * g, rows, lambda k: vh[k], lambda k: vl[k], 1)
    for q in range(3):
        n = 512 if q < 2 else 128
        r = slice(q * 512, q * 512 + n)
        if q < 2:
            sup = [column_labels([c_ref[4 * q + t, 512 + k:513 + k] for t in range(4)], n) for k in range(4)]
        else:
            sup = [column_labels([z_ref[512 + k:513 + k]], n) for k in range(4)]
        bh, bl = gather_blocks(6 * g, sup, lambda k: ch[k, :, r], lambda k: cl[k, :, r], 0)
        value = product(ah, al, bh, bl, NN)
        if q < 2:
            o_ref[:, r] += value
        else:
            total[...] += value

    if last:
        @pl.when(g == 3)
        def _():
            row, col, p = info[0], info[1], info[2]
            same = lax.broadcasted_iota(jnp.int32, (128, 128), 0) == lax.broadcasted_iota(jnp.int32, (128, 128), 1)
            ih, il = split(e_ref[8 * (1 - p)])
            total[:128] += jnp.where(same & (row == 0), jnp.broadcast_to(h_ref[:1], (128, 128)), 0.0)
            th, tl = split(total[...])
            panel = product(th, tl, ih, il, NT)
            p_ref[...] = panel
            ph, plo = split(panel)
            zh, zl = split(z_ref[512:520])
            sides = product(zh, zl, ih, il, NT)
            xh, xl = split(sides)
            for t in range(4):
                tile = slice(t * 128, (t + 1) * 128)
                taken = product(xh, xl, ph[tile], plo[tile], NT)
                x_ref[t] = jnp.where(t * 16 + row > 0, y_ref[t] - taken[4:], sides[4:])
            for j in range(8):
                span = slice(j * 128, (j + 1) * 128)
                eh, el = split(e_ref[8 * p + j])
                qh, ql = split(product(eh, el, ih, il, NT))
                outer = product(ph, plo, qh, ql, NT)
                across = col * 8 + j
                for t in range(4):
                    tile = slice(t * 128, (t + 1) * 128)
                    down = t * 16 + row
                    diagonal = jnp.where(same & (down == across), jnp.broadcast_to(h_ref[t:t + 1], (128, 128)), 0.0)
                    o_ref[tile, span] += diagonal - jnp.where((down > 0) & (across > 0), outer[tile], 0.0)


def block_product(info, v, r, c, pick, z, d, tail=None):
    last = tail is not None
    args = [v, r, c, z, d] + (list(tail) if last else [])
    specs = [whole(u) for u in args]
    specs[2] = pl.BlockSpec((8, 520, 128), pick)
    shapes = [(512, 1024), (512, 128)] + ([(4, 4, 128)] if last else [])
    outs = [pl.BlockSpec((512, 1024), lambda g, i: (0, 0)), pl.BlockSpec((512, 128), lambda g, i: (0, 0)),
            pl.BlockSpec((4, 4, 128), lambda g, i: (0, 0, 0))]
    grid = pltpu.PrefetchScalarGridSpec(
        num_scalar_prefetch=1, grid=(4,), in_specs=specs, out_specs=outs[:len(shapes)],
        scratch_shapes=[pltpu.VMEM((4, 512, 128), BF)] * 2 + [pltpu.VMEM((4, 128, 1152), BF)] * 2
        + ([pltpu.VMEM((512, 128), F32)] if last else []))
    return pl.pallas_call(functools.partial(block_body, last), grid_spec=grid,
                          out_shape=[jax.ShapeDtypeStruct(u, F32) for u in shapes],
                          compiler_params=pltpu.CompilerParams(vmem_limit_bytes=VMEM), name="block",
                          cost_estimate=pl.CostEstimate(flops=2 * 3 * 512 * 3072 * 1152, bytes_accessed=10 << 20, transcendentals=0))(info, *args)


def inverse_body(c_ref, i_ref, o_ref):
    n = 128
    row = lax.broadcasted_iota(jnp.int32, (n, n), 0)
    col = lax.broadcasted_iota(jnp.int32, (n, n), 1)
    below = lax.broadcasted_iota(jnp.int32, (n, 1), 0)
    lane = lax.broadcasted_iota(jnp.int32, (1, n), 1)
    o_ref[...] = jnp.concatenate([c_ref[...], jnp.where(row == col, 1.0, 0.0).astype(F32)], axis=1)

    def at(v, k):
        return jnp.sum(jnp.where(lane == k, v, 0.0), axis=1, keepdims=True)

    def step(i, _):
        k = 2 * i
        line0 = o_ref[pl.ds(k, 1), :]
        line1 = o_ref[pl.ds(k + 1, 1), :]
        left = o_ref[:, :n]
        a, b, c = at(line0[:, :n], k), at(line0[:, :n], k + 1), at(line1[:, :n], k + 1)
        col0, col1 = at(left, k), at(left, k + 1)
        s0 = lax.rsqrt(a)
        b = b * s0
        s1 = lax.rsqrt(c - b * b)
        line0 = line0 * s0
        line1 = (line1 - b * line0) * s1
        f0 = jnp.where(below > k + 1, col0 * s0, 0.0)
        f1 = jnp.where(below > k + 1, (col1 - f0 * b) * s1, 0.0)
        o_ref[...] = o_ref[...] - f0 * line0 - f1 * line1
        o_ref[pl.ds(k, 1), :] = line0
        o_ref[pl.ds(k + 1, 1), :] = line1
        return 0

    lax.fori_loop(0, n // 2, step, 0)
    i_ref[...] = o_ref[:, n:]


def inverse_of(c):
    return pl.pallas_call(inverse_body, out_shape=jax.ShapeDtypeStruct((128, 128), F32), name="inverse",
                          scratch_shapes=[pltpu.VMEM((128, 256), F32)],
                          cost_estimate=pl.CostEstimate(flops=2 * 3 * 512 * 3072 * 768, bytes_accessed=1 << 20, transcendentals=0))(c)


SWAP = [(i, i ^ 1) for i in range(8)]
CHIPS = [[0, 2, 4, 6], [1, 3, 5, 7]]


def swap(v):
    return lax.ppermute(v, "cols", SWAP)


def exchange(v, axis, groups=None):
    return lax.all_to_all(v, axis, 0, 0, axis_index_groups=groups, tiled=True)


def repeat(v, n):
    return jnp.broadcast_to(v[None], (n,) + v.shape)


def over_rows(v, pairs):
    return lax.ppermute(v, "rows", pairs)


def local(coefficients, support, primal, dual_inverse, block_sizes, damping, right_sides):
    col = lax.axis_index("cols")
    r = lax.axis_index("rows")
    x = col // 2
    p = col % 2
    info = jnp.concatenate([jnp.stack([r, col, p, x]).astype(jnp.int32), block_sizes])
    sup = support.astype(F32)

    def message(t, extra):
        tile = lax.dynamic_index_in_dim(coefficients, t, 0, keepdims=False)
        tile = lax.dynamic_slice_in_dim(tile, p * 128, 128, 2)
        return jnp.concatenate([jnp.transpose(tile, (1, 2, 0)).reshape(512, 128),
                                lax.dynamic_index_in_dim(sup, t, 0, keepdims=False).T, extra], axis=0)

    gathered = lax.all_gather(message(x, jnp.zeros((4, 128), F32)), "rows")

    own = jnp.transpose(coefficients, (2, 0, 1, 3)).reshape(4, 512, 256)
    own_sup = jnp.transpose(sup, (2, 0, 1)).reshape(4, 512)
    own_sup = jnp.broadcast_to(own_sup[:, :, None], (4, 512, 128))
    eye = jnp.eye(128, dtype=F32)

    head = jnp.where(r == 0, message(0, right_sides[0]), 0.0)
    head_next = over_rows(head, [(0, 2)])
    kept, given = partial(info, own, own_sup, primal, dual_inverse)
    head_next, kept, given = lax.optimization_barrier((head_next, kept, given))
    head = head + head_next
    head_next = over_rows(head, [(0, 1), (2, 3)])
    half = kept + swap(given)
    head_next, half = lax.optimization_barrier((head_next, half))
    head = head + head_next
    head_next = over_rows(head, [(z, 8 + z) for z in range(4)])
    terms = exchange(half, "cols", CHIPS)
    head_next, terms = lax.optimization_barrier((head_next, terms))
    head = head + head_next
    head_next = over_rows(head, [(y + z, y + 4 + z) for y in (0, 8) for z in range(4)])
    total = jnp.sum(terms, axis=0)
    v_own = exchange(repeat(total[:4], 4), "cols", CHIPS)
    inverse = inverse_of(total[4] + eye * damping[0])
    head_next, v_own, inverse, gathered = lax.optimization_barrier((head_next, v_own, inverse, gathered))
    v_other = swap(v_own)
    head = head + head_next
    head_other = swap(head)
    second = over_rows(inverse, [(0, 8)])
    gathered, v_other, head_other, second = lax.optimization_barrier((gathered, v_other, head_other, second))
    swapped = swap(gathered)
    every = exchange(lead(info, v_own, v_other, own_sup, head, head_other, inverse, second), "rows")

    start = block_product(info, v_own, own_sup, gathered, lambda g, i: (i[2], 0, 0), head, head)
    updated, panel, solved = block_product(info, v_other, own_sup, swapped, lambda g, i: (i[2], 0, 0), head, head_other,
                                           list(start) + [every, damping, right_sides])
    return updated.reshape(4, 128, 1024), panel.reshape(4, 128, 128), solved


def solution(mesh):
    in_specs = (
        P(None, "rows", None, None),
        P(None, "rows", None),
        P("cols", None, None),
        P("cols", None, None),
        P("cols"),
        P(None, "rows"),
        P(None, "cols", "rows"),
    )
    out_specs = (P(None, "rows", "cols"), P(None, "rows", None), P(None, "cols", "rows"))
    return jax.shard_map(local, mesh=mesh, in_specs=in_specs, out_specs=out_specs, check_vma=False)
```

```python
import functools
import jax
import jax.numpy as jnp
from jax import lax
from jax.experimental import pallas as pl
from jax.experimental.pallas import tpu as pltpu
from jax.sharding import PartitionSpec as P

BF = jnp.bfloat16
F32 = jnp.float32
NT = (((1,), (1,)), ((), ()))
NN = (((1,), (0,)), ((), ()))
VMEM = 56 << 20


def split(v):
    h = v.astype(BF)
    return h, (v - h.astype(F32)).astype(BF)


def product(ah, al, bh, bl, dims):
    side = dims[0][1][0]
    left = jnp.concatenate([ah, al, ah], axis=1)
    right = jnp.concatenate([bh, bh, bl], axis=side)
    return lax.dot_general(left, right, dims, preferred_element_type=F32)


def choose(masks, values):
    out = jnp.zeros_like(values[0])
    for m, v in zip(masks, values):
        out = jnp.where(m, v, out)
    return out


def partial_body(info, c_ref, s_ref, x_ref, y_ref, z_ref, v_ref, wh, wl, total):
    t = pl.program_id(0)
    col, p = info[1], info[2]
    mine = pl.ds(pl.multiple_of(p * 128, 128), 128)

    @pl.when(t == 0)
    def _():
        row = lax.broadcasted_iota(jnp.int32, (256, 128), 0)
        lane = lax.broadcasted_iota(jnp.int32, (256, 128), 1)
        for u in range(3):
            size = info[4 + u]
            w = jnp.where((row < size) & (lane + p * 128 < size), x_ref[u, :, mine] * y_ref[u, :, mine], 0.0)
            wh[u], wl[u] = split(w)
            wh[3 + u], wl[3 + u] = split(z_ref[u])

    parts = [jnp.zeros((128, 128), F32)] * 4
    masks = []
    for u in range(6):
        block = ((col if u < 3 else col + 1 - 2 * p) * 3 + u % 3).astype(F32)
        m = [s_ref[k] == block for k in range(4)]
        masks.append(m)
        d = jnp.concatenate([choose(m, [c_ref[k, :, q * 128:(q + 1) * 128] for k in range(4)]) for q in range(2)], axis=1)
        dh, dl = split(d)
        v = product(dh, dl, wh[u], wl[u], NN)
        parts = [jnp.where(m[k], v, parts[k]) for k in range(4)]
    for k in range(4):
        v_ref[0, k] = parts[k]

    @pl.when(t == 0)
    def _():
        vs, es = [], []
        for m in masks:
            vs.append(choose(m, parts))
            es.append(choose(m, [c_ref[k, :, mine] for k in range(4)]))
        vh, vl = split(jnp.concatenate(vs, axis=1))
        eh, el = split(jnp.concatenate(es, axis=1))
        total[...] = product(vh, vl, eh, el, NT)

    v_ref[0, 4] = total[...]


def whole(v):
    return pl.BlockSpec(v.shape, lambda g, i: (0,) * v.ndim)


def partial(info, c, s, x, y, z):
    out = jax.ShapeDtypeStruct((4, 5, 128, 128), F32)
    grid = pltpu.PrefetchScalarGridSpec(
        num_scalar_prefetch=1, grid=(4,),
        in_specs=[pl.BlockSpec((4, 128, 256), lambda t, i: (0, t, 0)), pl.BlockSpec((4, 128, 128), lambda t, i: (0, t, 0)), whole(x), whole(y), whole(z)],
        out_specs=pl.BlockSpec((1, 5, 128, 128), lambda t, i: (t, 0, 0, 0)),
        scratch_shapes=[pltpu.VMEM((6, 256, 128), BF)] * 2 + [pltpu.VMEM((128, 128), F32)])
    return pl.pallas_call(partial_body, grid_spec=grid, out_shape=out,
                          compiler_params=pltpu.CompilerParams(vmem_limit_bytes=VMEM), name="partial",
                          cost_estimate=pl.CostEstimate(flops=2 * 3 * 512 * 768 * 256, bytes_accessed=8 << 20, transcendentals=0))(info, c, s, x, y, z)


def gather_blocks(base, sup, high, low, axis):
    highs, lows = [], []
    for u in range(6):
        block = (base + u).astype(F32).astype(BF)
        m = [s == block for s in sup]
        highs.append(choose(m, [high(k) for k in range(4)]))
        lows.append(choose(m, [low(k) for k in range(4)]))
    return jnp.concatenate(highs, axis=axis), jnp.concatenate(lows, axis=axis)


def column_labels(rows, n):
    return jnp.broadcast_to(jnp.concatenate(rows, axis=1), (128, n)).astype(BF)


def lead_body(info, v0_ref, v1_ref, s_ref, d0_ref, d1_ref, f_ref, n_ref, o_ref, vh, vl, dh, dl, a_ref):
    g = pl.program_id(0)

    @pl.when(g == 0)
    def _():
        for j, (v_ref, d_ref) in enumerate(((v0_ref, d0_ref), (v1_ref, d1_ref))):
            for k in range(4):
                vh[j, k], vl[j, k] = split(v_ref[0, k])
                dh[j, k], dl[j, k] = split(d_ref[k * 128:(k + 1) * 128])
        a_ref[...] = jnp.zeros_like(a_ref)

    sup = [s_ref[k].astype(BF) for k in range(4)]
    first = [column_labels([d0_ref[512 + k:513 + k]], 128) for k in range(4)]
    for j in range(2):
        ah, al = gather_blocks(6 * g, sup, lambda k: vh[j, k], lambda k: vl[j, k], 1)
        bh, bl = gather_blocks(6 * g, first, lambda k: dh[j, k], lambda k: dl[j, k], 0)
        a_ref[...] += product(ah, al, bh, bl, NN)

    @pl.when(g == 3)
    def _():
        r, p = info[0], info[2]
        sent = jnp.where((r == 0) & (p == 1), f_ref[...], jnp.where((r == 8) & (p == 0), n_ref[...], a_ref[...]))
        for j in range(16):
            o_ref[j] = sent


def lead(info, v0, v1, s, d0, d1, f, n):
    args = [v0, v1, s, d0, d1, f, n]
    specs = [whole(v) for v in args]
    specs[0] = specs[1] = pl.BlockSpec((1, 4, 128, 128), lambda g, i: (i[3], 0, 0, 0))
    specs[2] = pl.BlockSpec((4, 128, 128), lambda g, i: (0, i[3], 0))
    grid = pltpu.PrefetchScalarGridSpec(
        num_scalar_prefetch=1, grid=(4,), in_specs=specs, out_specs=pl.BlockSpec((16, 128, 128), lambda g, i: (0, 0, 0)),
        scratch_shapes=[pltpu.VMEM((2, 4, 128, 128), BF)] * 4 + [pltpu.VMEM((128, 128), F32)])
    return pl.pallas_call(lead_body, grid_spec=grid, out_shape=jax.ShapeDtypeStruct((16, 128, 128), F32),
                          compiler_params=pltpu.CompilerParams(vmem_limit_bytes=VMEM), name="lead",
                          cost_estimate=pl.CostEstimate(flops=2 * 3 * 128 * 6144 * 128, bytes_accessed=6 << 20, transcendentals=0))(info, *args)


def block_body(last, info, v_ref, r_ref, c_ref, z_ref, d_ref, *rest):
    if last:
        s_ref, b_ref, e_ref, h_ref, y_ref, o_ref, p_ref, x_ref, vh, vl, ch, cl, total = rest
    else:
        o_ref, total, vh, vl, ch, cl = rest
    g = pl.program_id(0)

    @pl.when(g == 0)
    def _():
        for k in range(4):
            for t in range(4):
                vh[k, t * 128:(t + 1) * 128], vl[k, t * 128:(t + 1) * 128] = split(v_ref[t, k])
            for t in range(8):
                ch[k, :, t * 128:(t + 1) * 128], cl[k, :, t * 128:(t + 1) * 128] = split(c_ref[t, k * 128:(k + 1) * 128])
            ch[k, :, 1024:], cl[k, :, 1024:] = split(d_ref[k * 128:(k + 1) * 128])
        o_ref[...] = s_ref[...] if last else jnp.zeros_like(o_ref)
        total[...] = b_ref[...] if last else jnp.zeros_like(total)

    rows = [r_ref[k].astype(BF) for k in range(4)]
    ah, al = gather_blocks(6 * g, rows, lambda k: vh[k], lambda k: vl[k], 1)
    for q in range(3):
        n = 512 if q < 2 else 128
        r = slice(q * 512, q * 512 + n)
        if q < 2:
            sup = [column_labels([c_ref[4 * q + t, 512 + k:513 + k] for t in range(4)], n) for k in range(4)]
        else:
            sup = [column_labels([z_ref[512 + k:513 + k]], n) for k in range(4)]
        bh, bl = gather_blocks(6 * g, sup, lambda k: ch[k, :, r], lambda k: cl[k, :, r], 0)
        value = product(ah, al, bh, bl, NN)
        if q < 2:
            o_ref[:, r] += value
        else:
            total[...] += value

    if last:
        @pl.when(g == 3)
        def _():
            row, col, p = info[0], info[1], info[2]
            same = lax.broadcasted_iota(jnp.int32, (128, 128), 0) == lax.broadcasted_iota(jnp.int32, (128, 128), 1)
            ih, il = split(e_ref[8 * (1 - p)])
            total[:128] += jnp.where(same & (row == 0), jnp.broadcast_to(h_ref[:1], (128, 128)), 0.0)
            th, tl = split(total[...])
            panel = product(th, tl, ih, il, NT)
            p_ref[...] = panel
            ph, plo = split(panel)
            zh, zl = split(z_ref[512:520])
            sides = product(zh, zl, ih, il, NT)
            xh, xl = split(sides)
            for t in range(4):
                tile = slice(t * 128, (t + 1) * 128)
                taken = product(xh, xl, ph[tile], plo[tile], NT)
                x_ref[t] = jnp.where(t * 16 + row > 0, y_ref[t] - taken[4:], sides[4:])
            for j in range(8):
                span = slice(j * 128, (j + 1) * 128)
                eh, el = split(e_ref[8 * p + j])
                qh, ql = split(product(eh, el, ih, il, NT))
                outer = product(ph, plo, qh, ql, NT)
                across = col * 8 + j
                for t in range(4):
                    tile = slice(t * 128, (t + 1) * 128)
                    down = t * 16 + row
                    diagonal = jnp.where(same & (down == across), jnp.broadcast_to(h_ref[t:t + 1], (128, 128)), 0.0)
                    o_ref[tile, span] += diagonal - jnp.where((down > 0) & (across > 0), outer[tile], 0.0)


def block_product(info, v, r, c, pick, z, d, tail=None):
    last = tail is not None
    args = [v, r, c, z, d] + (list(tail) if last else [])
    specs = [whole(u) for u in args]
    specs[2] = pl.BlockSpec((8, 520, 128), pick)
    shapes = [(512, 1024), (512, 128)] + ([(4, 4, 128)] if last else [])
    outs = [pl.BlockSpec((512, 1024), lambda g, i: (0, 0)), pl.BlockSpec((512, 128), lambda g, i: (0, 0)),
            pl.BlockSpec((4, 4, 128), lambda g, i: (0, 0, 0))]
    grid = pltpu.PrefetchScalarGridSpec(
        num_scalar_prefetch=1, grid=(4,), in_specs=specs, out_specs=outs[:len(shapes)],
        scratch_shapes=[pltpu.VMEM((4, 512, 128), BF)] * 2 + [pltpu.VMEM((4, 128, 1152), BF)] * 2
        + ([pltpu.VMEM((512, 128), F32)] if last else []))
    return pl.pallas_call(functools.partial(block_body, last), grid_spec=grid,
                          out_shape=[jax.ShapeDtypeStruct(u, F32) for u in shapes],
                          compiler_params=pltpu.CompilerParams(vmem_limit_bytes=VMEM), name="block",
                          cost_estimate=pl.CostEstimate(flops=2 * 3 * 512 * 3072 * 1152, bytes_accessed=10 << 20, transcendentals=0))(info, *args)


def inverse_body(c_ref, i_ref, o_ref):
    n = 128
    row = lax.broadcasted_iota(jnp.int32, (n, n), 0)
    col = lax.broadcasted_iota(jnp.int32, (n, n), 1)
    below = lax.broadcasted_iota(jnp.int32, (n, 1), 0)
    lane = lax.broadcasted_iota(jnp.int32, (1, n), 1)
    o_ref[...] = jnp.concatenate([c_ref[...], jnp.where(row == col, 1.0, 0.0).astype(F32)], axis=1)

    def at(v, k):
        return jnp.sum(jnp.where(lane == k, v, 0.0), axis=1, keepdims=True)

    def step(i, _):
        k = 2 * i
        line0 = o_ref[pl.ds(k, 1), :]
        line1 = o_ref[pl.ds(k + 1, 1), :]
        left = o_ref[:, :n]
        a, b, c = at(line0[:, :n], k), at(line0[:, :n], k + 1), at(line1[:, :n], k + 1)
        col0, col1 = at(left, k), at(left, k + 1)
        s0 = lax.rsqrt(a)
        b = b * s0
        s1 = lax.rsqrt(c - b * b)
        line0 = line0 * s0
        line1 = (line1 - b * line0) * s1
        f0 = jnp.where(below > k + 1, col0 * s0, 0.0)
        f1 = jnp.where(below > k + 1, (col1 - f0 * b) * s1, 0.0)
        o_ref[...] = o_ref[...] - f0 * line0 - f1 * line1
        o_ref[pl.ds(k, 1), :] = line0
        o_ref[pl.ds(k + 1, 1), :] = line1
        return 0

    lax.fori_loop(0, n // 2, step, 0)
    i_ref[...] = o_ref[:, n:]


def inverse_of(c):
    return pl.pallas_call(inverse_body, out_shape=jax.ShapeDtypeStruct((128, 128), F32), name="inverse",
                          scratch_shapes=[pltpu.VMEM((128, 256), F32)],
                          cost_estimate=pl.CostEstimate(flops=2 * 3 * 512 * 3072 * 768, bytes_accessed=1 << 20, transcendentals=0))(c)


SWAP = [(i, i ^ 1) for i in range(8)]
CHIPS = [[0, 2, 4, 6], [1, 3, 5, 7]]


def swap(v):
    return lax.ppermute(v, "cols", SWAP)


def exchange(v, axis, groups=None):
    return lax.all_to_all(v, axis, 0, 0, axis_index_groups=groups, tiled=True)


def repeat(v, n):
    return jnp.broadcast_to(v[None], (n,) + v.shape)


def over_rows(v, pairs):
    return lax.ppermute(v, "rows", pairs)


def local(coefficients, support, primal, dual_inverse, block_sizes, damping, right_sides):
    col = lax.axis_index("cols")
    r = lax.axis_index("rows")
    x = col // 2
    p = col % 2
    info = jnp.concatenate([jnp.stack([r, col, p, x]).astype(jnp.int32), block_sizes])
    sup = support.astype(F32)

    def message(t, extra):
        tile = lax.dynamic_index_in_dim(coefficients, t, 0, keepdims=False)
        tile = lax.dynamic_slice_in_dim(tile, p * 128, 128, 2)
        return jnp.concatenate([jnp.transpose(tile, (1, 2, 0)).reshape(512, 128),
                                lax.dynamic_index_in_dim(sup, t, 0, keepdims=False).T, extra], axis=0)

    gathered = lax.all_gather(message(x, jnp.zeros((4, 128), F32)), "rows")

    own = jnp.transpose(coefficients, (2, 0, 1, 3)).reshape(4, 512, 256)
    own_sup = jnp.transpose(sup, (2, 0, 1)).reshape(4, 512)
    own_sup = jnp.broadcast_to(own_sup[:, :, None], (4, 512, 128))
    eye = jnp.eye(128, dtype=F32)

    pair = [lax.dynamic_slice_in_dim(v, 128 - p * 128, 128, 2) for v in (primal, dual_inverse)]
    places = jnp.arange(256)[None, :, None], 128 - p * 128 + jnp.arange(128)[None, None, :]
    inside = (places[0] < block_sizes[:, None, None]) & (places[1] < block_sizes[:, None, None])
    lent = swap(jnp.where(inside, pair[0] * pair[1], 0.0))
    head = jnp.where(r == 0, message(0, right_sides[0]), 0.0)
    head_next = over_rows(head, [(0, 2)])
    half = partial(info, own, own_sup, primal, dual_inverse, lent)
    head_next, half = lax.optimization_barrier((head_next, half))
    head = head + head_next
    head_next = over_rows(head, [(0, 1), (2, 3)])
    head = head + head_next
    head_next = over_rows(head, [(z, 8 + z) for z in range(4)])
    terms = exchange(half, "cols", CHIPS)
    head_next, terms = lax.optimization_barrier((head_next, terms))
    head = head + head_next
    head_next = over_rows(head, [(y + z, y + 4 + z) for y in (0, 8) for z in range(4)])
    total = jnp.sum(terms, axis=0)
    v_own = exchange(repeat(total[:4], 4), "cols", CHIPS)
    corner = total[4] + eye * jnp.where(p == 0, damping[0], 0.0)
    inverse = inverse_of(corner + swap(corner))
    head_next, v_own, inverse, gathered = lax.optimization_barrier((head_next, v_own, inverse, gathered))
    v_other = swap(v_own)
    head = head + head_next
    head_other = swap(head)
    second = over_rows(inverse, [(0, 8)])
    gathered, v_other, head_other, second = lax.optimization_barrier((gathered, v_other, head_other, second))
    swapped = swap(gathered)
    every = exchange(lead(info, v_own, v_other, own_sup, head, head_other, inverse, second), "rows")

    start = block_product(info, v_own, own_sup, gathered, lambda g, i: (i[2], 0, 0), head, head)
    updated, panel, solved = block_product(info, v_other, own_sup, swapped, lambda g, i: (i[2], 0, 0), head, head_other,
                                           list(start) + [every, damping, right_sides])
    return updated.reshape(4, 128, 1024), panel.reshape(4, 128, 128), solved


def solution(mesh):
    in_specs = (
        P(None, "rows", None, None),
        P(None, "rows", None),
        P("cols", None, None),
        P("cols", None, None),
        P("cols"),
        P(None, "rows"),
        P(None, "cols", "rows"),
    )
    out_specs = (P(None, "rows", "cols"), P(None, "rows", None), P(None, "cols", "rows"))
    return jax.shard_map(local, mesh=mesh, in_specs=in_specs, out_specs=out_specs, check_vma=False)
```

```python
import functools
import jax
import jax.numpy as jnp
from jax import lax
from jax.experimental import pallas as pl
from jax.experimental.pallas import tpu as pltpu
from jax.sharding import PartitionSpec as P

BF = jnp.bfloat16
F32 = jnp.float32
NT = (((1,), (1,)), ((), ()))
NN = (((1,), (0,)), ((), ()))
VMEM = 56 << 20


def split(v):
    h = v.astype(BF)
    return h, (v - h.astype(F32)).astype(BF)


def product(ah, al, bh, bl, dims):
    side = dims[0][1][0]
    left = jnp.concatenate([ah, al, ah], axis=1)
    right = jnp.concatenate([bh, bh, bl], axis=side)
    return lax.dot_general(left, right, dims, preferred_element_type=F32)


def choose(masks, values):
    out = jnp.zeros_like(values[0])
    for m, v in zip(masks, values):
        out = jnp.where(m, v, out)
    return out


def partial_body(info, c_ref, s_ref, x_ref, y_ref, z_ref, v_ref, wh, wl, total):
    t = pl.program_id(0)
    col, p = info[1], info[2]
    mine = pl.ds(pl.multiple_of(p * 128, 128), 128)

    @pl.when(t == 0)
    def _():
        row = lax.broadcasted_iota(jnp.int32, (256, 128), 0)
        lane = lax.broadcasted_iota(jnp.int32, (256, 128), 1)
        for u in range(3):
            size = info[4 + u]
            w = jnp.where((row < size) & (lane + p * 128 < size), x_ref[u, :, mine] * y_ref[u, :, mine], 0.0)
            wh[u], wl[u] = split(w)
            wh[3 + u], wl[3 + u] = split(z_ref[u])

    parts = [jnp.zeros((128, 128), F32)] * 4
    masks = []
    for u in range(6):
        block = ((col if u < 3 else col + 1 - 2 * p) * 3 + u % 3).astype(F32)
        m = [s_ref[k] == block for k in range(4)]
        masks.append(m)
        d = jnp.concatenate([choose(m, [c_ref[k, :, q * 128:(q + 1) * 128] for k in range(4)]) for q in range(2)], axis=1)
        dh, dl = split(d)
        v = product(dh, dl, wh[u], wl[u], NN)
        parts = [jnp.where(m[k], v, parts[k]) for k in range(4)]
    for k in range(4):
        v_ref[0, k] = parts[k]

    @pl.when(t == 0)
    def _():
        vs, es = [], []
        for m in masks:
            vs.append(choose(m, parts))
            es.append(choose(m, [c_ref[k, :, mine] for k in range(4)]))
        vh, vl = split(jnp.concatenate(vs, axis=1))
        eh, el = split(jnp.concatenate(es, axis=1))
        total[...] = product(vh, vl, eh, el, NT)

    v_ref[0, 4] = total[...]


def whole(v):
    return pl.BlockSpec(v.shape, lambda g, i: (0,) * v.ndim)


def partial(info, c, s, x, y, z):
    out = jax.ShapeDtypeStruct((4, 5, 128, 128), F32)
    grid = pltpu.PrefetchScalarGridSpec(
        num_scalar_prefetch=1, grid=(4,),
        in_specs=[pl.BlockSpec((4, 128, 256), lambda t, i: (0, t, 0)), pl.BlockSpec((4, 128, 128), lambda t, i: (0, t, 0)), whole(x), whole(y), whole(z)],
        out_specs=pl.BlockSpec((1, 5, 128, 128), lambda t, i: (t, 0, 0, 0)),
        scratch_shapes=[pltpu.VMEM((6, 256, 128), BF)] * 2 + [pltpu.VMEM((128, 128), F32)])
    return pl.pallas_call(partial_body, grid_spec=grid, out_shape=out,
                          compiler_params=pltpu.CompilerParams(vmem_limit_bytes=VMEM), name="partial",
                          cost_estimate=pl.CostEstimate(flops=2 * 3 * 512 * 768 * 256, bytes_accessed=8 << 20, transcendentals=0))(info, c, s, x, y, z)


def gather_blocks(base, sup, high, low, axis):
    highs, lows = [], []
    for u in range(6):
        block = (base + u).astype(F32).astype(BF)
        m = [s == block for s in sup]
        highs.append(choose(m, [high(k) for k in range(4)]))
        lows.append(choose(m, [low(k) for k in range(4)]))
    return jnp.concatenate(highs, axis=axis), jnp.concatenate(lows, axis=axis)


def column_labels(rows, n):
    return jnp.broadcast_to(jnp.concatenate(rows, axis=1), (128, n)).astype(BF)


def lead_body(info, v0_ref, v1_ref, s_ref, z_ref, f_ref, n_ref, o_ref, vh, vl, dh, dl, a_ref):
    g = pl.program_id(0)

    @pl.when(g == 0)
    def _():
        for j, v_ref in enumerate((v0_ref, v1_ref)):
            for k in range(4):
                vh[j, k], vl[j, k] = split(v_ref[info[3], k])
                dh[j, k], dl[j, k] = split(v_ref[k, 4])
        a_ref[...] = jnp.zeros_like(a_ref)

    sup = [s_ref[k].astype(BF) for k in range(4)]
    first = [column_labels([z_ref[128 + k:129 + k]], 128) for k in range(4)]
    for j in range(2):
        ah, al = gather_blocks(6 * g, sup, lambda k: vh[j, k], lambda k: vl[j, k], 1)
        bh, bl = gather_blocks(6 * g, first, lambda k: dh[j, k], lambda k: dl[j, k], 0)
        a_ref[...] += product(ah, al, bh, bl, NN)

    @pl.when(g == 3)
    def _():
        r, p = info[0], info[2]
        sent = jnp.where((r == 0) & (p == 1), f_ref[...], jnp.where((r == 8) & (p == 0), n_ref[...], a_ref[...]))
        for j in range(16):
            o_ref[j] = sent


def lead(info, v0, v1, s, z, f, n):
    args = [v0, v1, s, z, f, n]
    specs = [whole(v) for v in args]
    specs[2] = pl.BlockSpec((4, 128, 128), lambda g, i: (0, i[3], 0))
    grid = pltpu.PrefetchScalarGridSpec(
        num_scalar_prefetch=1, grid=(4,), in_specs=specs, out_specs=pl.BlockSpec((16, 128, 128), lambda g, i: (0, 0, 0)),
        scratch_shapes=[pltpu.VMEM((2, 4, 128, 128), BF)] * 4 + [pltpu.VMEM((128, 128), F32)])
    return pl.pallas_call(lead_body, grid_spec=grid, out_shape=jax.ShapeDtypeStruct((16, 128, 128), F32),
                          compiler_params=pltpu.CompilerParams(vmem_limit_bytes=VMEM), name="lead",
                          cost_estimate=pl.CostEstimate(flops=2 * 3 * 128 * 6144 * 128, bytes_accessed=6 << 20, transcendentals=0))(info, *args)


def block_body(last, info, v_ref, r_ref, c_ref, z_ref, *rest):
    if last:
        s_ref, b_ref, e_ref, h_ref, y_ref, o_ref, p_ref, x_ref, vh, vl, ch, cl, total = rest
    else:
        o_ref, total, vh, vl, ch, cl = rest
    g = pl.program_id(0)

    @pl.when(g == 0)
    def _():
        for k in range(4):
            for t in range(4):
                vh[k, t * 128:(t + 1) * 128], vl[k, t * 128:(t + 1) * 128] = split(v_ref[t, k])
            for t in range(8):
                ch[k, :, t * 128:(t + 1) * 128], cl[k, :, t * 128:(t + 1) * 128] = split(c_ref[t, k * 128:(k + 1) * 128])
            ch[k, :, 1024:], cl[k, :, 1024:] = split(v_ref[k, 4])
        o_ref[...] = s_ref[...] if last else jnp.zeros_like(o_ref)
        total[...] = b_ref[...] if last else jnp.zeros_like(total)

    rows = [r_ref[k].astype(BF) for k in range(4)]
    ah, al = gather_blocks(6 * g, rows, lambda k: vh[k], lambda k: vl[k], 1)
    for q in range(3):
        n = 512 if q < 2 else 128
        r = slice(q * 512, q * 512 + n)
        if q < 2:
            sup = [column_labels([c_ref[4 * q + t, 512 + k:513 + k] for t in range(4)], n) for k in range(4)]
        else:
            sup = [column_labels([z_ref[128 + k:129 + k]], n) for k in range(4)]
        bh, bl = gather_blocks(6 * g, sup, lambda k: ch[k, :, r], lambda k: cl[k, :, r], 0)
        value = product(ah, al, bh, bl, NN)
        if q < 2:
            o_ref[:, r] += value
        else:
            total[...] += value

    if last:
        @pl.when(g == 3)
        def _():
            row, col, p = info[0], info[1], info[2]
            same = lax.broadcasted_iota(jnp.int32, (128, 128), 0) == lax.broadcasted_iota(jnp.int32, (128, 128), 1)
            ih, il = split(e_ref[8 * (1 - p)])
            total[:128] += jnp.where(same & (row == 0), jnp.broadcast_to(h_ref[:1], (128, 128)), 0.0)
            th, tl = split(total[...])
            panel = product(th, tl, ih, il, NT)
            p_ref[...] = panel
            ph, plo = split(panel)
            zh, zl = split(z_ref[128:136])
            sides = product(zh, zl, ih, il, NT)
            xh, xl = split(sides)
            for t in range(4):
                tile = slice(t * 128, (t + 1) * 128)
                taken = product(xh, xl, ph[tile], plo[tile], NT)
                x_ref[t] = jnp.where(t * 16 + row > 0, y_ref[t] - taken[4:], sides[4:])
            for j in range(8):
                span = slice(j * 128, (j + 1) * 128)
                eh, el = split(e_ref[8 * p + j])
                qh, ql = split(product(eh, el, ih, il, NT))
                outer = product(ph, plo, qh, ql, NT)
                across = col * 8 + j
                for t in range(4):
                    tile = slice(t * 128, (t + 1) * 128)
                    down = t * 16 + row
                    diagonal = jnp.where(same & (down == across), jnp.broadcast_to(h_ref[t:t + 1], (128, 128)), 0.0)
                    o_ref[tile, span] += diagonal - jnp.where((down > 0) & (across > 0), outer[tile], 0.0)


def block_product(info, v, r, c, pick, z, tail=None):
    last = tail is not None
    args = [v, r, c, z] + (list(tail) if last else [])
    specs = [whole(u) for u in args]
    specs[2] = pl.BlockSpec((8, 520, 128), pick)
    shapes = [(512, 1024), (512, 128)] + ([(4, 4, 128)] if last else [])
    outs = [pl.BlockSpec((512, 1024), lambda g, i: (0, 0)), pl.BlockSpec((512, 128), lambda g, i: (0, 0)),
            pl.BlockSpec((4, 4, 128), lambda g, i: (0, 0, 0))]
    grid = pltpu.PrefetchScalarGridSpec(
        num_scalar_prefetch=1, grid=(4,), in_specs=specs, out_specs=outs[:len(shapes)],
        scratch_shapes=[pltpu.VMEM((4, 512, 128), BF)] * 2 + [pltpu.VMEM((4, 128, 1152), BF)] * 2
        + ([pltpu.VMEM((512, 128), F32)] if last else []))
    return pl.pallas_call(functools.partial(block_body, last), grid_spec=grid,
                          out_shape=[jax.ShapeDtypeStruct(u, F32) for u in shapes],
                          compiler_params=pltpu.CompilerParams(vmem_limit_bytes=VMEM), name="block",
                          cost_estimate=pl.CostEstimate(flops=2 * 3 * 512 * 3072 * 1152, bytes_accessed=10 << 20, transcendentals=0))(info, *args)


def inverse_body(c_ref, i_ref, o_ref):
    n = 128
    row = lax.broadcasted_iota(jnp.int32, (n, n), 0)
    col = lax.broadcasted_iota(jnp.int32, (n, n), 1)
    below = lax.broadcasted_iota(jnp.int32, (n, 1), 0)
    lane = lax.broadcasted_iota(jnp.int32, (1, n), 1)
    o_ref[...] = jnp.concatenate([c_ref[...], jnp.where(row == col, 1.0, 0.0).astype(F32)], axis=1)

    def at(v, k):
        return jnp.sum(jnp.where(lane == k, v, 0.0), axis=1, keepdims=True)

    def step(i, _):
        k = 2 * i
        line0 = o_ref[pl.ds(k, 1), :]
        line1 = o_ref[pl.ds(k + 1, 1), :]
        left = o_ref[:, :n]
        a, b, c = at(line0[:, :n], k), at(line0[:, :n], k + 1), at(line1[:, :n], k + 1)
        col0, col1 = at(left, k), at(left, k + 1)
        s0 = lax.rsqrt(a)
        b = b * s0
        s1 = lax.rsqrt(c - b * b)
        line0 = line0 * s0
        line1 = (line1 - b * line0) * s1
        f0 = jnp.where(below > k + 1, col0 * s0, 0.0)
        f1 = jnp.where(below > k + 1, (col1 - f0 * b) * s1, 0.0)
        o_ref[...] = o_ref[...] - f0 * line0 - f1 * line1
        o_ref[pl.ds(k, 1), :] = line0
        o_ref[pl.ds(k + 1, 1), :] = line1
        return 0

    lax.fori_loop(0, n // 2, step, 0)
    i_ref[...] = o_ref[:, n:]


def inverse_of(c):
    return pl.pallas_call(inverse_body, out_shape=jax.ShapeDtypeStruct((128, 128), F32), name="inverse",
                          scratch_shapes=[pltpu.VMEM((128, 256), F32)],
                          cost_estimate=pl.CostEstimate(flops=2 * 3 * 512 * 3072 * 768, bytes_accessed=1 << 20, transcendentals=0))(c)


SWAP = [(i, i ^ 1) for i in range(8)]
CHIPS = [[0, 2, 4, 6], [1, 3, 5, 7]]


def swap(v):
    return lax.ppermute(v, "cols", SWAP)


def exchange(v, axis, groups=None):
    return lax.all_to_all(v, axis, 0, 0, axis_index_groups=groups, tiled=True)


def repeat(v, n):
    return jnp.broadcast_to(v[None], (n,) + v.shape)


def over_rows(v, pairs):
    return lax.ppermute(v, "rows", pairs)


def local(coefficients, support, primal, dual_inverse, block_sizes, damping, right_sides):
    col = lax.axis_index("cols")
    r = lax.axis_index("rows")
    x = col // 2
    p = col % 2
    info = jnp.concatenate([jnp.stack([r, col, p, x]).astype(jnp.int32), block_sizes])
    sup = support.astype(F32)

    def message(t, extra):
        tile = lax.dynamic_index_in_dim(coefficients, t, 0, keepdims=False)
        tile = lax.dynamic_slice_in_dim(tile, p * 128, 128, 2)
        return jnp.concatenate([jnp.transpose(tile, (1, 2, 0)).reshape(512, 128),
                                lax.dynamic_index_in_dim(sup, t, 0, keepdims=False).T, extra], axis=0)

    gathered = lax.all_gather(message(x, jnp.zeros((4, 128), F32)), "rows")

    own = jnp.transpose(coefficients, (2, 0, 1, 3)).reshape(4, 512, 256)
    own_sup = jnp.transpose(sup, (2, 0, 1)).reshape(4, 512)
    own_sup = jnp.broadcast_to(own_sup[:, :, None], (4, 512, 128))
    eye = jnp.eye(128, dtype=F32)

    active = (jnp.arange(256, dtype=jnp.int32)[None, :] < block_sizes[:, None]).astype(F32)
    away = 128 - p * 128
    lent = lax.dynamic_slice_in_dim(primal, away, 128, 2) * lax.dynamic_slice_in_dim(dual_inverse, away, 128, 2)
    lent = swap(lent * active[:, :, None] * lax.dynamic_slice_in_dim(active, away, 128, 1)[:, None, :])

    head = lax.dynamic_slice_in_dim(lax.dynamic_index_in_dim(coefficients[0], x, 1, keepdims=False), p * 128, 128, 1)
    head = jnp.concatenate([head.T, sup[0].T, right_sides[0]], axis=0)
    head = jnp.where(r == 0, head, 0.0)
    head_next = over_rows(head, [(0, 2)])
    head_next, lent = lax.optimization_barrier((head_next, lent))
    head = head + head_next
    head_next = over_rows(head, [(0, 1), (2, 3)])
    half = partial(info, own, own_sup, primal, dual_inverse, lent)
    head_next, half = lax.optimization_barrier((head_next, half))
    head = head + head_next
    head_next = over_rows(head, [(z, 8 + z) for z in range(4)])
    head = head + head_next
    head_next = over_rows(head, [(y + z, y + 4 + z) for y in (0, 8) for z in range(4)])
    terms = exchange(half, "cols", CHIPS)
    head_next, terms = lax.optimization_barrier((head_next, terms))
    head = head + head_next
    total = jnp.sum(terms, axis=0)
    v_own = exchange(repeat(jnp.concatenate([total[:4], head[None, :128]], axis=0), 4), "cols", CHIPS)
    corner = total[4] + eye * jnp.where(p == 0, damping[0], 0.0)
    inverse = inverse_of(corner + swap(corner))
    second = over_rows(inverse, [(0, 8)])
    v_own, inverse, second, gathered = lax.optimization_barrier((v_own, inverse, second, gathered))
    v_other = swap(v_own)
    gathered, v_other = lax.optimization_barrier((gathered, v_other))
    swapped = swap(gathered)
    every = exchange(lead(info, v_own, v_other, own_sup, head, inverse, second), "rows")

    start = block_product(info, v_own, own_sup, gathered, lambda g, i: (i[2], 0, 0), head)
    updated, panel, solved = block_product(info, v_other, own_sup, swapped, lambda g, i: (i[2], 0, 0), head,
                                           list(start) + [every, damping, right_sides])
    return updated.reshape(4, 128, 1024), panel.reshape(4, 128, 128), solved


def solution(mesh):
    in_specs = (
        P(None, "rows", None, None),
        P(None, "rows", None),
        P("cols", None, None),
        P("cols", None, None),
        P("cols"),
        P(None, "rows"),
        P(None, "cols", "rows"),
    )
    out_specs = (P(None, "rows", "cols"), P(None, "rows", None), P(None, "cols", "rows"))
    return jax.shard_map(local, mesh=mesh, in_specs=in_specs, out_specs=out_specs, check_vma=False)
```

```python
import functools
import jax
import jax.numpy as jnp
from jax import lax
from jax.experimental import pallas as pl
from jax.experimental.pallas import tpu as pltpu
from jax.sharding import PartitionSpec as P

BF = jnp.bfloat16
F32 = jnp.float32
NT = (((1,), (1,)), ((), ()))
NN = (((1,), (0,)), ((), ()))
VMEM = 56 << 20


def split(v):
    h = v.astype(BF)
    return h, (v - h.astype(F32)).astype(BF)


def product(ah, al, bh, bl, dims):
    side = dims[0][1][0]
    left = jnp.concatenate([ah, al, ah], axis=1)
    right = jnp.concatenate([bh, bh, bl], axis=side)
    return lax.dot_general(left, right, dims, preferred_element_type=F32)


def choose(masks, values):
    out = jnp.zeros_like(values[0])
    for m, v in zip(masks, values):
        out = jnp.where(m, v, out)
    return out


def partial_body(info, c_ref, s_ref, x_ref, y_ref, z_ref, v_ref, wh, wl, total):
    t = pl.program_id(0)
    col, p = info[1], info[2]
    mine = pl.ds(pl.multiple_of(p * 128, 128), 128)

    @pl.when(t == 0)
    def _():
        row = lax.broadcasted_iota(jnp.int32, (256, 128), 0)
        lane = lax.broadcasted_iota(jnp.int32, (256, 128), 1)
        for u in range(3):
            size = info[4 + u]
            w = jnp.where((row < size) & (lane + p * 128 < size), x_ref[u, :, mine] * y_ref[u, :, mine], 0.0)
            wh[u], wl[u] = split(w)
            wh[3 + u], wl[3 + u] = split(z_ref[u])

    parts = [jnp.zeros((128, 128), F32)] * 4
    masks = []
    for u in range(6):
        block = ((col if u < 3 else col + 1 - 2 * p) * 3 + u % 3).astype(F32)
        m = [s_ref[k] == block for k in range(4)]
        masks.append(m)
        d = jnp.concatenate([choose(m, [c_ref[k, :, q * 128:(q + 1) * 128] for k in range(4)]) for q in range(2)], axis=1)
        dh, dl = split(d)
        v = product(dh, dl, wh[u], wl[u], NN)
        parts = [jnp.where(m[k], v, parts[k]) for k in range(4)]
    for k in range(4):
        v_ref[0, k] = parts[k]

    @pl.when(t == 0)
    def _():
        vs, es = [], []
        for m in masks:
            vs.append(choose(m, parts))
            es.append(choose(m, [c_ref[k, :, mine] for k in range(4)]))
        vh, vl = split(jnp.concatenate(vs, axis=1))
        eh, el = split(jnp.concatenate(es, axis=1))
        total[...] = product(vh, vl, eh, el, NT)

    v_ref[0, 4] = total[...]


def whole(v):
    return pl.BlockSpec(v.shape, lambda g, i: (0,) * v.ndim)


def partial(info, c, s, x, y, z):
    out = jax.ShapeDtypeStruct((4, 5, 128, 128), F32)
    grid = pltpu.PrefetchScalarGridSpec(
        num_scalar_prefetch=1, grid=(4,),
        in_specs=[pl.BlockSpec((4, 128, 256), lambda t, i: (0, t, 0)), pl.BlockSpec((4, 128, 128), lambda t, i: (0, t, 0)), whole(x), whole(y), whole(z)],
        out_specs=pl.BlockSpec((1, 5, 128, 128), lambda t, i: (t, 0, 0, 0)),
        scratch_shapes=[pltpu.VMEM((6, 256, 128), BF)] * 2 + [pltpu.VMEM((128, 128), F32)])
    return pl.pallas_call(partial_body, grid_spec=grid, out_shape=out,
                          compiler_params=pltpu.CompilerParams(vmem_limit_bytes=VMEM), name="partial",
                          cost_estimate=pl.CostEstimate(flops=2 * 3 * 512 * 768 * 256, bytes_accessed=8 << 20, transcendentals=0))(info, c, s, x, y, z)


def gather_blocks(base, sup, high, low, axis):
    highs, lows = [], []
    for u in range(6):
        block = (base + u).astype(F32).astype(BF)
        m = [s == block for s in sup]
        highs.append(choose(m, [high(k) for k in range(4)]))
        lows.append(choose(m, [low(k) for k in range(4)]))
    return jnp.concatenate(highs, axis=axis), jnp.concatenate(lows, axis=axis)


def column_labels(rows, n):
    return jnp.broadcast_to(jnp.concatenate(rows, axis=1), (128, n)).astype(BF)


def lead_body(info, v0_ref, v1_ref, s_ref, z_ref, f_ref, n_ref, o_ref, vh, vl, dh, dl, a_ref):
    g = pl.program_id(0)

    @pl.when(g == 0)
    def _():
        for j, v_ref in enumerate((v0_ref, v1_ref)):
            for k in range(4):
                vh[j, k], vl[j, k] = split(v_ref[info[3], k])
                dh[j, k], dl[j, k] = split(v_ref[k, 4])
        a_ref[...] = jnp.zeros_like(a_ref)

    sup = [s_ref[k].astype(BF) for k in range(4)]
    first = [column_labels([z_ref[128 + k:129 + k]], 128) for k in range(4)]
    for j in range(2):
        ah, al = gather_blocks(6 * g, sup, lambda k: vh[j, k], lambda k: vl[j, k], 1)
        bh, bl = gather_blocks(6 * g, first, lambda k: dh[j, k], lambda k: dl[j, k], 0)
        a_ref[...] += product(ah, al, bh, bl, NN)

    @pl.when(g == 3)
    def _():
        r, p = info[0], info[2]
        sent = jnp.where((r == 0) & (p == 1), f_ref[...], jnp.where((r == 8) & (p == 0), n_ref[...], a_ref[...]))
        for j in range(16):
            o_ref[j] = sent


def lead(info, v0, v1, s, z, f, n):
    args = [v0, v1, s, z, f, n]
    specs = [whole(v) for v in args]
    specs[2] = pl.BlockSpec((4, 128, 128), lambda g, i: (0, i[3], 0))
    grid = pltpu.PrefetchScalarGridSpec(
        num_scalar_prefetch=1, grid=(4,), in_specs=specs, out_specs=pl.BlockSpec((16, 128, 128), lambda g, i: (0, 0, 0)),
        scratch_shapes=[pltpu.VMEM((2, 4, 128, 128), BF)] * 4 + [pltpu.VMEM((128, 128), F32)])
    return pl.pallas_call(lead_body, grid_spec=grid, out_shape=jax.ShapeDtypeStruct((16, 128, 128), F32),
                          compiler_params=pltpu.CompilerParams(vmem_limit_bytes=VMEM), name="lead",
                          cost_estimate=pl.CostEstimate(flops=2 * 3 * 128 * 6144 * 128, bytes_accessed=6 << 20, transcendentals=0))(info, *args)


def block_body(last, info, v_ref, r_ref, c_ref, z_ref, *rest):
    if last:
        s_ref, b_ref, e_ref, h_ref, y_ref, o_ref, p_ref, x_ref, vh, vl, ch, cl, total = rest
    else:
        o_ref, total, vh, vl, ch, cl = rest
    g = pl.program_id(0)

    @pl.when(g == 0)
    def _():
        for k in range(4):
            for t in range(4):
                vh[k, t * 128:(t + 1) * 128], vl[k, t * 128:(t + 1) * 128] = split(v_ref[t, k])
            for t in range(8):
                ch[k, :, t * 128:(t + 1) * 128], cl[k, :, t * 128:(t + 1) * 128] = split(c_ref[t, k * 128:(k + 1) * 128])
            ch[k, :, 1024:], cl[k, :, 1024:] = split(v_ref[k, 4])
        o_ref[...] = s_ref[...] if last else jnp.zeros_like(o_ref)
        total[...] = b_ref[...] if last else jnp.zeros_like(total)

    rows = [r_ref[k].astype(BF) for k in range(4)]
    ah, al = gather_blocks(6 * g, rows, lambda k: vh[k], lambda k: vl[k], 1)
    for q in range(3):
        n = 512 if q < 2 else 128
        r = slice(q * 512, q * 512 + n)
        if q < 2:
            sup = [column_labels([c_ref[4 * q + t, 512 + k:513 + k] for t in range(4)], n) for k in range(4)]
        else:
            sup = [column_labels([z_ref[128 + k:129 + k]], n) for k in range(4)]
        bh, bl = gather_blocks(6 * g, sup, lambda k: ch[k, :, r], lambda k: cl[k, :, r], 0)
        value = product(ah, al, bh, bl, NN)
        if q < 2:
            o_ref[:, r] += value
        else:
            total[...] += value

    if last:
        @pl.when(g == 3)
        def _():
            row, col, p = info[0], info[1], info[2]
            same = lax.broadcasted_iota(jnp.int32, (128, 128), 0) == lax.broadcasted_iota(jnp.int32, (128, 128), 1)
            ih, il = split(e_ref[8 * (1 - p)])
            total[:128] += jnp.where(same & (row == 0), jnp.broadcast_to(h_ref[:1], (128, 128)), 0.0)
            th, tl = split(total[...])
            panel = product(th, tl, ih, il, NT)
            p_ref[...] = panel
            ph, plo = split(panel)
            zh, zl = split(z_ref[128:136])
            sides = product(zh, zl, ih, il, NT)
            xh, xl = split(sides)
            for t in range(4):
                tile = slice(t * 128, (t + 1) * 128)
                taken = product(xh, xl, ph[tile], plo[tile], NT)
                x_ref[t] = jnp.where(t * 16 + row > 0, y_ref[t] - taken[4:], sides[4:])
            for j in range(8):
                span = slice(j * 128, (j + 1) * 128)
                eh, el = split(e_ref[8 * p + j])
                qh, ql = split(product(eh, el, ih, il, NT))
                outer = product(ph, plo, qh, ql, NT)
                across = col * 8 + j
                for t in range(4):
                    tile = slice(t * 128, (t + 1) * 128)
                    down = t * 16 + row
                    diagonal = jnp.where(same & (down == across), jnp.broadcast_to(h_ref[t:t + 1], (128, 128)), 0.0)
                    o_ref[tile, span] += diagonal - jnp.where((down > 0) & (across > 0), outer[tile], 0.0)


def block_product(info, v, r, c, pick, z, tail=None):
    last = tail is not None
    args = [v, r, c, z] + (list(tail) if last else [])
    specs = [whole(u) for u in args]
    specs[2] = pl.BlockSpec((8, 520, 128), pick)
    shapes = [(512, 1024), (512, 128)] + ([(4, 4, 128)] if last else [])
    outs = [pl.BlockSpec((512, 1024), lambda g, i: (0, 0)), pl.BlockSpec((512, 128), lambda g, i: (0, 0)),
            pl.BlockSpec((4, 4, 128), lambda g, i: (0, 0, 0))]
    grid = pltpu.PrefetchScalarGridSpec(
        num_scalar_prefetch=1, grid=(4,), in_specs=specs, out_specs=outs[:len(shapes)],
        scratch_shapes=[pltpu.VMEM((4, 512, 128), BF)] * 2 + [pltpu.VMEM((4, 128, 1152), BF)] * 2
        + ([pltpu.VMEM((512, 128), F32)] if last else []))
    return pl.pallas_call(functools.partial(block_body, last), grid_spec=grid,
                          out_shape=[jax.ShapeDtypeStruct(u, F32) for u in shapes],
                          compiler_params=pltpu.CompilerParams(vmem_limit_bytes=VMEM), name="block",
                          cost_estimate=pl.CostEstimate(flops=2 * 3 * 512 * 3072 * 1152, bytes_accessed=10 << 20, transcendentals=0))(info, *args)


def inverse_body(c_ref, i_ref, o_ref):
    n = 128
    row = lax.broadcasted_iota(jnp.int32, (n, n), 0)
    col = lax.broadcasted_iota(jnp.int32, (n, n), 1)
    below = lax.broadcasted_iota(jnp.int32, (n, 1), 0)
    lane = lax.broadcasted_iota(jnp.int32, (1, n), 1)
    o_ref[...] = jnp.concatenate([c_ref[...], jnp.where(row == col, 1.0, 0.0).astype(F32)], axis=1)

    def at(v, k):
        return jnp.sum(jnp.where(lane == k, v, 0.0), axis=1, keepdims=True)

    def step(i, _):
        k = 2 * i
        line0 = o_ref[pl.ds(k, 1), :]
        line1 = o_ref[pl.ds(k + 1, 1), :]
        left = o_ref[:, :n]
        a, b, c = at(line0[:, :n], k), at(line0[:, :n], k + 1), at(line1[:, :n], k + 1)
        col0, col1 = at(left, k), at(left, k + 1)
        s0 = lax.rsqrt(a)
        b = b * s0
        s1 = lax.rsqrt(c - b * b)
        line0 = line0 * s0
        line1 = (line1 - b * line0) * s1
        f0 = jnp.where(below > k + 1, col0 * s0, 0.0)
        f1 = jnp.where(below > k + 1, (col1 - f0 * b) * s1, 0.0)
        o_ref[...] = o_ref[...] - f0 * line0 - f1 * line1
        o_ref[pl.ds(k, 1), :] = line0
        o_ref[pl.ds(k + 1, 1), :] = line1
        return 0

    lax.fori_loop(0, n // 2, step, 0)
    i_ref[...] = o_ref[:, n:]


def inverse_of(c):
    return pl.pallas_call(inverse_body, out_shape=jax.ShapeDtypeStruct((128, 128), F32), name="inverse",
                          scratch_shapes=[pltpu.VMEM((128, 256), F32)],
                          cost_estimate=pl.CostEstimate(flops=2 * 3 * 512 * 3072 * 768, bytes_accessed=1 << 20, transcendentals=0))(c)


SWAP = [(i, i ^ 1) for i in range(8)]
CHIPS = [[0, 2, 4, 6], [1, 3, 5, 7]]


def swap(v):
    return lax.ppermute(v, "cols", SWAP)


def exchange(v, axis, groups=None):
    return lax.all_to_all(v, axis, 0, 0, axis_index_groups=groups, tiled=True)


def repeat(v, n):
    return jnp.broadcast_to(v[None], (n,) + v.shape)


def over_rows(v, pairs):
    return lax.ppermute(v, "rows", pairs)


def local(coefficients, support, primal, dual_inverse, block_sizes, damping, right_sides):
    col = lax.axis_index("cols")
    r = lax.axis_index("rows")
    x = col // 2
    p = col % 2
    info = jnp.concatenate([jnp.stack([r, col, p, x]).astype(jnp.int32), block_sizes])
    sup = support.astype(F32)

    own = jnp.transpose(coefficients, (2, 0, 1, 3)).reshape(4, 512, 256)
    own_sup = jnp.transpose(sup, (2, 0, 1)).reshape(4, 512)
    tile = lax.dynamic_slice(own, (0, x * 128, p * 128), (4, 128, 128))
    message = jnp.concatenate([jnp.swapaxes(tile, 1, 2).reshape(512, 128), lax.dynamic_slice_in_dim(own_sup, x * 128, 128, 1),
                               jnp.zeros((4, 128), F32)], axis=0)
    gathered = lax.all_gather(message, "rows")
    head = lax.dynamic_slice(own, (x, 0, p * 128), (1, 128, 128))[0]
    head = jnp.concatenate([head.T, own_sup[:, :128], right_sides[0]], axis=0)
    head = jnp.where(r == 0, head, 0.0)
    own_sup = jnp.broadcast_to(own_sup[:, :, None], (4, 512, 128))
    eye = jnp.eye(128, dtype=F32)

    active = (jnp.arange(256, dtype=jnp.int32)[None, :] < block_sizes[:, None]).astype(F32)
    away = 128 - p * 128
    lent = lax.dynamic_slice_in_dim(primal, away, 128, 2) * lax.dynamic_slice_in_dim(dual_inverse, away, 128, 2)
    lent = swap(lent * active[:, :, None] * lax.dynamic_slice_in_dim(active, away, 128, 1)[:, None, :])

    half = partial(info, own, own_sup, primal, dual_inverse, lent)
    head, half = lax.optimization_barrier((head, half))
    for pairs in ([(0, 2)], [(0, 1), (2, 3)], [(z, 8 + z) for z in range(4)]):
        head = head + over_rows(head, pairs)
    head_next = over_rows(head, [(y + z, y + 4 + z) for y in (0, 8) for z in range(4)])
    terms = exchange(half, "cols", CHIPS)
    head_next, terms = lax.optimization_barrier((head_next, terms))
    head = head + head_next
    total = jnp.sum(terms, axis=0)
    v_own = exchange(repeat(jnp.concatenate([total[:4], head[None, :128]], axis=0), 4), "cols", CHIPS)
    corner = total[4] + eye * jnp.where(p == 0, damping[0], 0.0)
    inverse = inverse_of(corner + swap(corner))
    second = over_rows(inverse, [(0, 8)])
    v_own, inverse, second, gathered = lax.optimization_barrier((v_own, inverse, second, gathered))
    v_other = swap(v_own)
    gathered, v_other = lax.optimization_barrier((gathered, v_other))
    swapped = swap(gathered)
    every = exchange(lead(info, v_own, v_other, own_sup, head, inverse, second), "rows")

    start = block_product(info, v_own, own_sup, gathered, lambda g, i: (i[2], 0, 0), head)
    updated, panel, solved = block_product(info, v_other, own_sup, swapped, lambda g, i: (i[2], 0, 0), head,
                                           list(start) + [every, damping, right_sides])
    return updated.reshape(4, 128, 1024), panel.reshape(4, 128, 128), solved


def solution(mesh):
    in_specs = (
        P(None, "rows", None, None),
        P(None, "rows", None),
        P("cols", None, None),
        P("cols", None, None),
        P("cols"),
        P(None, "rows"),
        P(None, "cols", "rows"),
    )
    out_specs = (P(None, "rows", "cols"), P(None, "rows", None), P(None, "cols", "rows"))
    return jax.shard_map(local, mesh=mesh, in_specs=in_specs, out_specs=out_specs, check_vma=False)
```

```python
import functools
import jax
import jax.numpy as jnp
from jax import lax
from jax.experimental import pallas as pl
from jax.experimental.pallas import tpu as pltpu
from jax.sharding import PartitionSpec as P

BF = jnp.bfloat16
F32 = jnp.float32
NT = (((1,), (1,)), ((), ()))
NN = (((1,), (0,)), ((), ()))
VMEM = 56 << 20


def split(v):
    h = v.astype(BF)
    return h, (v - h.astype(F32)).astype(BF)


def product(ah, al, bh, bl, dims):
    side = dims[0][1][0]
    left = jnp.concatenate([ah, al, ah], axis=1)
    right = jnp.concatenate([bh, bh, bl], axis=side)
    return lax.dot_general(left, right, dims, preferred_element_type=F32)


def choose(masks, values):
    out = jnp.zeros_like(values[0])
    for m, v in zip(masks, values):
        out = jnp.where(m, v, out)
    return out


def partial_body(info, c_ref, s_ref, x_ref, y_ref, z_ref, v_ref, wh, wl, total):
    t = pl.program_id(0)
    col, p = info[1], info[2]
    mine = pl.ds(pl.multiple_of(p * 128, 128), 128)

    @pl.when(t == 0)
    def _():
        row = lax.broadcasted_iota(jnp.int32, (256, 128), 0)
        lane = lax.broadcasted_iota(jnp.int32, (256, 128), 1)
        for u in range(3):
            size = info[4 + u]
            w = jnp.where((row < size) & (lane + p * 128 < size), x_ref[u, :, mine] * y_ref[u, :, mine], 0.0)
            wh[u], wl[u] = split(w)
            wh[3 + u], wl[3 + u] = split(z_ref[u])

    parts = [jnp.zeros((256, 128), F32)] * 4
    masks = []
    for u in range(6):
        block = ((col if u < 3 else col + 1 - 2 * p) * 3 + u % 3).astype(F32)
        m = [s_ref[k] == block for k in range(4)]
        masks.append(m)
        d = jnp.concatenate([choose(m, [c_ref[k, :, q * 128:(q + 1) * 128] for k in range(4)]) for q in range(2)], axis=1)
        dh, dl = split(d)
        v = product(dh, dl, wh[u], wl[u], NN)
        parts = [jnp.where(m[k], v, parts[k]) for k in range(4)]
    for k in range(4):
        for h in range(2):
            v_ref[h, k] = parts[k][h * 128:(h + 1) * 128]

    @pl.when(t == 0)
    def _():
        vs, es = [], []
        for m in masks:
            top = [z[:128] for z in m]
            vs.append(choose(top, [z[:128] for z in parts]))
            es.append(choose(top, [c_ref[k, :128, mine] for k in range(4)]))
        vh, vl = split(jnp.concatenate(vs, axis=1))
        eh, el = split(jnp.concatenate(es, axis=1))
        total[...] = product(vh, vl, eh, el, NT)

    for h in range(2):
        v_ref[h, 4] = total[...]


def whole(v):
    return pl.BlockSpec(v.shape, lambda g, i: (0,) * v.ndim)


def partial(info, c, s, x, y, z):
    out = jax.ShapeDtypeStruct((4, 5, 128, 128), F32)
    grid = pltpu.PrefetchScalarGridSpec(
        num_scalar_prefetch=1, grid=(2,),
        in_specs=[pl.BlockSpec((4, 256, 256), lambda t, i: (0, t, 0)), pl.BlockSpec((4, 256, 128), lambda t, i: (0, t, 0)), whole(x), whole(y), whole(z)],
        out_specs=pl.BlockSpec((2, 5, 128, 128), lambda t, i: (t, 0, 0, 0)),
        scratch_shapes=[pltpu.VMEM((6, 256, 128), BF)] * 2 + [pltpu.VMEM((128, 128), F32)])
    return pl.pallas_call(partial_body, grid_spec=grid, out_shape=out,
                          compiler_params=pltpu.CompilerParams(vmem_limit_bytes=VMEM), name="partial",
                          cost_estimate=pl.CostEstimate(flops=2 * 3 * 512 * 768 * 256, bytes_accessed=8 << 20, transcendentals=0))(info, c, s, x, y, z)


def gather_blocks(base, sup, high, low, axis, count=6):
    highs, lows = [], []
    for u in range(count):
        block = (base + u).astype(F32).astype(BF)
        m = [s == block for s in sup]
        highs.append(choose(m, [high(k) for k in range(4)]))
        lows.append(choose(m, [low(k) for k in range(4)]))
    return jnp.concatenate(highs, axis=axis), jnp.concatenate(lows, axis=axis)


def column_labels(rows, n):
    return jnp.broadcast_to(jnp.concatenate(rows, axis=1), (128, n)).astype(BF)


def lead_body(last, info, v_ref, s_ref, z_ref, *rest):
    if last:
        b_ref, f_ref, n_ref, o_ref, a_ref = rest
    else:
        (a_ref,) = rest
    g = pl.program_id(0)

    @pl.when(g == 0)
    def _():
        a_ref[...] = b_ref[...] if last else jnp.zeros_like(a_ref)

    rows = [split(v_ref[info[3], k]) for k in range(4)]
    tiles = [split(v_ref[k, 4]) for k in range(4)]
    sup = [s_ref[k].astype(BF) for k in range(4)]
    first = [column_labels([z_ref[128 + k:129 + k]], 128) for k in range(4)]
    ah, al = gather_blocks(12 * g, sup, lambda k: rows[k][0], lambda k: rows[k][1], 1, 12)
    bh, bl = gather_blocks(12 * g, first, lambda k: tiles[k][0], lambda k: tiles[k][1], 0, 12)
    a_ref[...] += product(ah, al, bh, bl, NN)

    if last:
        @pl.when(g == 1)
        def _():
            r, p = info[0], info[2]
            sent = jnp.where((r == 0) & (p == 1), f_ref[...], jnp.where((r == 8) & (p == 0), n_ref[...], a_ref[...]))
            for j in range(16):
                o_ref[j] = sent


def lead(info, v, s, z, more=None):
    last = more is not None
    args = [v, s, z] + (list(more) if last else [])
    specs = [whole(u) for u in args]
    specs[1] = pl.BlockSpec((4, 128, 128), lambda g, i: (0, i[3], 0))
    shape = (16, 128, 128) if last else (128, 128)
    grid = pltpu.PrefetchScalarGridSpec(
        num_scalar_prefetch=1, grid=(2,), in_specs=specs, out_specs=pl.BlockSpec(shape, lambda g, i: (0,) * len(shape)),
        scratch_shapes=[pltpu.VMEM((128, 128), F32)] if last else [])
    return pl.pallas_call(functools.partial(lead_body, last), grid_spec=grid, out_shape=jax.ShapeDtypeStruct(shape, F32),
                          compiler_params=pltpu.CompilerParams(vmem_limit_bytes=VMEM), name="lead",
                          cost_estimate=pl.CostEstimate(flops=2 * 3 * 128 * 6144 * 128, bytes_accessed=3 << 20, transcendentals=0))(info, *args)


def block_body(last, info, v_ref, r_ref, c_ref, z_ref, *rest):
    if last:
        s_ref, b_ref, e_ref, h_ref, y_ref, o_ref, p_ref, x_ref, vh, vl, ch, cl, total = rest
    else:
        o_ref, total, vh, vl, ch, cl = rest
    g = pl.program_id(0)

    @pl.when(g == 0)
    def _():
        for k in range(4):
            for t in range(4):
                vh[k, t * 128:(t + 1) * 128], vl[k, t * 128:(t + 1) * 128] = split(v_ref[t, k])
            for t in range(8):
                ch[k, :, t * 128:(t + 1) * 128], cl[k, :, t * 128:(t + 1) * 128] = split(c_ref[t, k * 128:(k + 1) * 128])
            ch[k, :, 1024:], cl[k, :, 1024:] = split(v_ref[k, 4])
        o_ref[...] = s_ref[...] if last else jnp.zeros_like(o_ref)
        total[...] = b_ref[...] if last else jnp.zeros_like(total)

    rows = [r_ref[k].astype(BF) for k in range(4)]
    ah, al = gather_blocks(6 * g, rows, lambda k: vh[k], lambda k: vl[k], 1)
    for q in range(3):
        n = 512 if q < 2 else 128
        r = slice(q * 512, q * 512 + n)
        if q < 2:
            sup = [column_labels([c_ref[4 * q + t, 512 + k:513 + k] for t in range(4)], n) for k in range(4)]
        else:
            sup = [column_labels([z_ref[128 + k:129 + k]], n) for k in range(4)]
        bh, bl = gather_blocks(6 * g, sup, lambda k: ch[k, :, r], lambda k: cl[k, :, r], 0)
        value = product(ah, al, bh, bl, NN)
        if q < 2:
            o_ref[:, r] += value
        else:
            total[...] += value

    if last:
        @pl.when(g == 3)
        def _():
            row, col, p = info[0], info[1], info[2]
            same = lax.broadcasted_iota(jnp.int32, (128, 128), 0) == lax.broadcasted_iota(jnp.int32, (128, 128), 1)
            ih, il = split(e_ref[8 * (1 - p)])
            total[:128] += jnp.where(same & (row == 0), jnp.broadcast_to(h_ref[:1], (128, 128)), 0.0)
            th, tl = split(total[...])
            panel = product(th, tl, ih, il, NT)
            p_ref[...] = panel
            ph, plo = split(panel)
            zh, zl = split(z_ref[128:136])
            sides = product(zh, zl, ih, il, NT)
            xh, xl = split(sides)
            for t in range(4):
                tile = slice(t * 128, (t + 1) * 128)
                taken = product(xh, xl, ph[tile], plo[tile], NT)
                x_ref[t] = jnp.where(t * 16 + row > 0, y_ref[t] - taken[4:], sides[4:])
            eh, el = split(e_ref[pl.ds(8 * p, 8)].reshape(1024, 128))
            qh, ql = split(product(eh, el, ih, il, NT))
            for t in range(4):
                tile = slice(t * 128, (t + 1) * 128)
                down = t * 16 + row
                outer = product(ph[tile], plo[tile], qh, ql, NT)
                for j in range(8):
                    span = slice(j * 128, (j + 1) * 128)
                    across = col * 8 + j
                    diagonal = jnp.where(same & (down == across), jnp.broadcast_to(h_ref[t:t + 1], (128, 128)), 0.0)
                    o_ref[tile, span] += diagonal - jnp.where((down > 0) & (across > 0), outer[:, span], 0.0)


def block_product(info, v, r, c, pick, z, tail=None):
    last = tail is not None
    args = [v, r, c, z] + (list(tail) if last else [])
    specs = [whole(u) for u in args]
    specs[2] = pl.BlockSpec((8, 520, 128), pick)
    shapes = [(512, 1024), (512, 128)] + ([(4, 4, 128)] if last else [])
    outs = [pl.BlockSpec((512, 1024), lambda g, i: (0, 0)), pl.BlockSpec((512, 128), lambda g, i: (0, 0)),
            pl.BlockSpec((4, 4, 128), lambda g, i: (0, 0, 0))]
    grid = pltpu.PrefetchScalarGridSpec(
        num_scalar_prefetch=1, grid=(4,), in_specs=specs, out_specs=outs[:len(shapes)],
        scratch_shapes=[pltpu.VMEM((4, 512, 128), BF)] * 2 + [pltpu.VMEM((4, 128, 1152), BF)] * 2
        + ([pltpu.VMEM((512, 128), F32)] if last else []))
    return pl.pallas_call(functools.partial(block_body, last), grid_spec=grid,
                          out_shape=[jax.ShapeDtypeStruct(u, F32) for u in shapes],
                          compiler_params=pltpu.CompilerParams(vmem_limit_bytes=VMEM), name="block",
                          cost_estimate=pl.CostEstimate(flops=2 * 3 * 512 * 3072 * 1152, bytes_accessed=10 << 20, transcendentals=0))(info, *args)


def inverse_body(c_ref, i_ref, o_ref):
    n = 128
    row = lax.broadcasted_iota(jnp.int32, (n, n), 0)
    col = lax.broadcasted_iota(jnp.int32, (n, n), 1)
    below = lax.broadcasted_iota(jnp.int32, (n, 1), 0)
    lane = lax.broadcasted_iota(jnp.int32, (1, n), 1)
    o_ref[...] = jnp.concatenate([c_ref[...], jnp.where(row == col, 1.0, 0.0).astype(F32)], axis=1)

    def at(v, k):
        return jnp.sum(jnp.where(lane == k, v, 0.0), axis=1, keepdims=True)

    def step(i, _):
        k = 2 * i
        line0 = o_ref[pl.ds(k, 1), :]
        line1 = o_ref[pl.ds(k + 1, 1), :]
        left = o_ref[:, :n]
        a, b, c = at(line0[:, :n], k), at(line0[:, :n], k + 1), at(line1[:, :n], k + 1)
        col0, col1 = at(left, k), at(left, k + 1)
        s0 = lax.rsqrt(a)
        b = b * s0
        s1 = lax.rsqrt(c - b * b)
        line0 = line0 * s0
        line1 = (line1 - b * line0) * s1
        f0 = jnp.where(below > k + 1, col0 * s0, 0.0)
        f1 = jnp.where(below > k + 1, (col1 - f0 * b) * s1, 0.0)
        o_ref[...] = o_ref[...] - f0 * line0 - f1 * line1
        o_ref[pl.ds(k, 1), :] = line0
        o_ref[pl.ds(k + 1, 1), :] = line1
        return 0

    lax.fori_loop(0, n // 2, step, 0)
    i_ref[...] = o_ref[:, n:]


def inverse_of(c):
    return pl.pallas_call(inverse_body, out_shape=jax.ShapeDtypeStruct((128, 128), F32), name="inverse",
                          scratch_shapes=[pltpu.VMEM((128, 256), F32)],
                          cost_estimate=pl.CostEstimate(flops=2 * 3 * 512 * 3072 * 768, bytes_accessed=1 << 20, transcendentals=0))(c)


SWAP = [(i, i ^ 1) for i in range(8)]
CHIPS = [[0, 2, 4, 6], [1, 3, 5, 7]]


def swap(v):
    return lax.ppermute(v, "cols", SWAP)


def exchange(v, axis, groups=None):
    return lax.all_to_all(v, axis, 0, 0, axis_index_groups=groups, tiled=True)


def repeat(v, n):
    return jnp.broadcast_to(v[None], (n,) + v.shape)


def over_rows(v, pairs):
    return lax.ppermute(v, "rows", pairs)


def local(coefficients, support, primal, dual_inverse, block_sizes, damping, right_sides):
    col = lax.axis_index("cols")
    r = lax.axis_index("rows")
    x = col // 2
    p = col % 2
    info = jnp.concatenate([jnp.stack([r, col, p, x]).astype(jnp.int32), block_sizes])
    sup = support.astype(F32)

    own = jnp.transpose(coefficients, (2, 0, 1, 3)).reshape(4, 512, 256)
    own_sup = jnp.transpose(sup, (2, 0, 1)).reshape(4, 512)
    tile = lax.dynamic_slice(own, (0, x * 128, p * 128), (4, 128, 128))
    message = jnp.concatenate([jnp.swapaxes(tile, 1, 2).reshape(512, 128), lax.dynamic_slice_in_dim(own_sup, x * 128, 128, 1),
                               jnp.zeros((4, 128), F32)], axis=0)
    gathered = lax.all_gather(message, "rows")
    head = lax.dynamic_slice(own, (x, 0, p * 128), (1, 128, 128))[0]
    head = jnp.concatenate([head.T, own_sup[:, :128], right_sides[0]], axis=0)
    head = jnp.where(r == 0, head, 0.0)
    own_sup = jnp.broadcast_to(own_sup[:, :, None], (4, 512, 128))
    eye = jnp.eye(128, dtype=F32)

    active = (jnp.arange(256, dtype=jnp.int32)[None, :] < block_sizes[:, None]).astype(F32)
    away = 128 - p * 128
    lent = lax.dynamic_slice_in_dim(primal, away, 128, 2) * lax.dynamic_slice_in_dim(dual_inverse, away, 128, 2)
    lent = swap(lent * active[:, :, None] * lax.dynamic_slice_in_dim(active, away, 128, 1)[:, None, :])

    half = partial(info, own, own_sup, primal, dual_inverse, lent)
    head, half = lax.optimization_barrier((head, half))
    for pairs in ([(0, 2)], [(0, 1), (2, 3)], [(z, 8 + z) for z in range(4)]):
        head = head + over_rows(head, pairs)
    head_next = over_rows(head, [(y + z, y + 4 + z) for y in (0, 8) for z in range(4)])
    terms = exchange(half, "cols", CHIPS)
    head_next, terms = lax.optimization_barrier((head_next, terms))
    head = head + head_next
    total = jnp.sum(terms, axis=0)
    v_own = exchange(repeat(jnp.concatenate([total[:4], head[None, :128]], axis=0), 4), "cols", CHIPS)
    corner = total[4] + eye * jnp.where(p == 0, damping[0], 0.0)
    inverse = inverse_of(corner + swap(corner))
    second = over_rows(inverse, [(0, 8)])
    v_own, inverse, second, gathered = lax.optimization_barrier((v_own, inverse, second, gathered))
    v_other = swap(v_own)
    begun = lead(info, v_own, own_sup, head)
    gathered, v_other, begun = lax.optimization_barrier((gathered, v_other, begun))
    swapped = swap(gathered)
    every = exchange(lead(info, v_other, own_sup, head, [begun, inverse, second]), "rows")

    start = block_product(info, v_own, own_sup, gathered, lambda g, i: (i[2], 0, 0), head)
    updated, panel, solved = block_product(info, v_other, own_sup, swapped, lambda g, i: (i[2], 0, 0), head,
                                           list(start) + [every, damping, right_sides])
    return updated.reshape(4, 128, 1024), panel.reshape(4, 128, 128), solved


def solution(mesh):
    in_specs = (
        P(None, "rows", None, None),
        P(None, "rows", None),
        P("cols", None, None),
        P("cols", None, None),
        P("cols"),
        P(None, "rows"),
        P(None, "cols", "rows"),
    )
    out_specs = (P(None, "rows", "cols"), P(None, "rows", None), P(None, "cols", "rows"))
    return jax.shard_map(local, mesh=mesh, in_specs=in_specs, out_specs=out_specs, check_vma=False)
```

```python
import functools
import jax
import jax.numpy as jnp
from jax import lax
from jax.experimental import pallas as pl
from jax.experimental.pallas import tpu as pltpu
from jax.sharding import PartitionSpec as P

BF = jnp.bfloat16
F32 = jnp.float32
NT = (((1,), (1,)), ((), ()))
NN = (((1,), (0,)), ((), ()))
VMEM = 32 << 20


def split(v):
    h = v.astype(BF)
    return h, (v - h.astype(F32)).astype(BF)


def product(ah, al, bh, bl, dims):
    side = dims[0][1][0]
    left = jnp.concatenate([ah, al, ah], axis=1)
    right = jnp.concatenate([bh, bh, bl], axis=side)
    return lax.dot_general(left, right, dims, preferred_element_type=F32)


def choose(masks, values):
    out = jnp.zeros_like(values[0])
    for m, v in zip(masks, values):
        out = jnp.where(m, v, out)
    return out


def partial_body(info, c_ref, s_ref, x_ref, y_ref, z_ref, v_ref, wh, wl, total):
    t = pl.program_id(0)
    col, p = info[1], info[2]
    mine = pl.ds(pl.multiple_of(p * 128, 128), 128)

    @pl.when(t == 0)
    def _():
        row = lax.broadcasted_iota(jnp.int32, (256, 128), 0)
        lane = lax.broadcasted_iota(jnp.int32, (256, 128), 1)
        for u in range(3):
            size = info[4 + u]
            w = jnp.where((row < size) & (lane + p * 128 < size), x_ref[u, :, mine] * y_ref[u, :, mine], 0.0)
            wh[u], wl[u] = split(w)
            wh[3 + u], wl[3 + u] = split(z_ref[u])

    parts = [jnp.zeros((256, 128), F32)] * 4
    masks = []
    for u in range(6):
        block = ((col if u < 3 else col + 1 - 2 * p) * 3 + u % 3).astype(F32)
        m = [s_ref[k] == block for k in range(4)]
        masks.append(m)
        d = jnp.concatenate([choose(m, [c_ref[k, :, q * 128:(q + 1) * 128] for k in range(4)]) for q in range(2)], axis=1)
        dh, dl = split(d)
        v = product(dh, dl, wh[u], wl[u], NN)
        parts = [jnp.where(m[k], v, parts[k]) for k in range(4)]
    for k in range(4):
        for h in range(2):
            v_ref[h, k] = parts[k][h * 128:(h + 1) * 128]

    @pl.when(t == 0)
    def _():
        vs, es = [], []
        for m in masks:
            top = [z[:128] for z in m]
            vs.append(choose(top, [z[:128] for z in parts]))
            es.append(choose(top, [c_ref[k, :128, mine] for k in range(4)]))
        vh, vl = split(jnp.concatenate(vs, axis=1))
        eh, el = split(jnp.concatenate(es, axis=1))
        total[...] = product(vh, vl, eh, el, NT)

    for h in range(2):
        v_ref[h, 4] = total[...]


def whole(v):
    return pl.BlockSpec(v.shape, lambda g, i: (0,) * v.ndim, pipeline_mode=pl.Buffered(1))


def partial(info, c, s, x, y, z):
    out = jax.ShapeDtypeStruct((4, 5, 128, 128), F32)
    grid = pltpu.PrefetchScalarGridSpec(
        num_scalar_prefetch=1, grid=(2,),
        in_specs=[pl.BlockSpec((4, 256, 256), lambda t, i: (0, t, 0)), pl.BlockSpec((4, 256, 128), lambda t, i: (0, t, 0)), whole(x), whole(y), whole(z)],
        out_specs=pl.BlockSpec((2, 5, 128, 128), lambda t, i: (t, 0, 0, 0)),
        scratch_shapes=[pltpu.VMEM((6, 256, 128), BF)] * 2 + [pltpu.VMEM((128, 128), F32)])
    return pl.pallas_call(partial_body, grid_spec=grid, out_shape=out,
                          compiler_params=pltpu.CompilerParams(vmem_limit_bytes=VMEM), name="partial",
                          cost_estimate=pl.CostEstimate(flops=2 * 3 * 512 * 768 * 256, bytes_accessed=8 << 20, transcendentals=0))(info, c, s, x, y, z)


def gather_blocks(base, sup, high, low, axis, count=6):
    highs, lows = [], []
    for u in range(count):
        block = (base + u).astype(F32).astype(BF)
        m = [s == block for s in sup]
        highs.append(choose(m, [high(k) for k in range(4)]))
        lows.append(choose(m, [low(k) for k in range(4)]))
    return jnp.concatenate(highs, axis=axis), jnp.concatenate(lows, axis=axis)


def column_labels(rows, n):
    return jnp.broadcast_to(jnp.concatenate(rows, axis=1), (128, n)).astype(BF)


def lead_body(last, info, v_ref, s_ref, z_ref, *rest):
    if last:
        b_ref, f_ref, n_ref, o_ref, a_ref = rest
    else:
        (a_ref,) = rest
    g = pl.program_id(0)

    @pl.when(g == 0)
    def _():
        a_ref[...] = b_ref[...] if last else jnp.zeros_like(a_ref)

    rows = [split(v_ref[info[3], k]) for k in range(4)]
    tiles = [split(v_ref[k, 4]) for k in range(4)]
    sup = [s_ref[k].astype(BF) for k in range(4)]
    first = [column_labels([z_ref[128 + k:129 + k]], 128) for k in range(4)]
    ah, al = gather_blocks(12 * g, sup, lambda k: rows[k][0], lambda k: rows[k][1], 1, 12)
    bh, bl = gather_blocks(12 * g, first, lambda k: tiles[k][0], lambda k: tiles[k][1], 0, 12)
    a_ref[...] += product(ah, al, bh, bl, NN)

    if last:
        @pl.when(g == 1)
        def _():
            r, p = info[0], info[2]
            sent = jnp.where((r == 0) & (p == 1), f_ref[...], jnp.where((r == 8) & (p == 0), n_ref[...], a_ref[...]))
            for j in range(16):
                o_ref[j] = sent


def lead(info, v, s, z, more=None):
    last = more is not None
    args = [v, s, z] + (list(more) if last else [])
    specs = [whole(u) for u in args]
    specs[1] = pl.BlockSpec((4, 128, 128), lambda g, i: (0, i[3], 0))
    shape = (16, 128, 128) if last else (128, 128)
    grid = pltpu.PrefetchScalarGridSpec(
        num_scalar_prefetch=1, grid=(2,), in_specs=specs, out_specs=pl.BlockSpec(shape, lambda g, i: (0,) * len(shape)),
        scratch_shapes=[pltpu.VMEM((128, 128), F32)] if last else [])
    return pl.pallas_call(functools.partial(lead_body, last), grid_spec=grid, out_shape=jax.ShapeDtypeStruct(shape, F32),
                          compiler_params=pltpu.CompilerParams(vmem_limit_bytes=VMEM), name="lead",
                          cost_estimate=pl.CostEstimate(flops=2 * 3 * 128 * 6144 * 128, bytes_accessed=3 << 20, transcendentals=0))(info, *args)


def block_body(last, info, v_ref, r_ref, c_ref, z_ref, *rest):
    if last:
        s_ref, b_ref, e_ref, h_ref, y_ref, o_ref, p_ref, x_ref, vh, vl, ch, cl, total = rest
    else:
        o_ref, total, vh, vl, ch, cl = rest
    g = pl.program_id(0)

    @pl.when(g == 0)
    def _():
        for k in range(4):
            for t in range(4):
                vh[k, t * 128:(t + 1) * 128], vl[k, t * 128:(t + 1) * 128] = split(v_ref[t, k])
            for t in range(8):
                ch[k, :, t * 128:(t + 1) * 128], cl[k, :, t * 128:(t + 1) * 128] = split(c_ref[t, k * 128:(k + 1) * 128])
            ch[k, :, 1024:], cl[k, :, 1024:] = split(v_ref[k, 4])
        o_ref[...] = s_ref[...] if last else jnp.zeros_like(o_ref)
        total[...] = b_ref[...] if last else jnp.zeros_like(total)

    rows = [r_ref[k].astype(BF) for k in range(4)]
    ah, al = gather_blocks(6 * g, rows, lambda k: vh[k], lambda k: vl[k], 1)
    for q in range(3):
        n = 512 if q < 2 else 128
        r = slice(q * 512, q * 512 + n)
        if q < 2:
            sup = [column_labels([c_ref[4 * q + t, 512 + k:513 + k] for t in range(4)], n) for k in range(4)]
        else:
            sup = [column_labels([z_ref[128 + k:129 + k]], n) for k in range(4)]
        bh, bl = gather_blocks(6 * g, sup, lambda k: ch[k, :, r], lambda k: cl[k, :, r], 0)
        value = product(ah, al, bh, bl, NN)
        if q < 2:
            o_ref[:, r] += value
        else:
            total[...] += value

    if last:
        @pl.when(g == 3)
        def _():
            row, col, p = info[0], info[1], info[2]
            same = lax.broadcasted_iota(jnp.int32, (128, 128), 0) == lax.broadcasted_iota(jnp.int32, (128, 128), 1)
            ih, il = split(e_ref[8 * (1 - p)])
            total[:128] += jnp.where(same & (row == 0), jnp.broadcast_to(h_ref[:1], (128, 128)), 0.0)
            th, tl = split(total[...])
            panel = product(th, tl, ih, il, NT)
            p_ref[...] = panel
            ph, plo = split(panel)
            zh, zl = split(z_ref[128:136])
            sides = product(zh, zl, ih, il, NT)
            xh, xl = split(sides)
            for t in range(4):
                tile = slice(t * 128, (t + 1) * 128)
                taken = product(xh, xl, ph[tile], plo[tile], NT)
                x_ref[t] = jnp.where(t * 16 + row > 0, y_ref[t] - taken[4:], sides[4:])
            eh, el = split(e_ref[pl.ds(8 * p, 8)].reshape(1024, 128))
            qh, ql = split(product(eh, el, ih, il, NT))
            for t in range(4):
                tile = slice(t * 128, (t + 1) * 128)
                down = t * 16 + row
                outer = product(ph[tile], plo[tile], qh, ql, NT)
                for j in range(8):
                    span = slice(j * 128, (j + 1) * 128)
                    across = col * 8 + j
                    diagonal = jnp.where(same & (down == across), jnp.broadcast_to(h_ref[t:t + 1], (128, 128)), 0.0)
                    o_ref[tile, span] += diagonal - jnp.where((down > 0) & (across > 0), outer[:, span], 0.0)


def block_product(info, v, r, c, pick, z, tail=None):
    last = tail is not None
    args = [v, r, c, z] + (list(tail) if last else [])
    specs = [whole(u) for u in args]
    specs[2] = pl.BlockSpec((8, 520, 128), pick, pipeline_mode=pl.Buffered(1))
    shapes = [(512, 1024), (512, 128)] + ([(4, 4, 128)] if last else [])
    outs = [pl.BlockSpec((512, 1024), lambda g, i: (0, 0)), pl.BlockSpec((512, 128), lambda g, i: (0, 0)),
            pl.BlockSpec((4, 4, 128), lambda g, i: (0, 0, 0))]
    grid = pltpu.PrefetchScalarGridSpec(
        num_scalar_prefetch=1, grid=(4,), in_specs=specs, out_specs=outs[:len(shapes)],
        scratch_shapes=[pltpu.VMEM((4, 512, 128), BF)] * 2 + [pltpu.VMEM((4, 128, 1152), BF)] * 2
        + ([pltpu.VMEM((512, 128), F32)] if last else []))
    return pl.pallas_call(functools.partial(block_body, last), grid_spec=grid,
                          out_shape=[jax.ShapeDtypeStruct(u, F32) for u in shapes],
                          compiler_params=pltpu.CompilerParams(vmem_limit_bytes=VMEM), name="block",
                          cost_estimate=pl.CostEstimate(flops=2 * 3 * 512 * 3072 * 1152, bytes_accessed=10 << 20, transcendentals=0))(info, *args)


def inverse_body(c_ref, i_ref, o_ref):
    n = 128
    row = lax.broadcasted_iota(jnp.int32, (n, n), 0)
    col = lax.broadcasted_iota(jnp.int32, (n, n), 1)
    below = lax.broadcasted_iota(jnp.int32, (n, 1), 0)
    lane = lax.broadcasted_iota(jnp.int32, (1, n), 1)
    o_ref[...] = jnp.concatenate([c_ref[...], jnp.where(row == col, 1.0, 0.0).astype(F32)], axis=1)

    def at(v, k):
        return jnp.sum(jnp.where(lane == k, v, 0.0), axis=1, keepdims=True)

    def step(i, _):
        k = 2 * i
        line0 = o_ref[pl.ds(k, 1), :]
        line1 = o_ref[pl.ds(k + 1, 1), :]
        left = o_ref[:, :n]
        a, b, c = at(line0[:, :n], k), at(line0[:, :n], k + 1), at(line1[:, :n], k + 1)
        col0, col1 = at(left, k), at(left, k + 1)
        s0 = lax.rsqrt(a)
        b = b * s0
        s1 = lax.rsqrt(c - b * b)
        line0 = line0 * s0
        line1 = (line1 - b * line0) * s1
        f0 = jnp.where(below > k + 1, col0 * s0, 0.0)
        f1 = jnp.where(below > k + 1, (col1 - f0 * b) * s1, 0.0)
        o_ref[...] = o_ref[...] - f0 * line0 - f1 * line1
        o_ref[pl.ds(k, 1), :] = line0
        o_ref[pl.ds(k + 1, 1), :] = line1
        return 0

    lax.fori_loop(0, n // 2, step, 0)
    i_ref[...] = o_ref[:, n:]


def inverse_of(c):
    return pl.pallas_call(inverse_body, out_shape=jax.ShapeDtypeStruct((128, 128), F32), name="inverse",
                          scratch_shapes=[pltpu.VMEM((128, 256), F32)],
                          cost_estimate=pl.CostEstimate(flops=2 * 3 * 512 * 3072 * 768, bytes_accessed=1 << 20, transcendentals=0))(c)


SWAP = [(i, i ^ 1) for i in range(8)]
CHIPS = [[0, 2, 4, 6], [1, 3, 5, 7]]


def swap(v):
    return lax.ppermute(v, "cols", SWAP)


def exchange(v, axis, groups=None):
    return lax.all_to_all(v, axis, 0, 0, axis_index_groups=groups, tiled=True)


def repeat(v, n):
    return jnp.broadcast_to(v[None], (n,) + v.shape)


def over_rows(v, pairs):
    return lax.ppermute(v, "rows", pairs)


def local(coefficients, support, primal, dual_inverse, block_sizes, damping, right_sides):
    col = lax.axis_index("cols")
    r = lax.axis_index("rows")
    x = col // 2
    p = col % 2
    info = jnp.concatenate([jnp.stack([r, col, p, x]).astype(jnp.int32), block_sizes])
    sup = support.astype(F32)

    own = jnp.transpose(coefficients, (2, 0, 1, 3)).reshape(4, 512, 256)
    own_sup = jnp.transpose(sup, (2, 0, 1)).reshape(4, 512)
    tile = lax.dynamic_slice(own, (0, x * 128, p * 128), (4, 128, 128))
    message = jnp.concatenate([jnp.swapaxes(tile, 1, 2).reshape(512, 128), lax.dynamic_slice_in_dim(own_sup, x * 128, 128, 1),
                               jnp.zeros((4, 128), F32)], axis=0)
    gathered = lax.all_gather(message, "rows")
    head = lax.dynamic_slice(own, (x, 0, p * 128), (1, 128, 128))[0]
    head = jnp.concatenate([head.T, own_sup[:, :128], right_sides[0]], axis=0)
    head = jnp.where(r == 0, head, 0.0)
    own_sup = jnp.broadcast_to(own_sup[:, :, None], (4, 512, 128))
    eye = jnp.eye(128, dtype=F32)

    active = (jnp.arange(256, dtype=jnp.int32)[None, :] < block_sizes[:, None]).astype(F32)
    away = 128 - p * 128
    lent = lax.dynamic_slice_in_dim(primal, away, 128, 2) * lax.dynamic_slice_in_dim(dual_inverse, away, 128, 2)
    lent = swap(lent * active[:, :, None] * lax.dynamic_slice_in_dim(active, away, 128, 1)[:, None, :])

    half = partial(info, own, own_sup, primal, dual_inverse, lent)
    head, half = lax.optimization_barrier((head, half))
    for pairs in ([(0, 2)], [(0, 1), (2, 3)], [(z, 8 + z) for z in range(4)]):
        head = head + over_rows(head, pairs)
    head_next = over_rows(head, [(y + z, y + 4 + z) for y in (0, 8) for z in range(4)])
    terms = exchange(half, "cols", CHIPS)
    head_next, terms = lax.optimization_barrier((head_next, terms))
    head = head + head_next
    total = jnp.sum(terms, axis=0)
    v_own = exchange(repeat(jnp.concatenate([total[:4], head[None, :128]], axis=0), 4), "cols", CHIPS)
    corner = total[4] + eye * jnp.where(p == 0, damping[0], 0.0)
    inverse = inverse_of(corner + swap(corner))
    second = over_rows(inverse, [(0, 8)])
    v_own, inverse, second, gathered = lax.optimization_barrier((v_own, inverse, second, gathered))
    v_other = swap(v_own)
    begun = lead(info, v_own, own_sup, head)
    gathered, v_other, begun = lax.optimization_barrier((gathered, v_other, begun))
    swapped = swap(gathered)
    every = exchange(lead(info, v_other, own_sup, head, [begun, inverse, second]), "rows")

    start = block_product(info, v_own, own_sup, gathered, lambda g, i: (i[2], 0, 0), head)
    updated, panel, solved = block_product(info, v_other, own_sup, swapped, lambda g, i: (i[2], 0, 0), head,
                                           list(start) + [every, damping, right_sides])
    return updated.reshape(4, 128, 1024), panel.reshape(4, 128, 128), solved


def solution(mesh):
    in_specs = (
        P(None, "rows", None, None),
        P(None, "rows", None),
        P("cols", None, None),
        P("cols", None, None),
        P("cols"),
        P(None, "rows"),
        P(None, "cols", "rows"),
    )
    out_specs = (P(None, "rows", "cols"), P(None, "rows", None), P(None, "cols", "rows"))
    return jax.shard_map(local, mesh=mesh, in_specs=in_specs, out_specs=out_specs, check_vma=False)
```

```python
import functools
import jax
import jax.numpy as jnp
from jax import lax
from jax.experimental import pallas as pl
from jax.experimental.pallas import tpu as pltpu
from jax.sharding import PartitionSpec as P

BF = jnp.bfloat16
F32 = jnp.float32
NT = (((1,), (1,)), ((), ()))
NN = (((1,), (0,)), ((), ()))
VMEM = 32 << 20
LARGE = 52 << 20


def split(v):
    h = v.astype(BF)
    return h, (v - h.astype(F32)).astype(BF)


def product(ah, al, bh, bl, dims):
    side = dims[0][1][0]
    left = jnp.concatenate([ah, al, ah], axis=1)
    right = jnp.concatenate([bh, bh, bl], axis=side)
    return lax.dot_general(left, right, dims, preferred_element_type=F32)


def choose(masks, values):
    out = jnp.zeros_like(values[0])
    for m, v in zip(masks, values):
        out = jnp.where(m, v, out)
    return out


def partial_body(info, c_ref, s_ref, x_ref, y_ref, z_ref, v_ref, wh, wl, total):
    t = pl.program_id(0)
    col, p = info[1], info[2]
    mine = pl.ds(pl.multiple_of(p * 128, 128), 128)

    @pl.when(t == 0)
    def _():
        row = lax.broadcasted_iota(jnp.int32, (256, 128), 0)
        lane = lax.broadcasted_iota(jnp.int32, (256, 128), 1)
        for u in range(3):
            size = info[4 + u]
            w = jnp.where((row < size) & (lane + p * 128 < size), x_ref[u, :, mine] * y_ref[u, :, mine], 0.0)
            wh[u], wl[u] = split(w)
            wh[3 + u], wl[3 + u] = split(z_ref[u])

    parts = [jnp.zeros((256, 128), F32)] * 4
    masks = []
    for u in range(6):
        block = ((col if u < 3 else col + 1 - 2 * p) * 3 + u % 3).astype(F32)
        m = [s_ref[k] == block for k in range(4)]
        masks.append(m)
        d = jnp.concatenate([choose(m, [c_ref[k, :, q * 128:(q + 1) * 128] for k in range(4)]) for q in range(2)], axis=1)
        dh, dl = split(d)
        v = product(dh, dl, wh[u], wl[u], NN)
        parts = [jnp.where(m[k], v, parts[k]) for k in range(4)]
    for k in range(4):
        for h in range(2):
            v_ref[h, k] = parts[k][h * 128:(h + 1) * 128]

    @pl.when(t == 0)
    def _():
        vs, es = [], []
        for m in masks:
            top = [z[:128] for z in m]
            vs.append(choose(top, [z[:128] for z in parts]))
            es.append(choose(top, [c_ref[k, :128, mine] for k in range(4)]))
        vh, vl = split(jnp.concatenate(vs, axis=1))
        eh, el = split(jnp.concatenate(es, axis=1))
        total[...] = product(vh, vl, eh, el, NT)

    for h in range(2):
        v_ref[h, 4] = total[...]


def whole(v):
    return pl.BlockSpec(v.shape, lambda g, i: (0,) * v.ndim, pipeline_mode=pl.Buffered(1))


def partial(info, c, s, x, y, z):
    out = jax.ShapeDtypeStruct((4, 5, 128, 128), F32)
    grid = pltpu.PrefetchScalarGridSpec(
        num_scalar_prefetch=1, grid=(2,),
        in_specs=[pl.BlockSpec((4, 256, 256), lambda t, i: (0, t, 0)), pl.BlockSpec((4, 256, 128), lambda t, i: (0, t, 0)), whole(x), whole(y), whole(z)],
        out_specs=pl.BlockSpec((2, 5, 128, 128), lambda t, i: (t, 0, 0, 0)),
        scratch_shapes=[pltpu.VMEM((6, 256, 128), BF)] * 2 + [pltpu.VMEM((128, 128), F32)])
    return pl.pallas_call(partial_body, grid_spec=grid, out_shape=out,
                          compiler_params=pltpu.CompilerParams(vmem_limit_bytes=VMEM), name="partial",
                          cost_estimate=pl.CostEstimate(flops=2 * 3 * 512 * 768 * 256, bytes_accessed=8 << 20, transcendentals=0))(info, c, s, x, y, z)


def gather_blocks(base, sup, high, low, axis, count=6):
    highs, lows = [], []
    for u in range(count):
        block = (base + u).astype(F32).astype(BF)
        m = [s == block for s in sup]
        highs.append(choose(m, [high(k) for k in range(4)]))
        lows.append(choose(m, [low(k) for k in range(4)]))
    return jnp.concatenate(highs, axis=axis), jnp.concatenate(lows, axis=axis)


def column_labels(rows, n):
    return jnp.broadcast_to(jnp.concatenate(rows, axis=1), (128, n)).astype(BF)


def lead_body(last, info, v_ref, s_ref, z_ref, *rest):
    if last:
        b_ref, f_ref, n_ref, o_ref, a_ref = rest
    else:
        (a_ref,) = rest
    g = pl.program_id(0)

    @pl.when(g == 0)
    def _():
        a_ref[...] = b_ref[...] if last else jnp.zeros_like(a_ref)

    rows = [split(v_ref[info[3], k]) for k in range(4)]
    tiles = [split(v_ref[k, 4]) for k in range(4)]
    sup = [s_ref[k].astype(BF) for k in range(4)]
    first = [column_labels([z_ref[128 + k:129 + k]], 128) for k in range(4)]
    ah, al = gather_blocks(12 * g, sup, lambda k: rows[k][0], lambda k: rows[k][1], 1, 12)
    bh, bl = gather_blocks(12 * g, first, lambda k: tiles[k][0], lambda k: tiles[k][1], 0, 12)
    a_ref[...] += product(ah, al, bh, bl, NN)

    if last:
        @pl.when(g == 1)
        def _():
            r, p = info[0], info[2]
            sent = jnp.where((r == 0) & (p == 1), f_ref[...], jnp.where((r == 8) & (p == 0), n_ref[...], a_ref[...]))
            for j in range(16):
                o_ref[j] = sent


def lead(info, v, s, z, more=None):
    last = more is not None
    args = [v, s, z] + (list(more) if last else [])
    specs = [whole(u) for u in args]
    specs[1] = pl.BlockSpec((4, 128, 128), lambda g, i: (0, i[3], 0))
    shape = (16, 128, 128) if last else (128, 128)
    grid = pltpu.PrefetchScalarGridSpec(
        num_scalar_prefetch=1, grid=(2,), in_specs=specs, out_specs=pl.BlockSpec(shape, lambda g, i: (0,) * len(shape)),
        scratch_shapes=[pltpu.VMEM((128, 128), F32)] if last else [])
    return pl.pallas_call(functools.partial(lead_body, last), grid_spec=grid, out_shape=jax.ShapeDtypeStruct(shape, F32),
                          compiler_params=pltpu.CompilerParams(vmem_limit_bytes=VMEM), name="lead",
                          cost_estimate=pl.CostEstimate(flops=2 * 3 * 128 * 6144 * 128, bytes_accessed=3 << 20, transcendentals=0))(info, *args)


def block_body(last, info, v_ref, r_ref, c_ref, z_ref, *rest):
    if last:
        s_ref, b_ref, e_ref, h_ref, y_ref, o_ref, p_ref, x_ref, vh, vl, ch, cl, total = rest
    else:
        o_ref, total, vh, vl, ch, cl = rest
    g = pl.program_id(0)

    @pl.when(g == 0)
    def _():
        for k in range(4):
            for t in range(4):
                vh[k, t * 128:(t + 1) * 128], vl[k, t * 128:(t + 1) * 128] = split(v_ref[t, k])
            for t in range(8):
                ch[k, :, t * 128:(t + 1) * 128], cl[k, :, t * 128:(t + 1) * 128] = split(c_ref[t, k * 128:(k + 1) * 128])
            ch[k, :, 1024:], cl[k, :, 1024:] = split(v_ref[k, 4])
        o_ref[...] = s_ref[...] if last else jnp.zeros_like(o_ref)
        total[...] = b_ref[...] if last else jnp.zeros_like(total)

    rows = [r_ref[k].astype(BF) for k in range(4)]
    ah, al = gather_blocks(6 * g, rows, lambda k: vh[k], lambda k: vl[k], 1)
    for q in range(3):
        n = 512 if q < 2 else 128
        r = slice(q * 512, q * 512 + n)
        if q < 2:
            sup = [column_labels([c_ref[4 * q + t, 512 + k:513 + k] for t in range(4)], n) for k in range(4)]
        else:
            sup = [column_labels([z_ref[128 + k:129 + k]], n) for k in range(4)]
        bh, bl = gather_blocks(6 * g, sup, lambda k: ch[k, :, r], lambda k: cl[k, :, r], 0)
        value = product(ah, al, bh, bl, NN)
        if q < 2:
            o_ref[:, r] += value
        else:
            total[...] += value

    if last:
        @pl.when(g == 3)
        def _():
            row, col, p = info[0], info[1], info[2]
            same = lax.broadcasted_iota(jnp.int32, (128, 128), 0) == lax.broadcasted_iota(jnp.int32, (128, 128), 1)
            ih, il = split(e_ref[8 * (1 - p)])
            total[:128] += jnp.where(same & (row == 0), jnp.broadcast_to(h_ref[:1], (128, 128)), 0.0)
            th, tl = split(total[...])
            panel = product(th, tl, ih, il, NT)
            p_ref[...] = panel
            ph, plo = split(panel)
            zh, zl = split(z_ref[128:136])
            sides = product(zh, zl, ih, il, NT)
            xh, xl = split(sides)
            for t in range(4):
                tile = slice(t * 128, (t + 1) * 128)
                taken = product(xh, xl, ph[tile], plo[tile], NT)
                x_ref[t] = jnp.where(t * 16 + row > 0, y_ref[t] - taken[4:], sides[4:])
            eh, el = split(e_ref[pl.ds(8 * p, 8)].reshape(1024, 128))
            qh, ql = split(product(eh, el, ih, il, NT))
            for t in range(4):
                tile = slice(t * 128, (t + 1) * 128)
                down = t * 16 + row
                outer = product(ph[tile], plo[tile], qh, ql, NT)
                for j in range(8):
                    span = slice(j * 128, (j + 1) * 128)
                    across = col * 8 + j
                    diagonal = jnp.where(same & (down == across), jnp.broadcast_to(h_ref[t:t + 1], (128, 128)), 0.0)
                    o_ref[tile, span] += diagonal - jnp.where((down > 0) & (across > 0), outer[:, span], 0.0)


def block_product(info, v, r, c, pick, z, tail=None):
    last = tail is not None
    args = [v, r, c, z] + (list(tail) if last else [])
    specs = [whole(u) for u in args]
    specs[2] = pl.BlockSpec((8, 520, 128), pick, pipeline_mode=pl.Buffered(1))
    shapes = [(512, 1024), (512, 128)] + ([(4, 4, 128)] if last else [])
    outs = [pl.BlockSpec((512, 1024), lambda g, i: (0, 0)), pl.BlockSpec((512, 128), lambda g, i: (0, 0)),
            pl.BlockSpec((4, 4, 128), lambda g, i: (0, 0, 0))]
    grid = pltpu.PrefetchScalarGridSpec(
        num_scalar_prefetch=1, grid=(4,), in_specs=specs, out_specs=outs[:len(shapes)],
        scratch_shapes=[pltpu.VMEM((4, 512, 128), BF)] * 2 + [pltpu.VMEM((4, 128, 1152), BF)] * 2
        + ([pltpu.VMEM((512, 128), F32)] if last else []))
    return pl.pallas_call(functools.partial(block_body, last), grid_spec=grid,
                          out_shape=[jax.ShapeDtypeStruct(u, F32) for u in shapes],
                          compiler_params=pltpu.CompilerParams(vmem_limit_bytes=LARGE), name="block",
                          cost_estimate=pl.CostEstimate(flops=2 * 3 * 512 * 3072 * 1152, bytes_accessed=10 << 20, transcendentals=0))(info, *args)


def inverse_body(c_ref, i_ref, o_ref):
    n = 128
    row = lax.broadcasted_iota(jnp.int32, (n, n), 0)
    col = lax.broadcasted_iota(jnp.int32, (n, n), 1)
    below = lax.broadcasted_iota(jnp.int32, (n, 1), 0)
    lane = lax.broadcasted_iota(jnp.int32, (1, n), 1)
    o_ref[...] = jnp.concatenate([c_ref[...], jnp.where(row == col, 1.0, 0.0).astype(F32)], axis=1)

    def at(v, k):
        return jnp.sum(jnp.where(lane == k, v, 0.0), axis=1, keepdims=True)

    def step(i, _):
        k = 2 * i
        line0 = o_ref[pl.ds(k, 1), :]
        line1 = o_ref[pl.ds(k + 1, 1), :]
        left = o_ref[:, :n]
        a, b, c = at(line0[:, :n], k), at(line0[:, :n], k + 1), at(line1[:, :n], k + 1)
        col0, col1 = at(left, k), at(left, k + 1)
        s0 = lax.rsqrt(a)
        b = b * s0
        s1 = lax.rsqrt(c - b * b)
        line0 = line0 * s0
        line1 = (line1 - b * line0) * s1
        f0 = jnp.where(below > k + 1, col0 * s0, 0.0)
        f1 = jnp.where(below > k + 1, (col1 - f0 * b) * s1, 0.0)
        o_ref[...] = o_ref[...] - f0 * line0 - f1 * line1
        o_ref[pl.ds(k, 1), :] = line0
        o_ref[pl.ds(k + 1, 1), :] = line1
        return 0

    lax.fori_loop(0, n // 2, step, 0)
    i_ref[...] = o_ref[:, n:]


def inverse_of(c):
    return pl.pallas_call(inverse_body, out_shape=jax.ShapeDtypeStruct((128, 128), F32), name="inverse",
                          scratch_shapes=[pltpu.VMEM((128, 256), F32)],
                          cost_estimate=pl.CostEstimate(flops=2 * 3 * 512 * 3072 * 768, bytes_accessed=1 << 20, transcendentals=0))(c)


SWAP = [(i, i ^ 1) for i in range(8)]
CHIPS = [[0, 2, 4, 6], [1, 3, 5, 7]]


def swap(v):
    return lax.ppermute(v, "cols", SWAP)


def exchange(v, axis, groups=None):
    return lax.all_to_all(v, axis, 0, 0, axis_index_groups=groups, tiled=True)


def repeat(v, n):
    return jnp.broadcast_to(v[None], (n,) + v.shape)


def over_rows(v, pairs):
    return lax.ppermute(v, "rows", pairs)


def local(coefficients, support, primal, dual_inverse, block_sizes, damping, right_sides):
    col = lax.axis_index("cols")
    r = lax.axis_index("rows")
    x = col // 2
    p = col % 2
    info = jnp.concatenate([jnp.stack([r, col, p, x]).astype(jnp.int32), block_sizes])
    sup = support.astype(F32)

    own = jnp.transpose(coefficients, (2, 0, 1, 3)).reshape(4, 512, 256)
    own_sup = jnp.transpose(sup, (2, 0, 1)).reshape(4, 512)
    tile = lax.dynamic_slice(own, (0, x * 128, p * 128), (4, 128, 128))
    message = jnp.concatenate([jnp.swapaxes(tile, 1, 2).reshape(512, 128), lax.dynamic_slice_in_dim(own_sup, x * 128, 128, 1),
                               jnp.zeros((4, 128), F32)], axis=0)
    gathered = lax.all_gather(message, "rows")
    head = lax.dynamic_slice(own, (x, 0, p * 128), (1, 128, 128))[0]
    head = jnp.concatenate([head.T, own_sup[:, :128], right_sides[0]], axis=0)
    head = jnp.where(r == 0, head, 0.0)
    own_sup = jnp.broadcast_to(own_sup[:, :, None], (4, 512, 128))
    eye = jnp.eye(128, dtype=F32)

    active = (jnp.arange(256, dtype=jnp.int32)[None, :] < block_sizes[:, None]).astype(F32)
    away = 128 - p * 128
    lent = lax.dynamic_slice_in_dim(primal, away, 128, 2) * lax.dynamic_slice_in_dim(dual_inverse, away, 128, 2)
    lent = swap(lent * active[:, :, None] * lax.dynamic_slice_in_dim(active, away, 128, 1)[:, None, :])

    half = partial(info, own, own_sup, primal, dual_inverse, lent)
    head, half = lax.optimization_barrier((head, half))
    for pairs in ([(0, 2)], [(0, 1), (2, 3)], [(z, 8 + z) for z in range(4)]):
        head = head + over_rows(head, pairs)
    head_next = over_rows(head, [(y + z, y + 4 + z) for y in (0, 8) for z in range(4)])
    terms = exchange(half, "cols", CHIPS)
    head_next, terms = lax.optimization_barrier((head_next, terms))
    head = head + head_next
    total = jnp.sum(terms, axis=0)
    v_own = exchange(repeat(jnp.concatenate([total[:4], head[None, :128]], axis=0), 4), "cols", CHIPS)
    corner = total[4] + eye * jnp.where(p == 0, damping[0], 0.0)
    inverse = inverse_of(corner + swap(corner))
    second = over_rows(inverse, [(0, 8)])
    v_own, inverse, second, gathered = lax.optimization_barrier((v_own, inverse, second, gathered))
    v_other = swap(v_own)
    begun = lead(info, v_own, own_sup, head)
    gathered, v_other, begun = lax.optimization_barrier((gathered, v_other, begun))
    swapped = swap(gathered)
    every = exchange(lead(info, v_other, own_sup, head, [begun, inverse, second]), "rows")

    start = block_product(info, v_own, own_sup, gathered, lambda g, i: (i[2], 0, 0), head)
    updated, panel, solved = block_product(info, v_other, own_sup, swapped, lambda g, i: (i[2], 0, 0), head,
                                           list(start) + [every, damping, right_sides])
    return updated.reshape(4, 128, 1024), panel.reshape(4, 128, 128), solved


def solution(mesh):
    in_specs = (
        P(None, "rows", None, None),
        P(None, "rows", None),
        P("cols", None, None),
        P("cols", None, None),
        P("cols"),
        P(None, "rows"),
        P(None, "cols", "rows"),
    )
    out_specs = (P(None, "rows", "cols"), P(None, "rows", None), P(None, "cols", "rows"))
    return jax.shard_map(local, mesh=mesh, in_specs=in_specs, out_specs=out_specs, check_vma=False)
```

```python
import functools
import jax
import jax.numpy as jnp
from jax import lax
from jax.experimental import pallas as pl
from jax.experimental.pallas import tpu as pltpu
from jax.sharding import PartitionSpec as P

BF = jnp.bfloat16
F32 = jnp.float32
NT = (((1,), (1,)), ((), ()))
NN = (((1,), (0,)), ((), ()))
VMEM = 32 << 20
LARGE = 52 << 20


def split(v):
    h = v.astype(BF)
    return h, (v - h.astype(F32)).astype(BF)


def product(ah, al, bh, bl, dims):
    side = dims[0][1][0]
    left = jnp.concatenate([ah, al, ah], axis=1)
    right = jnp.concatenate([bh, bh, bl], axis=side)
    return lax.dot_general(left, right, dims, preferred_element_type=F32)


def choose(masks, values):
    out = jnp.zeros_like(values[0])
    for m, v in zip(masks, values):
        out = jnp.where(m, v, out)
    return out


def partial_body(info, c_ref, s_ref, x_ref, y_ref, z_ref, v_ref, wh, wl, total):
    t = pl.program_id(0)
    col, p = info[1], info[2]
    mine = pl.ds(pl.multiple_of(p * 128, 128), 128)

    @pl.when(t == 0)
    def _():
        row = lax.broadcasted_iota(jnp.int32, (256, 128), 0)
        lane = lax.broadcasted_iota(jnp.int32, (256, 128), 1)
        for u in range(3):
            size = info[4 + u]
            w = jnp.where((row < size) & (lane + p * 128 < size), x_ref[u, :, mine] * y_ref[u, :, mine], 0.0)
            wh[u], wl[u] = split(w)
            wh[3 + u], wl[3 + u] = split(z_ref[u])

    parts = [jnp.zeros((256, 128), F32)] * 4
    masks = []
    for u in range(6):
        block = ((col if u < 3 else col + 1 - 2 * p) * 3 + u % 3).astype(F32)
        m = [s_ref[k] == block for k in range(4)]
        masks.append(m)
        d = jnp.concatenate([choose(m, [c_ref[k, :, q * 128:(q + 1) * 128] for k in range(4)]) for q in range(2)], axis=1)
        dh, dl = split(d)
        v = product(dh, dl, wh[u], wl[u], NN)
        parts = [jnp.where(m[k], v, parts[k]) for k in range(4)]
    for k in range(4):
        for h in range(2):
            v_ref[h, k] = parts[k][h * 128:(h + 1) * 128]

    @pl.when(t == 0)
    def _():
        vs, es = [], []
        for m in masks:
            top = [z[:128] for z in m]
            vs.append(choose(top, [z[:128] for z in parts]))
            es.append(choose(top, [c_ref[k, :128, mine] for k in range(4)]))
        vh, vl = split(jnp.concatenate(vs, axis=1))
        eh, el = split(jnp.concatenate(es, axis=1))
        total[...] = product(vh, vl, eh, el, NT)

    for h in range(2):
        v_ref[h, 4] = total[...]


def whole(v):
    return pl.BlockSpec(v.shape, lambda g, i: (0,) * v.ndim, pipeline_mode=pl.Buffered(1))


def partial(info, c, s, x, y, z):
    out = jax.ShapeDtypeStruct((4, 5, 128, 128), F32)
    grid = pltpu.PrefetchScalarGridSpec(
        num_scalar_prefetch=1, grid=(2,),
        in_specs=[pl.BlockSpec((4, 256, 256), lambda t, i: (0, t, 0)), pl.BlockSpec((4, 256, 128), lambda t, i: (0, t, 0)), whole(x), whole(y), whole(z)],
        out_specs=pl.BlockSpec((2, 5, 128, 128), lambda t, i: (t, 0, 0, 0)),
        scratch_shapes=[pltpu.VMEM((6, 256, 128), BF)] * 2 + [pltpu.VMEM((128, 128), F32)])
    return pl.pallas_call(partial_body, grid_spec=grid, out_shape=out,
                          compiler_params=pltpu.CompilerParams(vmem_limit_bytes=VMEM), name="partial",
                          cost_estimate=pl.CostEstimate(flops=2 * 3 * 512 * 768 * 256, bytes_accessed=8 << 20, transcendentals=0))(info, c, s, x, y, z)


def gather_blocks(base, sup, high, low, axis, count=6):
    highs, lows = [], []
    for u in range(count):
        block = (base + u).astype(F32).astype(BF)
        m = [s == block for s in sup]
        highs.append(choose(m, [high(k) for k in range(4)]))
        lows.append(choose(m, [low(k) for k in range(4)]))
    return jnp.concatenate(highs, axis=axis), jnp.concatenate(lows, axis=axis)


def column_labels(rows, n):
    return jnp.broadcast_to(jnp.concatenate(rows, axis=1), (128, n)).astype(BF)


def lead_body(last, info, v_ref, s_ref, z_ref, *rest):
    if last:
        b_ref, f_ref, n_ref, o_ref, a_ref = rest
    else:
        (a_ref,) = rest
    g = pl.program_id(0)

    @pl.when(g == 0)
    def _():
        a_ref[...] = b_ref[...] if last else jnp.zeros_like(a_ref)

    rows = [split(v_ref[info[3], k]) for k in range(4)]
    tiles = [split(v_ref[k, 4]) for k in range(4)]
    sup = [s_ref[k].astype(BF) for k in range(4)]
    first = [column_labels([z_ref[128 + k:129 + k]], 128) for k in range(4)]
    ah, al = gather_blocks(12 * g, sup, lambda k: rows[k][0], lambda k: rows[k][1], 1, 12)
    bh, bl = gather_blocks(12 * g, first, lambda k: tiles[k][0], lambda k: tiles[k][1], 0, 12)
    a_ref[...] += product(ah, al, bh, bl, NN)

    if last:
        @pl.when(g == 1)
        def _():
            r, p = info[0], info[2]
            sent = jnp.where((r == 0) & (p == 1), f_ref[...], jnp.where((r == 12) & (p == 0), n_ref[...], a_ref[...]))
            for j in range(16):
                o_ref[j] = sent


def lead(info, v, s, z, more=None):
    last = more is not None
    args = [v, s, z] + (list(more) if last else [])
    specs = [whole(u) for u in args]
    specs[1] = pl.BlockSpec((4, 128, 128), lambda g, i: (0, i[3], 0))
    shape = (16, 128, 128) if last else (128, 128)
    grid = pltpu.PrefetchScalarGridSpec(
        num_scalar_prefetch=1, grid=(2,), in_specs=specs, out_specs=pl.BlockSpec(shape, lambda g, i: (0,) * len(shape)),
        scratch_shapes=[pltpu.VMEM((128, 128), F32)] if last else [])
    return pl.pallas_call(functools.partial(lead_body, last), grid_spec=grid, out_shape=jax.ShapeDtypeStruct(shape, F32),
                          compiler_params=pltpu.CompilerParams(vmem_limit_bytes=VMEM), name="lead",
                          cost_estimate=pl.CostEstimate(flops=2 * 3 * 128 * 6144 * 128, bytes_accessed=3 << 20, transcendentals=0))(info, *args)


def block_body(last, info, v_ref, r_ref, c_ref, z_ref, *rest):
    if last:
        s_ref, b_ref, e_ref, h_ref, y_ref, o_ref, p_ref, x_ref, vh, vl, ch, cl, total = rest
    else:
        o_ref, total, vh, vl, ch, cl = rest
    g = pl.program_id(0)

    @pl.when(g == 0)
    def _():
        for k in range(4):
            for t in range(4):
                vh[k, t * 128:(t + 1) * 128], vl[k, t * 128:(t + 1) * 128] = split(v_ref[t, k])
            for t in range(8):
                ch[k, :, t * 128:(t + 1) * 128], cl[k, :, t * 128:(t + 1) * 128] = split(c_ref[t, k * 128:(k + 1) * 128])
            ch[k, :, 1024:], cl[k, :, 1024:] = split(v_ref[k, 4])
        o_ref[...] = s_ref[...] if last else jnp.zeros_like(o_ref)
        total[...] = b_ref[...] if last else jnp.zeros_like(total)

    rows = [r_ref[k].astype(BF) for k in range(4)]
    ah, al = gather_blocks(6 * g, rows, lambda k: vh[k], lambda k: vl[k], 1)
    for q in range(3):
        n = 512 if q < 2 else 128
        r = slice(q * 512, q * 512 + n)
        if q < 2:
            sup = [column_labels([c_ref[4 * q + t, 512 + k:513 + k] for t in range(4)], n) for k in range(4)]
        else:
            sup = [column_labels([z_ref[128 + k:129 + k]], n) for k in range(4)]
        bh, bl = gather_blocks(6 * g, sup, lambda k: ch[k, :, r], lambda k: cl[k, :, r], 0)
        value = product(ah, al, bh, bl, NN)
        if q < 2:
            o_ref[:, r] += value
        else:
            total[...] += value

    if last:
        @pl.when(g == 3)
        def _():
            row, col, p = info[0], info[1], info[2]
            same = lax.broadcasted_iota(jnp.int32, (128, 128), 0) == lax.broadcasted_iota(jnp.int32, (128, 128), 1)
            ih, il = split(e_ref[12 * (1 - p)])
            total[:128] += jnp.where(same & (row == 0), jnp.broadcast_to(h_ref[:1], (128, 128)), 0.0)
            th, tl = split(total[...])
            panel = product(th, tl, ih, il, NT)
            p_ref[...] = panel
            ph, plo = split(panel)
            zh, zl = split(z_ref[128:136])
            sides = product(zh, zl, ih, il, NT)
            xh, xl = split(sides)
            for t in range(4):
                tile = slice(t * 128, (t + 1) * 128)
                taken = product(xh, xl, ph[tile], plo[tile], NT)
                x_ref[t] = jnp.where(t * 16 + row > 0, y_ref[t] - taken[4:], sides[4:])
            eh, el = split(e_ref[pl.ds(8 * p, 8)].reshape(1024, 128))
            qh, ql = split(product(eh, el, ih, il, NT))
            for t in range(4):
                tile = slice(t * 128, (t + 1) * 128)
                down = t * 16 + row
                outer = product(ph[tile], plo[tile], qh, ql, NT)
                for j in range(8):
                    span = slice(j * 128, (j + 1) * 128)
                    across = col * 8 + j
                    diagonal = jnp.where(same & (down == across), jnp.broadcast_to(h_ref[t:t + 1], (128, 128)), 0.0)
                    o_ref[tile, span] += diagonal - jnp.where((down > 0) & (across > 0), outer[:, span], 0.0)


def block_product(info, v, r, c, pick, z, tail=None):
    last = tail is not None
    args = [v, r, c, z] + (list(tail) if last else [])
    specs = [whole(u) for u in args]
    specs[2] = pl.BlockSpec((8, 520, 128), pick, pipeline_mode=pl.Buffered(1))
    shapes = [(512, 1024), (512, 128)] + ([(4, 4, 128)] if last else [])
    outs = [pl.BlockSpec((512, 1024), lambda g, i: (0, 0)), pl.BlockSpec((512, 128), lambda g, i: (0, 0)),
            pl.BlockSpec((4, 4, 128), lambda g, i: (0, 0, 0))]
    grid = pltpu.PrefetchScalarGridSpec(
        num_scalar_prefetch=1, grid=(4,), in_specs=specs, out_specs=outs[:len(shapes)],
        scratch_shapes=[pltpu.VMEM((4, 512, 128), BF)] * 2 + [pltpu.VMEM((4, 128, 1152), BF)] * 2
        + ([pltpu.VMEM((512, 128), F32)] if last else []))
    return pl.pallas_call(functools.partial(block_body, last), grid_spec=grid,
                          out_shape=[jax.ShapeDtypeStruct(u, F32) for u in shapes],
                          compiler_params=pltpu.CompilerParams(vmem_limit_bytes=LARGE), name="block",
                          cost_estimate=pl.CostEstimate(flops=2 * 3 * 512 * 3072 * 1152, bytes_accessed=10 << 20, transcendentals=0))(info, *args)


def inverse_body(c_ref, i_ref, o_ref):
    n = 128
    row = lax.broadcasted_iota(jnp.int32, (n, n), 0)
    col = lax.broadcasted_iota(jnp.int32, (n, n), 1)
    below = lax.broadcasted_iota(jnp.int32, (n, 1), 0)
    lane = lax.broadcasted_iota(jnp.int32, (1, n), 1)
    o_ref[...] = jnp.concatenate([c_ref[...], jnp.where(row == col, 1.0, 0.0).astype(F32)], axis=1)

    def at(v, k):
        return jnp.sum(jnp.where(lane == k, v, 0.0), axis=1, keepdims=True)

    def step(i, _):
        k = 2 * i
        line0 = o_ref[pl.ds(k, 1), :]
        line1 = o_ref[pl.ds(k + 1, 1), :]
        left = o_ref[:, :n]
        a, b, c = at(line0[:, :n], k), at(line0[:, :n], k + 1), at(line1[:, :n], k + 1)
        col0, col1 = at(left, k), at(left, k + 1)
        s0 = lax.rsqrt(a)
        b = b * s0
        s1 = lax.rsqrt(c - b * b)
        line0 = line0 * s0
        line1 = (line1 - b * line0) * s1
        f0 = jnp.where(below > k + 1, col0 * s0, 0.0)
        f1 = jnp.where(below > k + 1, (col1 - f0 * b) * s1, 0.0)
        o_ref[...] = o_ref[...] - f0 * line0 - f1 * line1
        o_ref[pl.ds(k, 1), :] = line0
        o_ref[pl.ds(k + 1, 1), :] = line1
        return 0

    lax.fori_loop(0, n // 2, step, 0)
    i_ref[...] = o_ref[:, n:]


def inverse_of(c):
    return pl.pallas_call(inverse_body, out_shape=jax.ShapeDtypeStruct((128, 128), F32), name="inverse",
                          scratch_shapes=[pltpu.VMEM((128, 256), F32)],
                          cost_estimate=pl.CostEstimate(flops=2 * 3 * 512 * 3072 * 768, bytes_accessed=1 << 20, transcendentals=0))(c)


SWAP = [(i, i ^ 1) for i in range(8)]
CHIPS = [[0, 2, 4, 6], [1, 3, 5, 7]]


def swap(v):
    return lax.ppermute(v, "cols", SWAP)


def exchange(v, axis, groups=None):
    return lax.all_to_all(v, axis, 0, 0, axis_index_groups=groups, tiled=True)


def repeat(v, n):
    return jnp.broadcast_to(v[None], (n,) + v.shape)


def over_rows(v, pairs):
    return lax.ppermute(v, "rows", pairs)


def local(coefficients, support, primal, dual_inverse, block_sizes, damping, right_sides):
    col = lax.axis_index("cols")
    r = lax.axis_index("rows")
    x = col // 2
    p = col % 2
    info = jnp.concatenate([jnp.stack([r, col, p, x]).astype(jnp.int32), block_sizes])
    sup = support.astype(F32)

    own = jnp.transpose(coefficients, (2, 0, 1, 3)).reshape(4, 512, 256)
    own_sup = jnp.transpose(sup, (2, 0, 1)).reshape(4, 512)
    tile = lax.dynamic_slice(own, (0, x * 128, p * 128), (4, 128, 128))
    message = jnp.concatenate([jnp.swapaxes(tile, 1, 2).reshape(512, 128), lax.dynamic_slice_in_dim(own_sup, x * 128, 128, 1),
                               jnp.zeros((4, 128), F32)], axis=0)
    gathered = lax.all_gather(message, "rows")
    head = lax.dynamic_slice(own, (x, 0, p * 128), (1, 128, 128))[0]
    head = jnp.concatenate([head.T, own_sup[:, :128], right_sides[0]], axis=0)
    head = jnp.where(r == 0, head, 0.0)
    own_sup = jnp.broadcast_to(own_sup[:, :, None], (4, 512, 128))
    eye = jnp.eye(128, dtype=F32)

    active = (jnp.arange(256, dtype=jnp.int32)[None, :] < block_sizes[:, None]).astype(F32)
    away = 128 - p * 128
    lent = lax.dynamic_slice_in_dim(primal, away, 128, 2) * lax.dynamic_slice_in_dim(dual_inverse, away, 128, 2)
    lent = swap(lent * active[:, :, None] * lax.dynamic_slice_in_dim(active, away, 128, 1)[:, None, :])

    half = partial(info, own, own_sup, primal, dual_inverse, lent)
    head, half = lax.optimization_barrier((head, half))
    for pairs in ([(0, 1)], [(0, 3), (1, 2)], [(z, 4 + z) for z in range(4)]):
        head = head + over_rows(head, pairs)
    head_next = over_rows(head, [(y + z, (12 if y == 0 else 8) + z) for y in (0, 4) for z in range(4)])
    terms = exchange(half, "cols", CHIPS)
    head_next, terms = lax.optimization_barrier((head_next, terms))
    head = head + head_next
    total = jnp.sum(terms, axis=0)
    v_own = exchange(repeat(jnp.concatenate([total[:4], head[None, :128]], axis=0), 4), "cols", CHIPS)
    corner = total[4] + eye * jnp.where(p == 0, damping[0], 0.0)
    inverse = inverse_of(corner + swap(corner))
    second = over_rows(inverse, [(0, 12)])
    v_own, inverse, second, gathered = lax.optimization_barrier((v_own, inverse, second, gathered))
    v_other = swap(v_own)
    begun = lead(info, v_own, own_sup, head)
    gathered, v_other, begun = lax.optimization_barrier((gathered, v_other, begun))
    swapped = swap(gathered)
    every = exchange(lead(info, v_other, own_sup, head, [begun, inverse, second]), "rows")

    start = block_product(info, v_own, own_sup, gathered, lambda g, i: (i[2], 0, 0), head)
    updated, panel, solved = block_product(info, v_other, own_sup, swapped, lambda g, i: (i[2], 0, 0), head,
                                           list(start) + [every, damping, right_sides])
    return updated.reshape(4, 128, 1024), panel.reshape(4, 128, 128), solved


def solution(mesh):
    in_specs = (
        P(None, "rows", None, None),
        P(None, "rows", None),
        P("cols", None, None),
        P("cols", None, None),
        P("cols"),
        P(None, "rows"),
        P(None, "cols", "rows"),
    )
    out_specs = (P(None, "rows", "cols"), P(None, "rows", None), P(None, "cols", "rows"))
    return jax.shard_map(local, mesh=mesh, in_specs=in_specs, out_specs=out_specs, check_vma=False)
```

```python
import functools
import jax
import jax.numpy as jnp
from jax import lax
from jax.experimental import pallas as pl
from jax.experimental.pallas import tpu as pltpu
from jax.sharding import PartitionSpec as P

BF = jnp.bfloat16
F32 = jnp.float32
NT = (((1,), (1,)), ((), ()))
NN = (((1,), (0,)), ((), ()))
VMEM = 32 << 20
LARGE = 51 << 20


def split(v):
    h = v.astype(BF)
    return h, (v - h.astype(F32)).astype(BF)


def product(ah, al, bh, bl, dims):
    side = dims[0][1][0]
    left = jnp.concatenate([ah, al, ah], axis=1)
    right = jnp.concatenate([bh, bh, bl], axis=side)
    return lax.dot_general(left, right, dims, preferred_element_type=F32)


def choose(masks, values):
    out = jnp.zeros_like(values[0])
    for m, v in zip(masks, values):
        out = jnp.where(m, v, out)
    return out


def partial_body(info, c_ref, s_ref, x_ref, y_ref, z_ref, v_ref, wh, wl, total):
    t = pl.program_id(0)
    col, p = info[1], info[2]
    mine = pl.ds(pl.multiple_of(p * 128, 128), 128)

    @pl.when(t == 0)
    def _():
        row = lax.broadcasted_iota(jnp.int32, (256, 128), 0)
        lane = lax.broadcasted_iota(jnp.int32, (256, 128), 1)
        for u in range(3):
            size = info[4 + u]
            w = jnp.where((row < size) & (lane + p * 128 < size), x_ref[u, :, mine] * y_ref[u, :, mine], 0.0)
            wh[u], wl[u] = split(w)
            wh[3 + u], wl[3 + u] = split(z_ref[u])

    parts = [jnp.zeros((256, 128), F32)] * 4
    masks = []
    for u in range(6):
        block = ((col if u < 3 else col + 1 - 2 * p) * 3 + u % 3).astype(F32)
        m = [s_ref[k] == block for k in range(4)]
        masks.append(m)
        d = jnp.concatenate([choose(m, [c_ref[k, :, q * 128:(q + 1) * 128] for k in range(4)]) for q in range(2)], axis=1)
        dh, dl = split(d)
        v = product(dh, dl, wh[u], wl[u], NN)
        parts = [jnp.where(m[k], v, parts[k]) for k in range(4)]
    for k in range(4):
        for h in range(2):
            v_ref[h, k] = parts[k][h * 128:(h + 1) * 128]

    @pl.when(t == 0)
    def _():
        vs, es = [], []
        for m in masks:
            top = [z[:128] for z in m]
            vs.append(choose(top, [z[:128] for z in parts]))
            es.append(choose(top, [c_ref[k, :128, mine] for k in range(4)]))
        vh, vl = split(jnp.concatenate(vs, axis=1))
        eh, el = split(jnp.concatenate(es, axis=1))
        total[...] = product(vh, vl, eh, el, NT)

    for h in range(2):
        v_ref[h, 4] = total[...]


def whole(v):
    return pl.BlockSpec(v.shape, lambda g, i: (0,) * v.ndim, pipeline_mode=pl.Buffered(1))


def partial(info, c, s, x, y, z):
    out = jax.ShapeDtypeStruct((4, 5, 128, 128), F32)
    grid = pltpu.PrefetchScalarGridSpec(
        num_scalar_prefetch=1, grid=(2,),
        in_specs=[pl.BlockSpec((4, 256, 256), lambda t, i: (0, t, 0)), pl.BlockSpec((4, 256, 128), lambda t, i: (0, t, 0)), whole(x), whole(y), whole(z)],
        out_specs=pl.BlockSpec((2, 5, 128, 128), lambda t, i: (t, 0, 0, 0)),
        scratch_shapes=[pltpu.VMEM((6, 256, 128), BF)] * 2 + [pltpu.VMEM((128, 128), F32)])
    return pl.pallas_call(partial_body, grid_spec=grid, out_shape=out,
                          compiler_params=pltpu.CompilerParams(vmem_limit_bytes=VMEM), name="partial",
                          cost_estimate=pl.CostEstimate(flops=2 * 3 * 512 * 768 * 256, bytes_accessed=8 << 20, transcendentals=0))(info, c, s, x, y, z)


def gather_blocks(base, sup, high, low, axis, count=6):
    highs, lows = [], []
    for u in range(count):
        block = (base + u).astype(F32).astype(BF)
        m = [s == block for s in sup]
        highs.append(choose(m, [high(k) for k in range(4)]))
        lows.append(choose(m, [low(k) for k in range(4)]))
    return jnp.concatenate(highs, axis=axis), jnp.concatenate(lows, axis=axis)


def column_labels(rows, n):
    return jnp.broadcast_to(jnp.concatenate(rows, axis=1), (128, n)).astype(BF)


def assemble_body(t_ref, h_ref, o_ref, c_ref):
    for k in range(5):
        total = t_ref[0, k] + t_ref[1, k] + t_ref[2, k] + t_ref[3, k]
        if k == 4:
            c_ref[...] = total
        for j in range(4):
            o_ref[j, k] = h_ref[:128] if k == 4 else total


def assemble(terms, head):
    return pl.pallas_call(assemble_body, out_shape=[jax.ShapeDtypeStruct((4, 5, 128, 128), F32), jax.ShapeDtypeStruct((128, 128), F32)],
                          compiler_params=pltpu.CompilerParams(vmem_limit_bytes=VMEM), name="assemble",
                          cost_estimate=pl.CostEstimate(flops=1 << 20, bytes_accessed=3 << 20, transcendentals=0))(terms, head)


def lead_body(last, info, v_ref, s_ref, z_ref, *rest):
    if last:
        b_ref, f_ref, n_ref, o_ref, a_ref = rest
    else:
        (a_ref,) = rest
    g = pl.program_id(0)

    @pl.when(g == 0)
    def _():
        a_ref[...] = b_ref[...] if last else jnp.zeros_like(a_ref)

    rows = [split(v_ref[info[3], k]) for k in range(4)]
    tiles = [split(v_ref[k, 4]) for k in range(4)]
    sup = [s_ref[k].astype(BF) for k in range(4)]
    first = [column_labels([z_ref[128 + k:129 + k]], 128) for k in range(4)]
    ah, al = gather_blocks(12 * g, sup, lambda k: rows[k][0], lambda k: rows[k][1], 1, 12)
    bh, bl = gather_blocks(12 * g, first, lambda k: tiles[k][0], lambda k: tiles[k][1], 0, 12)
    a_ref[...] += product(ah, al, bh, bl, NN)

    if last:
        @pl.when(g == 1)
        def _():
            r, p = info[0], info[2]
            sent = jnp.where((r == 0) & (p == 1), f_ref[...], jnp.where((r == 12) & (p == 0), n_ref[...], a_ref[...]))
            for j in range(16):
                o_ref[j] = sent


def lead(info, v, s, z, more=None):
    last = more is not None
    args = [v, s, z] + (list(more) if last else [])
    specs = [whole(u) for u in args]
    specs[1] = pl.BlockSpec((4, 128, 128), lambda g, i: (0, i[3], 0))
    shape = (16, 128, 128) if last else (128, 128)
    grid = pltpu.PrefetchScalarGridSpec(
        num_scalar_prefetch=1, grid=(2,), in_specs=specs, out_specs=pl.BlockSpec(shape, lambda g, i: (0,) * len(shape)),
        scratch_shapes=[pltpu.VMEM((128, 128), F32)] if last else [])
    return pl.pallas_call(functools.partial(lead_body, last), grid_spec=grid, out_shape=jax.ShapeDtypeStruct(shape, F32),
                          compiler_params=pltpu.CompilerParams(vmem_limit_bytes=VMEM), name="lead",
                          cost_estimate=pl.CostEstimate(flops=2 * 3 * 128 * 6144 * 128, bytes_accessed=3 << 20, transcendentals=0))(info, *args)


def block_body(last, info, v_ref, r_ref, c_ref, z_ref, *rest):
    if last:
        s_ref, b_ref, e_ref, h_ref, y_ref, o_ref, p_ref, x_ref, vh, vl, ch, cl, total = rest
    else:
        o_ref, total, vh, vl, ch, cl = rest
    g = pl.program_id(0)

    @pl.when(g == 0)
    def _():
        for k in range(4):
            for t in range(4):
                vh[k, t * 128:(t + 1) * 128], vl[k, t * 128:(t + 1) * 128] = split(v_ref[t, k])
            for t in range(8):
                ch[k, :, t * 128:(t + 1) * 128], cl[k, :, t * 128:(t + 1) * 128] = split(c_ref[t, k * 128:(k + 1) * 128])
            ch[k, :, 1024:], cl[k, :, 1024:] = split(v_ref[k, 4])
        o_ref[...] = s_ref[...] if last else jnp.zeros_like(o_ref)
        total[...] = b_ref[...] if last else jnp.zeros_like(total)

    rows = [r_ref[k].astype(BF) for k in range(4)]
    ah, al = gather_blocks(6 * g, rows, lambda k: vh[k], lambda k: vl[k], 1)
    for q in range(3):
        n = 512 if q < 2 else 128
        r = slice(q * 512, q * 512 + n)
        if q < 2:
            sup = [column_labels([c_ref[4 * q + t, 512 + k:513 + k] for t in range(4)], n) for k in range(4)]
        else:
            sup = [column_labels([z_ref[128 + k:129 + k]], n) for k in range(4)]
        bh, bl = gather_blocks(6 * g, sup, lambda k: ch[k, :, r], lambda k: cl[k, :, r], 0)
        value = product(ah, al, bh, bl, NN)
        if q < 2:
            o_ref[:, r] += value
        else:
            total[...] += value

    if last:
        @pl.when(g == 3)
        def _():
            row, col, p = info[0], info[1], info[2]
            same = lax.broadcasted_iota(jnp.int32, (128, 128), 0) == lax.broadcasted_iota(jnp.int32, (128, 128), 1)
            ih, il = split(e_ref[12 * (1 - p)])
            total[:128] += jnp.where(same & (row == 0), jnp.broadcast_to(h_ref[:1], (128, 128)), 0.0)
            th, tl = split(total[...])
            panel = product(th, tl, ih, il, NT)
            p_ref[...] = panel
            ph, plo = split(panel)
            zh, zl = split(z_ref[128:136])
            sides = product(zh, zl, ih, il, NT)
            xh, xl = split(sides)
            for t in range(4):
                tile = slice(t * 128, (t + 1) * 128)
                taken = product(xh, xl, ph[tile], plo[tile], NT)
                x_ref[t] = jnp.where(t * 16 + row > 0, y_ref[t] - taken[4:], sides[4:])
            eh, el = split(e_ref[pl.ds(8 * p, 8)].reshape(1024, 128))
            qh, ql = split(product(eh, el, ih, il, NT))
            for t in range(4):
                tile = slice(t * 128, (t + 1) * 128)
                down = t * 16 + row
                outer = product(ph[tile], plo[tile], qh, ql, NT)
                for j in range(8):
                    span = slice(j * 128, (j + 1) * 128)
                    across = col * 8 + j
                    diagonal = jnp.where(same & (down == across), jnp.broadcast_to(h_ref[t:t + 1], (128, 128)), 0.0)
                    o_ref[tile, span] += diagonal - jnp.where((down > 0) & (across > 0), outer[:, span], 0.0)


def block_product(info, v, r, c, pick, z, tail=None):
    last = tail is not None
    args = [v, r, c, z] + (list(tail) if last else [])
    specs = [whole(u) for u in args]
    specs[2] = pl.BlockSpec((8, 520, 128), pick, pipeline_mode=pl.Buffered(1))
    shapes = [(512, 1024), (512, 128)] + ([(4, 4, 128)] if last else [])
    outs = [pl.BlockSpec((512, 1024), lambda g, i: (0, 0)), pl.BlockSpec((512, 128), lambda g, i: (0, 0)),
            pl.BlockSpec((4, 4, 128), lambda g, i: (0, 0, 0))]
    grid = pltpu.PrefetchScalarGridSpec(
        num_scalar_prefetch=1, grid=(4,), in_specs=specs, out_specs=outs[:len(shapes)],
        scratch_shapes=[pltpu.VMEM((4, 512, 128), BF)] * 2 + [pltpu.VMEM((4, 128, 1152), BF)] * 2
        + ([pltpu.VMEM((512, 128), F32)] if last else []))
    return pl.pallas_call(functools.partial(block_body, last), grid_spec=grid,
                          out_shape=[jax.ShapeDtypeStruct(u, F32) for u in shapes],
                          compiler_params=pltpu.CompilerParams(vmem_limit_bytes=LARGE), name="block",
                          cost_estimate=pl.CostEstimate(flops=2 * 3 * 512 * 3072 * 1152, bytes_accessed=10 << 20, transcendentals=0))(info, *args)


def inverse_body(c_ref, i_ref, o_ref):
    n = 128
    row = lax.broadcasted_iota(jnp.int32, (n, n), 0)
    col = lax.broadcasted_iota(jnp.int32, (n, n), 1)
    below = lax.broadcasted_iota(jnp.int32, (n, 1), 0)
    lane = lax.broadcasted_iota(jnp.int32, (1, n), 1)
    o_ref[...] = jnp.concatenate([c_ref[...], jnp.where(row == col, 1.0, 0.0).astype(F32)], axis=1)

    def at(v, k):
        return jnp.sum(jnp.where(lane == k, v, 0.0), axis=1, keepdims=True)

    def step(i, _):
        k = 2 * i
        line0 = o_ref[pl.ds(k, 1), :]
        line1 = o_ref[pl.ds(k + 1, 1), :]
        left = o_ref[:, :n]
        a, b, c = at(line0[:, :n], k), at(line0[:, :n], k + 1), at(line1[:, :n], k + 1)
        col0, col1 = at(left, k), at(left, k + 1)
        s0 = lax.rsqrt(a)
        b = b * s0
        s1 = lax.rsqrt(c - b * b)
        line0 = line0 * s0
        line1 = (line1 - b * line0) * s1
        f0 = jnp.where(below > k + 1, col0 * s0, 0.0)
        f1 = jnp.where(below > k + 1, (col1 - f0 * b) * s1, 0.0)
        o_ref[...] = o_ref[...] - f0 * line0 - f1 * line1
        o_ref[pl.ds(k, 1), :] = line0
        o_ref[pl.ds(k + 1, 1), :] = line1
        return 0

    lax.fori_loop(0, n // 2, step, 0)
    i_ref[...] = o_ref[:, n:]


def inverse_of(c):
    return pl.pallas_call(inverse_body, out_shape=jax.ShapeDtypeStruct((128, 128), F32), name="inverse",
                          scratch_shapes=[pltpu.VMEM((128, 256), F32)],
                          cost_estimate=pl.CostEstimate(flops=2 * 3 * 512 * 3072 * 768, bytes_accessed=1 << 20, transcendentals=0))(c)


SWAP = [(i, i ^ 1) for i in range(8)]
CHIPS = [[0, 2, 4, 6], [1, 3, 5, 7]]


def swap(v):
    return lax.ppermute(v, "cols", SWAP)


def exchange(v, axis, groups=None):
    return lax.all_to_all(v, axis, 0, 0, axis_index_groups=groups, tiled=True)


def repeat(v, n):
    return jnp.broadcast_to(v[None], (n,) + v.shape)


def over_rows(v, pairs):
    return lax.ppermute(v, "rows", pairs)


def local(coefficients, support, primal, dual_inverse, block_sizes, damping, right_sides):
    col = lax.axis_index("cols")
    r = lax.axis_index("rows")
    x = col // 2
    p = col % 2
    info = jnp.concatenate([jnp.stack([r, col, p, x]).astype(jnp.int32), block_sizes])
    sup = support.astype(F32)

    own = jnp.transpose(coefficients, (2, 0, 1, 3)).reshape(4, 512, 256)
    own_sup = jnp.transpose(sup, (2, 0, 1)).reshape(4, 512)
    tile = lax.dynamic_slice(own, (0, x * 128, p * 128), (4, 128, 128))
    message = jnp.concatenate([jnp.swapaxes(tile, 1, 2).reshape(512, 128), lax.dynamic_slice_in_dim(own_sup, x * 128, 128, 1),
                               jnp.zeros((4, 128), F32)], axis=0)
    gathered = lax.all_gather(message, "rows")
    head = lax.dynamic_slice(own, (x, 0, p * 128), (1, 128, 128))[0]
    head = jnp.concatenate([head.T, own_sup[:, :128], right_sides[0]], axis=0)
    head = jnp.where(r == 0, head, 0.0)
    own_sup = jnp.broadcast_to(own_sup[:, :, None], (4, 512, 128))
    eye = jnp.eye(128, dtype=F32)

    active = (jnp.arange(256, dtype=jnp.int32)[None, :] < block_sizes[:, None]).astype(F32)
    away = 128 - p * 128
    lent = lax.dynamic_slice_in_dim(primal, away, 128, 2) * lax.dynamic_slice_in_dim(dual_inverse, away, 128, 2)
    lent = swap(lent * active[:, :, None] * lax.dynamic_slice_in_dim(active, away, 128, 1)[:, None, :])

    half = partial(info, own, own_sup, primal, dual_inverse, lent)
    head, half = lax.optimization_barrier((head, half))
    for pairs in ([(0, 1)], [(0, 3), (1, 2)], [(z, 4 + z) for z in range(4)]):
        head = head + over_rows(head, pairs)
    head_next = over_rows(head, [(y + z, (12 if y == 0 else 8) + z) for y in (0, 4) for z in range(4)])
    terms = exchange(half, "cols", CHIPS)
    head_next, terms = lax.optimization_barrier((head_next, terms))
    head = head + head_next
    mixed, corner = assemble(terms, head)
    v_own = exchange(mixed, "cols", CHIPS)
    corner = corner + eye * jnp.where(p == 0, damping[0], 0.0)
    inverse = inverse_of(corner + swap(corner))
    second = over_rows(inverse, [(0, 12)])
    v_own, inverse, second, gathered = lax.optimization_barrier((v_own, inverse, second, gathered))
    v_other = swap(v_own)
    begun = lead(info, v_own, own_sup, head)
    gathered, v_other, begun = lax.optimization_barrier((gathered, v_other, begun))
    swapped = swap(gathered)
    every = exchange(lead(info, v_other, own_sup, head, [begun, inverse, second]), "rows")

    start = block_product(info, v_own, own_sup, gathered, lambda g, i: (i[2], 0, 0), head)
    updated, panel, solved = block_product(info, v_other, own_sup, swapped, lambda g, i: (i[2], 0, 0), head,
                                           list(start) + [every, damping, right_sides])
    return updated.reshape(4, 128, 1024), panel.reshape(4, 128, 128), solved


def solution(mesh):
    in_specs = (
        P(None, "rows", None, None),
        P(None, "rows", None),
        P("cols", None, None),
        P("cols", None, None),
        P("cols"),
        P(None, "rows"),
        P(None, "cols", "rows"),
    )
    out_specs = (P(None, "rows", "cols"), P(None, "rows", None), P(None, "cols", "rows"))
    return jax.shard_map(local, mesh=mesh, in_specs=in_specs, out_specs=out_specs, check_vma=False)
```

```python
import functools
import jax
import jax.numpy as jnp
from jax import lax
from jax.experimental import pallas as pl
from jax.experimental.pallas import tpu as pltpu
from jax.sharding import PartitionSpec as P

BF = jnp.bfloat16
F32 = jnp.float32
NT = (((1,), (1,)), ((), ()))
NN = (((1,), (0,)), ((), ()))
VMEM = 32 << 20
LARGE = 51 << 20


def split(v):
    h = v.astype(BF)
    return h, (v - h.astype(F32)).astype(BF)


def product(ah, al, bh, bl, dims):
    side = dims[0][1][0]
    left = jnp.concatenate([ah, al, ah], axis=1)
    right = jnp.concatenate([bh, bh, bl], axis=side)
    return lax.dot_general(left, right, dims, preferred_element_type=F32)


def choose(masks, values):
    out = jnp.zeros_like(values[0])
    for m, v in zip(masks, values):
        out = jnp.where(m, v, out)
    return out


def partial_body(info, c_ref, s_ref, x_ref, y_ref, z_ref, v_ref, wh, wl, total):
    t = pl.program_id(0)
    col, p = info[1], info[2]
    mine = pl.ds(pl.multiple_of(p * 128, 128), 128)

    @pl.when(t == 0)
    def _():
        row = lax.broadcasted_iota(jnp.int32, (256, 128), 0)
        lane = lax.broadcasted_iota(jnp.int32, (256, 128), 1)
        for u in range(3):
            size = info[4 + u]
            w = jnp.where((row < size) & (lane + p * 128 < size), x_ref[u, :, mine] * y_ref[u, :, mine], 0.0)
            wh[u], wl[u] = split(w)
            wh[3 + u], wl[3 + u] = split(z_ref[u])

    parts = [jnp.zeros((256, 128), F32)] * 4
    masks = []
    for u in range(6):
        block = ((col if u < 3 else col + 1 - 2 * p) * 3 + u % 3).astype(F32)
        m = [s_ref[k] == block for k in range(4)]
        masks.append(m)
        d = jnp.concatenate([choose(m, [c_ref[k, :, q * 128:(q + 1) * 128] for k in range(4)]) for q in range(2)], axis=1)
        dh, dl = split(d)
        v = product(dh, dl, wh[u], wl[u], NN)
        parts = [jnp.where(m[k], v, parts[k]) for k in range(4)]
    for k in range(4):
        for h in range(2):
            v_ref[h, k] = parts[k][h * 128:(h + 1) * 128]

    @pl.when(t == 0)
    def _():
        vs, es = [], []
        for m in masks:
            top = [z[:128] for z in m]
            vs.append(choose(top, [z[:128] for z in parts]))
            es.append(choose(top, [c_ref[k, :128, mine] for k in range(4)]))
        vh, vl = split(jnp.concatenate(vs, axis=1))
        eh, el = split(jnp.concatenate(es, axis=1))
        total[...] = product(vh, vl, eh, el, NT)

    for h in range(2):
        v_ref[h, 4] = total[...]


def whole(v):
    return pl.BlockSpec(v.shape, lambda g, i: (0,) * v.ndim, pipeline_mode=pl.Buffered(1))


def partial(info, c, s, x, y, z):
    out = jax.ShapeDtypeStruct((4, 5, 128, 128), F32)
    grid = pltpu.PrefetchScalarGridSpec(
        num_scalar_prefetch=1, grid=(2,),
        in_specs=[pl.BlockSpec((4, 256, 256), lambda t, i: (0, t, 0)), pl.BlockSpec((4, 256, 128), lambda t, i: (0, t, 0)), whole(x), whole(y), whole(z)],
        out_specs=pl.BlockSpec((2, 5, 128, 128), lambda t, i: (t, 0, 0, 0)),
        scratch_shapes=[pltpu.VMEM((6, 256, 128), BF)] * 2 + [pltpu.VMEM((128, 128), F32)])
    return pl.pallas_call(partial_body, grid_spec=grid, out_shape=out,
                          compiler_params=pltpu.CompilerParams(vmem_limit_bytes=VMEM), name="partial",
                          cost_estimate=pl.CostEstimate(flops=2 * 3 * 512 * 768 * 256, bytes_accessed=8 << 20, transcendentals=0))(info, c, s, x, y, z)


def gather_blocks(base, sup, high, low, axis, count=6):
    highs, lows = [], []
    for u in range(count):
        block = (base + u).astype(F32).astype(BF)
        m = [s == block for s in sup]
        highs.append(choose(m, [high(k) for k in range(4)]))
        lows.append(choose(m, [low(k) for k in range(4)]))
    return jnp.concatenate(highs, axis=axis), jnp.concatenate(lows, axis=axis)


def column_labels(rows, n):
    return jnp.broadcast_to(jnp.concatenate(rows, axis=1), (128, n)).astype(BF)


def assemble_body(t_ref, h_ref, o_ref, c_ref):
    for k in range(5):
        total = t_ref[0, k] + t_ref[1, k] + t_ref[2, k] + t_ref[3, k]
        if k == 4:
            c_ref[...] = total
        for j in range(4):
            o_ref[j, k] = h_ref[:128] if k == 4 else total


def assemble(terms, head):
    return pl.pallas_call(assemble_body, out_shape=[jax.ShapeDtypeStruct((4, 5, 128, 128), F32), jax.ShapeDtypeStruct((128, 128), F32)],
                          compiler_params=pltpu.CompilerParams(vmem_limit_bytes=VMEM), name="assemble",
                          cost_estimate=pl.CostEstimate(flops=1 << 20, bytes_accessed=3 << 20, transcendentals=0))(terms, head)


def lead_body(last, info, v_ref, s_ref, z_ref, *rest):
    if last:
        b_ref, f_ref, n_ref, o_ref, a_ref = rest
    else:
        (a_ref,) = rest
    g = pl.program_id(0)

    @pl.when(g == 0)
    def _():
        a_ref[...] = b_ref[...] if last else jnp.zeros_like(a_ref)

    rows = [split(v_ref[info[3], k]) for k in range(4)]
    tiles = [split(v_ref[k, 4]) for k in range(4)]
    sup = [s_ref[k].astype(BF) for k in range(4)]
    first = [column_labels([z_ref[128 + k:129 + k]], 128) for k in range(4)]
    ah, al = gather_blocks(12 * g, sup, lambda k: rows[k][0], lambda k: rows[k][1], 1, 12)
    bh, bl = gather_blocks(12 * g, first, lambda k: tiles[k][0], lambda k: tiles[k][1], 0, 12)
    a_ref[...] += product(ah, al, bh, bl, NN)

    if last:
        @pl.when(g == 1)
        def _():
            r, p = info[0], info[2]
            sent = jnp.where((r == 0) & (p == 1), f_ref[...], jnp.where((r == 12) & (p == 0), n_ref[...], a_ref[...]))
            for j in range(16):
                o_ref[j] = sent


def lead(info, v, s, z, more=None):
    last = more is not None
    args = [v, s, z] + (list(more) if last else [])
    specs = [whole(u) for u in args]
    specs[1] = pl.BlockSpec((4, 128, 128), lambda g, i: (0, i[3], 0))
    shape = (16, 128, 128) if last else (128, 128)
    grid = pltpu.PrefetchScalarGridSpec(
        num_scalar_prefetch=1, grid=(2,), in_specs=specs, out_specs=pl.BlockSpec(shape, lambda g, i: (0,) * len(shape)),
        scratch_shapes=[pltpu.VMEM((128, 128), F32)] if last else [])
    return pl.pallas_call(functools.partial(lead_body, last), grid_spec=grid, out_shape=jax.ShapeDtypeStruct(shape, F32),
                          compiler_params=pltpu.CompilerParams(vmem_limit_bytes=VMEM), name="lead",
                          cost_estimate=pl.CostEstimate(flops=2 * 3 * 128 * 6144 * 128, bytes_accessed=3 << 20, transcendentals=0))(info, *args)


def block_body(last, info, v_ref, r_ref, c_ref, z_ref, *rest):
    if last:
        s_ref, b_ref, e_ref, h_ref, y_ref, o_ref, p_ref, x_ref, vh, vl, ch, cl, total = rest
    else:
        o_ref, total, vh, vl, ch, cl = rest
    g = pl.program_id(0)

    @pl.when(g == 0)
    def _():
        for k in range(4):
            for t in range(4):
                vh[k, t * 128:(t + 1) * 128], vl[k, t * 128:(t + 1) * 128] = split(v_ref[t, k])
            for t in range(8):
                ch[k, :, t * 128:(t + 1) * 128], cl[k, :, t * 128:(t + 1) * 128] = split(c_ref[t, k * 128:(k + 1) * 128])
            ch[k, :, 1024:], cl[k, :, 1024:] = split(v_ref[k, 4])
        o_ref[...] = s_ref[...] if last else jnp.zeros_like(o_ref)
        total[...] = b_ref[...] if last else jnp.zeros_like(total)

    rows = [r_ref[k].astype(BF) for k in range(4)]
    ah, al = gather_blocks(12 * g, rows, lambda k: vh[k], lambda k: vl[k], 1, 12)
    both = jnp.concatenate([ah, al], axis=0)
    for q in range(3):
        n = 512 if q < 2 else 128
        r = slice(q * 512, q * 512 + n)
        if q < 2:
            sup = [column_labels([c_ref[4 * q + t, 512 + k:513 + k] for t in range(4)], n) for k in range(4)]
        else:
            sup = [column_labels([z_ref[128 + k:129 + k]], n) for k in range(4)]
        bh, bl = gather_blocks(12 * g, sup, lambda k: ch[k, :, r], lambda k: cl[k, :, r], 0, 12)
        pair = lax.dot_general(both, bh, NN, preferred_element_type=F32)
        value = pair[:512] + pair[512:] + lax.dot_general(ah, bl, NN, preferred_element_type=F32)
        if q < 2:
            o_ref[:, r] += value
        else:
            total[...] += value

    if last:
        @pl.when(g == 1)
        def _():
            row, col, p = info[0], info[1], info[2]
            same = lax.broadcasted_iota(jnp.int32, (128, 128), 0) == lax.broadcasted_iota(jnp.int32, (128, 128), 1)
            ih, il = split(e_ref[12 * (1 - p)])
            total[:128] += jnp.where(same & (row == 0), jnp.broadcast_to(h_ref[:1], (128, 128)), 0.0)
            th, tl = split(total[...])
            panel = product(th, tl, ih, il, NT)
            p_ref[...] = panel
            ph, plo = split(panel)
            zh, zl = split(z_ref[128:136])
            sides = product(zh, zl, ih, il, NT)
            xh, xl = split(sides)
            for t in range(4):
                tile = slice(t * 128, (t + 1) * 128)
                taken = product(xh, xl, ph[tile], plo[tile], NT)
                x_ref[t] = jnp.where(t * 16 + row > 0, y_ref[t] - taken[4:], sides[4:])
            eh, el = split(e_ref[pl.ds(8 * p, 8)].reshape(1024, 128))
            qh, ql = split(product(eh, el, ih, il, NT))
            for t in range(4):
                tile = slice(t * 128, (t + 1) * 128)
                down = t * 16 + row
                outer = product(ph[tile], plo[tile], qh, ql, NT)
                for j in range(8):
                    span = slice(j * 128, (j + 1) * 128)
                    across = col * 8 + j
                    diagonal = jnp.where(same & (down == across), jnp.broadcast_to(h_ref[t:t + 1], (128, 128)), 0.0)
                    o_ref[tile, span] += diagonal - jnp.where((down > 0) & (across > 0), outer[:, span], 0.0)


def block_product(info, v, r, c, pick, z, tail=None):
    last = tail is not None
    args = [v, r, c, z] + (list(tail) if last else [])
    specs = [whole(u) for u in args]
    specs[2] = pl.BlockSpec((8, 520, 128), pick, pipeline_mode=pl.Buffered(1))
    shapes = [(512, 1024), (512, 128)] + ([(4, 4, 128)] if last else [])
    outs = [pl.BlockSpec((512, 1024), lambda g, i: (0, 0)), pl.BlockSpec((512, 128), lambda g, i: (0, 0)),
            pl.BlockSpec((4, 4, 128), lambda g, i: (0, 0, 0))]
    grid = pltpu.PrefetchScalarGridSpec(
        num_scalar_prefetch=1, grid=(2,), in_specs=specs, out_specs=outs[:len(shapes)],
        scratch_shapes=[pltpu.VMEM((4, 512, 128), BF)] * 2 + [pltpu.VMEM((4, 128, 1152), BF)] * 2
        + ([pltpu.VMEM((512, 128), F32)] if last else []))
    return pl.pallas_call(functools.partial(block_body, last), grid_spec=grid,
                          out_shape=[jax.ShapeDtypeStruct(u, F32) for u in shapes],
                          compiler_params=pltpu.CompilerParams(vmem_limit_bytes=LARGE), name="block",
                          cost_estimate=pl.CostEstimate(flops=2 * 3 * 512 * 3072 * 1152, bytes_accessed=10 << 20, transcendentals=0))(info, *args)


def inverse_body(c_ref, i_ref, o_ref):
    n = 128
    row = lax.broadcasted_iota(jnp.int32, (n, n), 0)
    col = lax.broadcasted_iota(jnp.int32, (n, n), 1)
    below = lax.broadcasted_iota(jnp.int32, (n, 1), 0)
    lane = lax.broadcasted_iota(jnp.int32, (1, n), 1)
    o_ref[...] = jnp.concatenate([c_ref[...], jnp.where(row == col, 1.0, 0.0).astype(F32)], axis=1)

    def at(v, k):
        return jnp.sum(jnp.where(lane == k, v, 0.0), axis=1, keepdims=True)

    def step(i, _):
        k = 2 * i
        line0 = o_ref[pl.ds(k, 1), :]
        line1 = o_ref[pl.ds(k + 1, 1), :]
        left = o_ref[:, :n]
        a, b, c = at(line0[:, :n], k), at(line0[:, :n], k + 1), at(line1[:, :n], k + 1)
        col0, col1 = at(left, k), at(left, k + 1)
        s0 = lax.rsqrt(a)
        b = b * s0
        s1 = lax.rsqrt(c - b * b)
        line0 = line0 * s0
        line1 = (line1 - b * line0) * s1
        f0 = jnp.where(below > k + 1, col0 * s0, 0.0)
        f1 = jnp.where(below > k + 1, (col1 - f0 * b) * s1, 0.0)
        o_ref[...] = o_ref[...] - f0 * line0 - f1 * line1
        o_ref[pl.ds(k, 1), :] = line0
        o_ref[pl.ds(k + 1, 1), :] = line1
        return 0

    lax.fori_loop(0, n // 2, step, 0)
    i_ref[...] = o_ref[:, n:]


def inverse_of(c):
    return pl.pallas_call(inverse_body, out_shape=jax.ShapeDtypeStruct((128, 128), F32), name="inverse",
                          scratch_shapes=[pltpu.VMEM((128, 256), F32)],
                          cost_estimate=pl.CostEstimate(flops=2 * 3 * 512 * 3072 * 768, bytes_accessed=1 << 20, transcendentals=0))(c)


SWAP = [(i, i ^ 1) for i in range(8)]
CHIPS = [[0, 2, 4, 6], [1, 3, 5, 7]]


def swap(v):
    return lax.ppermute(v, "cols", SWAP)


def exchange(v, axis, groups=None):
    return lax.all_to_all(v, axis, 0, 0, axis_index_groups=groups, tiled=True)


def repeat(v, n):
    return jnp.broadcast_to(v[None], (n,) + v.shape)


def over_rows(v, pairs):
    return lax.ppermute(v, "rows", pairs)


def local(coefficients, support, primal, dual_inverse, block_sizes, damping, right_sides):
    col = lax.axis_index("cols")
    r = lax.axis_index("rows")
    x = col // 2
    p = col % 2
    info = jnp.concatenate([jnp.stack([r, col, p, x]).astype(jnp.int32), block_sizes])
    sup = support.astype(F32)

    own = jnp.transpose(coefficients, (2, 0, 1, 3)).reshape(4, 512, 256)
    own_sup = jnp.transpose(sup, (2, 0, 1)).reshape(4, 512)
    tile = lax.dynamic_slice(own, (0, x * 128, p * 128), (4, 128, 128))
    message = jnp.concatenate([jnp.swapaxes(tile, 1, 2).reshape(512, 128), lax.dynamic_slice_in_dim(own_sup, x * 128, 128, 1),
                               jnp.zeros((4, 128), F32)], axis=0)
    gathered = lax.all_gather(message, "rows")
    head = lax.dynamic_slice(own, (x, 0, p * 128), (1, 128, 128))[0]
    head = jnp.concatenate([head.T, own_sup[:, :128], right_sides[0]], axis=0)
    head = jnp.where(r == 0, head, 0.0)
    own_sup = jnp.broadcast_to(own_sup[:, :, None], (4, 512, 128))
    eye = jnp.eye(128, dtype=F32)

    active = (jnp.arange(256, dtype=jnp.int32)[None, :] < block_sizes[:, None]).astype(F32)
    away = 128 - p * 128
    lent = lax.dynamic_slice_in_dim(primal, away, 128, 2) * lax.dynamic_slice_in_dim(dual_inverse, away, 128, 2)
    lent = swap(lent * active[:, :, None] * lax.dynamic_slice_in_dim(active, away, 128, 1)[:, None, :])

    half = partial(info, own, own_sup, primal, dual_inverse, lent)
    head, half = lax.optimization_barrier((head, half))
    for pairs in ([(0, 1)], [(0, 3), (1, 2)], [(z, 4 + z) for z in range(4)]):
        head = head + over_rows(head, pairs)
    head_next = over_rows(head, [(y + z, (12 if y == 0 else 8) + z) for y in (0, 4) for z in range(4)])
    terms = exchange(half, "cols", CHIPS)
    head_next, terms = lax.optimization_barrier((head_next, terms))
    head = head + head_next
    mixed, corner = assemble(terms, head)
    v_own = exchange(mixed, "cols", CHIPS)
    corner = corner + eye * jnp.where(p == 0, damping[0], 0.0)
    inverse = inverse_of(corner + swap(corner))
    second = over_rows(inverse, [(0, 12)])
    v_own, inverse, second, gathered = lax.optimization_barrier((v_own, inverse, second, gathered))
    v_other = swap(v_own)
    begun = lead(info, v_own, own_sup, head)
    gathered, v_other, begun = lax.optimization_barrier((gathered, v_other, begun))
    swapped = swap(gathered)
    every = exchange(lead(info, v_other, own_sup, head, [begun, inverse, second]), "rows")

    start = block_product(info, v_own, own_sup, gathered, lambda g, i: (i[2], 0, 0), head)
    updated, panel, solved = block_product(info, v_other, own_sup, swapped, lambda g, i: (i[2], 0, 0), head,
                                           list(start) + [every, damping, right_sides])
    return updated.reshape(4, 128, 1024), panel.reshape(4, 128, 128), solved


def solution(mesh):
    in_specs = (
        P(None, "rows", None, None),
        P(None, "rows", None),
        P("cols", None, None),
        P("cols", None, None),
        P("cols"),
        P(None, "rows"),
        P(None, "cols", "rows"),
    )
    out_specs = (P(None, "rows", "cols"), P(None, "rows", None), P(None, "cols", "rows"))
    return jax.shard_map(local, mesh=mesh, in_specs=in_specs, out_specs=out_specs, check_vma=False)
```
